32 devices in a mesh: lon: 8 (over z, y), trc: 4 (over x, core).
Axes of the slice: x: 2, y: 2, z: 4, core: 2. Of those that a mesh axis runs over, the one named last changes fastest.
Arguments:
- state_adjoint: float32 [8, 4, 24, 34, 256], P('trc', None, 'lon'), may hold values from -6 to 6
- switches: int32 [8, 2, 24, 34, 256], P('trc', None, 'lon'), may hold values from 0 to 2
- flags: int32 [2, 24, 34, 256], P(None, 'lon'), may hold values 0 or 1
- air_mass: float32 [24, 34, 256], P('lon', None, 'trc'), may hold values from 1 to 4
- x_flux: float32 [24, 34, 256], P('lon', None, 'trc'), may hold values from 0.02 to 0.45
- y_flux: float32 [24, 34, 256], P('lon', None, 'trc'), may hold values from 0.02 to 0.45
- vertical_mixing: float32 [24, 33, 256], P('lon', None, 'trc'), may hold values from 0.1 to 10
Outputs:
- prior_adjoint: float32 [8, 4, 24, 34, 256], P('trc', None, 'lon')
The draws below stay inside these ranges and needn't reach their ends.
All inputs are finite; a program needn't handle non-finite values. No bound on the sum of `flags` on one device may be relied on, other than what follows from the above.
Results may differ from the reference program's by a relative error of at most 0.0003.
Values sent between devices are 32-bit elements; how exact they have to be, the bound alone decides.
No kernel may reach another device: no remote copies, remote signals or barrier semaphores. Data moves between devices by JAX's collectives and lax.ppermute only.
A program may use at most 128 MiB of HBM per device.

```python
import math
import jax
import jax.numpy as jnp
from jax import lax

LAT = 256
LEV = 34
NX = 24
TRACERS = 8


def touch_ends(values, own_key, least, top_value):
    longest = values.shape.index(max(values.shape))
    spots = []
    for shift in (0, 1):
        where = [jax.random.randint(jax.random.fold_in(own_key, axis), (), 0, length) for axis, length in enumerate(values.shape)]
        where[longest] = (where[longest] + shift) % values.shape[longest]
        spots.append(tuple(where))
    return values.at[spots[0]].set(least).at[spots[1]].set(top_value)


def level_of(stream_key, shape, shards, least, top_value):
    factor_of, own = 1.0, jax.random.fold_in(stream_key, 6)
    for position, blocks in shards:
        steps = jnp.exp(jax.random.uniform(jax.random.fold_in(own, position), (blocks,), jnp.float32, least / len(shards), top_value / len(shards)))
        factor_of = factor_of * jnp.repeat(steps, shape[position] // blocks).reshape([-1 if axis == position else 1 for axis in range(len(shape))])
    return factor_of


def gaussian(key, dims, deviation, limit, shards=(), kind=jnp.bfloat16):
    factor_of = level_of(key, dims, shards, -0.22, 0.18) if shards else 1.0
    array = jax.random.normal(key, dims, jnp.float32) * deviation * factor_of
    return jnp.minimum(jnp.maximum(array, -limit), limit).astype(kind)


def setup_inputs(seed: int = 0) -> dict:
    keys = jax.random.split(jax.random.key(seed), 8)
    return {
        "state_adjoint": gaussian(keys[0], (TRACERS, 4, NX, LEV, LAT), 1.0, 6.0, ((0, 4), (2, 8)), jnp.float32),
        "switches": touch_ends(jax.random.randint(keys[1], (TRACERS, 2, NX, LEV, LAT), 0, 3), jax.random.fold_in(keys[1], 1), 0, 2).astype(jnp.int32),
        "flags": touch_ends((jax.random.randint(keys[2], (2, NX, LEV, LAT), 0, 2) < 1).astype(jnp.int32), jax.random.fold_in(keys[2], 1), 0, 1),
        "air_mass": jnp.clip(jnp.exp(math.log(4.0) - 1.3862944 * jax.random.uniform(keys[3], (NX, LEV, LAT), jnp.float32) ** level_of(keys[3], (NX, LEV, LAT), ((0, 8), (2, 4)), -0.2, 0.2)), 1.0, 4.0),
        "x_flux": jnp.clip(0.02 + 0.42999999 * jax.random.uniform(keys[4], (NX, LEV, LAT), jnp.float32) ** level_of(keys[4], (NX, LEV, LAT), ((0, 8), (2, 4)), -0.2, 0.2), 0.02, 0.45),
        "y_flux": jnp.clip(0.02 + 0.42999999 * jax.random.uniform(keys[5], (NX, LEV, LAT), jnp.float32) ** level_of(keys[5], (NX, LEV, LAT), ((0, 8), (2, 4)), -0.2, 0.2), 0.02, 0.45),
        "vertical_mixing": jnp.clip(jnp.exp(math.log(10.0) - 4.6051702 * jax.random.uniform(keys[6], (NX, LEV - 1, LAT), jnp.float32) ** level_of(keys[6], (NX, LEV - 1, LAT), ((0, 8), (2, 4)), -0.2, 0.2)), 0.1, 10.0),
    }


def shift_prev(values, along, periodic):
    if periodic:
        return jnp.roll(values, 1, along)
    count = values.shape[along]
    head = jnp.zeros_like(lax.slice_in_dim(values, 0, 1, axis=along))
    return jnp.concatenate([head, lax.slice_in_dim(values, 0, count - 1, axis=along)], along)

def shift_next(values, along, periodic):
    if periodic:
        return jnp.roll(values, -1, along)
    count = values.shape[along]
    tail = jnp.zeros_like(lax.slice_in_dim(values, 0, 1, axis=along))
    return jnp.concatenate([lax.slice_in_dim(values, 1, count, axis=along), tail], along)

def mixing_factors(mixing):
    levels = mixing.shape[-2] + 1
    inverse_list = []
    upper_list = []
    lower_list = []
    zero_plane = jnp.zeros_like(mixing[..., 0, :])
    for height in range(levels):
        diagonal = 1.0 + zero_plane
        if height > 0:
            below = mixing[..., height - 1, :]
            diagonal = diagonal + below
        if height < levels - 1:
            above = mixing[..., height, :]
            diagonal = diagonal + above
        if height > 0:
            diagonal = diagonal + below * upper_list[height - 1]
        inverse = 1.0 / diagonal
        inverse_list.append(inverse)
        upper_list.append(-above * inverse if height < levels - 1 else zero_plane)
        lower_list.append(below * inverse if height > 0 else zero_plane)
    return (jnp.stack(inverse_list, -2), jnp.stack(upper_list, -2), jnp.stack(lower_list, -2))

def mixing_solve(values, inverse, upper, lower):
    levels = values.shape[-2]
    partial_list = []
    carried = values[..., 0, :] * inverse[..., 0, :]
    partial_list.append(carried)
    for height in range(1, levels):
        carried = values[..., height, :] * inverse[..., height, :] + lower[..., height, :] * carried
        partial_list.append(carried)
    result = [None] * levels
    carried = partial_list[levels - 1]
    result[levels - 1] = carried
    for height in range(levels - 2, -1, -1):
        carried = partial_list[height] - upper[..., height, :] * carried
        result[height] = carried
    return jnp.stack(result, -2)

def advect_line(state, mass, west_flux, west_flag, keep_slope, take_mass, along, periodic, slope_index, passive):
    tracer_mass = state[0]
    slope = keep_slope * state[slope_index] + take_mass * tracer_mass
    upwind = west_flag
    sign = 2.0 * upwind - 1.0

    def from_up(values):
        return upwind * shift_prev(values, along, periodic) + (1.0 - upwind) * values
    fraction = west_flux / from_up(mass)
    flux = fraction * (from_up(tracer_mass) + sign * (1.0 - fraction) * from_up(slope))
    slope_flux = fraction * fraction * from_up(slope)
    outflow = fraction * (1.0 - upwind) + shift_next(fraction * upwind, along, periodic)
    moments = [None] * 4
    moments[0] = tracer_mass + sign * flux - shift_next(sign * flux, along, periodic)
    moments[slope_index] = (1.0 - outflow) * slope + upwind * slope_flux + shift_next((1.0 - upwind) * slope_flux, along, periodic)
    for index in passive:
        carried = fraction * from_up(state[index])
        moments[index] = (1.0 - outflow) * state[index] + upwind * carried + shift_next((1.0 - upwind) * carried, along, periodic)
    return jnp.stack(moments, 0)

def reference(state_adjoint, switches, flags, air_mass, x_flux, y_flux, vertical_mixing):
    inverse, upper, lower = mixing_factors(vertical_mixing)
    x_flag = flags[0].astype(jnp.float32)
    y_flag = flags[1].astype(jnp.float32)
    y_west_flux = shift_prev(y_flux, 2, False)
    y_west_flag = shift_prev(y_flag, 2, False)

    def one_tracer(inputs):
        cotangent, switch_pair = inputs
        keep_x = (switch_pair[0] == 0).astype(jnp.float32)
        take_x = (switch_pair[0] == 1).astype(jnp.float32) - (switch_pair[0] == 2).astype(jnp.float32)
        keep_y = (switch_pair[1] == 0).astype(jnp.float32)
        take_y = (switch_pair[1] == 1).astype(jnp.float32) - (switch_pair[1] == 2).astype(jnp.float32)

        def x_step(state):
            return advect_line(state, air_mass, x_flux, x_flag, keep_x, take_x, 0, True, 1, (2, 3))

        def y_step(state):
            return advect_line(state, air_mass, y_west_flux, y_west_flag, keep_y, take_y, 2, False, 2, (1, 3))

        def mix_step(state):
            mixed = mixing_solve(state[0:3], inverse, upper, lower)
            return jnp.concatenate([mixed, state[3:4]], 0)

        def hour(state):
            return x_step(y_step(mix_step(y_step(x_step(state)))))
        outputs, pullback = jax.vjp(hour, cotangent)
        return pullback(cotangent)[0]
    return lax.map(one_tracer, (state_adjoint, switches))
```

```python
import jax
import jax.numpy as jnp
from jax import lax
from jax.experimental import pallas as pl
from jax.experimental.pallas import tpu as pltpu
from jax.sharding import PartitionSpec as P

LANES = 128
MOMENTS = 4
VMEM = pl.BlockSpec(memory_space=pltpu.VMEM)


def state_view(x):
    t, m, c, l, n = x.shape
    b = n // LANES
    x = x.reshape(t, m, c, l, b, LANES).transpose(0, 2, 3, 4, 1, 5)
    return x.reshape(t, c, l, b * m, LANES)


def pair_view(x):
    t, d, c, l, n = x.shape
    b = n // LANES
    x = x.reshape(t, d, c, l, b, LANES).transpose(0, 2, 3, 4, 1, 5)
    return x.reshape(t, c, l // 2, 2 * b * d, LANES)


def state_back(y):
    t, c, l, rows, _ = y.shape
    b = rows // MOMENTS
    y = y.reshape(t, c, l, b, MOMENTS, LANES).transpose(0, 4, 1, 2, 3, 5)
    return y.reshape(t, MOMENTS, c, l, b * LANES)


def shifted(value, axis, by):
    count = lax.axis_size(axis)
    return lax.ppermute(value, axis, [(i, (i + by) % count) for i in range(count)])


def swapped(value, axis, mask):
    count = lax.axis_size(axis)
    return lax.ppermute(value, axis, [(i, i ^ mask) for i in range(count)])


def call(kernel, out, scratch, flops, moved, *args):
    return pl.pallas_call(
        kernel,
        out_shape=out,
        in_specs=[VMEM] * len(args),
        out_specs=jax.tree.map(lambda _: VMEM, out),
        scratch_shapes=scratch,
        compiler_params=pltpu.CompilerParams(vmem_limit_bytes=24 * 1024 * 1024),
        cost_estimate=pl.CostEstimate(flops=flops, bytes_accessed=moved, transcendentals=0),
    )(*args)


def f32(*shape):
    return jax.ShapeDtypeStruct(shape, jnp.float32)


def tile_masks(slope):
    row = lax.broadcasted_iota(jnp.int32, (8, LANES), 0) % MOMENTS
    return row == 0, row == slope


def pack_kernel(mass, xf, yf, km, flags, packed, face):
    half = LANES // 2
    levels = mass.shape[1]
    packed[0, :, :, :half] = mass[...]
    packed[0, :, :, half:] = xf[...]
    packed[1, :, :, :half] = yf[...]
    packed[1, :, : levels - 1, half:] = km[...]
    packed[1, :, levels - 1 :, half:] = jnp.zeros((mass.shape[0], 1, half), jnp.float32)
    face[:, :half] = xf[0, : levels // 2]
    face[:, half:] = xf[0, levels // 2 :]


def pre_kernel(own, first, second, third, face0, face1, face2, face3, flags, edge, switches, order,
               rates, factors, turn, fields, faces):
    columns, levels = own.shape[1], own.shape[2]
    half = LANES // 2
    odd = order[0] % 2 == 1
    high = order[0] >= 2
    lane = lax.broadcasted_iota(jnp.int32, (8, LANES), 1)
    row = lax.broadcasted_iota(jnp.int32, (8, LANES), 0)
    upper_block = row >= MOMENTS
    lane_low = lax.broadcasted_iota(jnp.int32, (levels, LANES), 1) < half

    def sorted_shards(a, b, c, d):
        a, b, c, d = (jnp.where(odd, b, a), jnp.where(odd, a, b), jnp.where(odd, d, c), jnp.where(odd, c, d))
        return (jnp.where(high, c, a), jnp.where(high, d, b), jnp.where(high, a, c), jnp.where(high, b, d))

    for pair in range(2):
        for c in range(columns):
            shards = sorted_shards(own[pair, c], first[pair, c], second[pair, c], third[pair, c])
            for b in range(2):
                lo, hi = shards[2 * b], shards[2 * b + 1]
                lo_r, hi_r = pltpu.roll(lo, half, 1), pltpu.roll(hi, half, 1)
                fields[2 * pair, c, b] = jnp.where(lane_low, lo, hi_r)
                fields[2 * pair + 1, c, b] = jnp.where(lane_low, lo_r, hi)
    shards = sorted_shards(face0[...], face1[...], face2[...], face3[...])
    short = lane_low[: levels // 2]
    for b in range(2):
        lo, hi = shards[2 * b], shards[2 * b + 1]
        faces[0, b] = jnp.where(short, lo, pltpu.roll(hi, half, 1))
        faces[1, b] = jnp.where(short, pltpu.roll(lo, half, 1), hi)

    def spread(ref, *where):
        blocks = [jnp.broadcast_to(ref[(*index, pl.ds(r, 1), slice(None))], (8, LANES)) for index, r in where]
        return jnp.where(upper_block, blocks[1], blocks[0])

    def field(f, c, l):
        return spread(fields, ((f, c, 0), l), ((f, c, 1), l))

    def flag(ref, c, l, d):
        base = (l % 2) * 4 + d
        return spread(ref, ((c, l // 2), base), ((c, l // 2), base + 2)).astype(jnp.float32)

    first_row = (lane == 0) & (row < MOMENTS)
    last_row = (lane == LANES - 1) & (row >= MOMENTS)
    for l in range(levels):
        flux_x = [field(1, c, l) for c in range(columns)]
        flag_x = [flag(flags, c, l, 0) for c in range(columns)]
        fl = l % (levels // 2)
        fh = l // (levels // 2)
        flux_x.append(spread(faces, ((fh, 0), fl), ((fh, 1), fl)))
        base = (l % 2) * 4
        flag_x.append(spread(edge, ((l // 2,), base), ((l // 2,), base + 2)).astype(jnp.float32))
        for c in range(columns):
            share = 1.0 / field(0, c, l)
            rates[0, c, l] = flag_x[c + 1] * flux_x[c + 1] * share
            rates[1, c, l] = (1.0 - flag_x[c]) * flux_x[c] * share
            flux_y = field(2, c, l)
            flag_y = flag(flags, c, l, 1)
            north = flag_y * flux_y
            south = pltpu.roll(flux_y - north, 1, 1)
            south = jnp.where(lane == 0, pltpu.roll(south, 4, 0), south)
            rates[2, c, l] = jnp.where(last_row, 0.0, north) * share
            rates[3, c, l] = jnp.where(first_row, 0.0, south) * share

    fixed = row % MOMENTS == 3
    for c in range(columns):
        below = None
        upper = None
        for l in range(levels):
            diagonal = jnp.ones((8, LANES), jnp.float32)
            if l > 0:
                diagonal = diagonal + below
            if l < levels - 1:
                above = field(3, c, l)
                diagonal = diagonal + above
            if l > 0:
                diagonal = diagonal + below * upper
            inverse = 1.0 / diagonal
            factors[0, c, l] = jnp.where(fixed, 1.0, inverse)
            factors[2, c, l] = jnp.where(fixed, 0.0, below * inverse) if l > 0 else jnp.zeros((8, LANES), jnp.float32)
            if l < levels - 1:
                upper = -above * inverse
                factors[1, c, l] = jnp.where(fixed, 0.0, upper)
                below = above
            else:
                factors[1, c, l] = jnp.zeros((8, LANES), jnp.float32)

    for t in range(switches.shape[0]):
        for c in range(columns):
            for l in range(levels):
                for d in range(2):
                    base = (l % 2) * 4 + d
                    sw = spread(switches, ((t, c, l // 2), base), ((t, c, l // 2), base + 2))
                    take = jnp.where(sw == 1, 1.0, jnp.where(sw == 2, -1.0, 0.0))
                    keep = jnp.where(sw == 0, 1.0, 0.0)
                    m = row % MOMENTS
                    turn[d, t, c, l] = jnp.where(m == 0, take, jnp.where(m == 1 + d, keep, 1.0))


def advect(own, east_side, west_side, east, west, turns, slope, masks):
    is_mass, is_slope = masks
    stay = 1.0 - (east + west)
    east_part = east * jnp.where(is_slope, east, 1.0)
    west_part = west * jnp.where(is_slope, west, 1.0)
    east_cross = east * (1.0 - east)
    west_cross = west * (1.0 - west)
    out = []
    for s, e, w, z in zip(own, east_side, west_side, turns):
        total = stay * s + east_part * e + west_part * w
        cross = east_cross * (e - s) - west_cross * (w - s)
        total = total + jnp.where(is_slope, pltpu.roll(cross, slope, 0), 0.0)
        slope_up = pltpu.roll(total, 8 - slope, 0)
        out.append(z * jnp.where(is_mass, slope_up, total) + jnp.where(is_mass, total, 0.0))
    return out


def mid_kernel(state, west_halo, east_halo, rates, factors, turn, out0, out1, out2):
    tracers, columns, levels = state.shape[0], state.shape[1], state.shape[2]
    outs = (out0, out1, out2)
    lane = lax.broadcasted_iota(jnp.int32, (8, LANES), 1)
    at_first, at_last = lane == 0, lane == LANES - 1
    x_masks, y_masks = tile_masks(1), tile_masks(2)

    def prev(v):
        r = pltpu.roll(v, 1, 1)
        return jnp.where(at_first, pltpu.roll(r, 4, 0), r)

    def following(v):
        r = pltpu.roll(v, LANES - 1, 1)
        return jnp.where(at_last, pltpu.roll(r, 4, 0), r)

    def y_step(values, c, l):
        return advect(values, [following(v) for v in values], [prev(v) for v in values],
                      rates[2, c, l], rates[3, c, l], [turn[1, t, c, l] for t in range(tracers)], 2, y_masks)

    carried = [[None] * tracers for _ in range(columns)]
    for l in range(levels):
        line = [[west_halo[t, l] for t in range(tracers)]]
        line += [[state[t, c, l] for t in range(tracers)] for c in range(columns)]
        line += [[east_halo[t, l] for t in range(tracers)]]
        for c in range(columns):
            values = advect(line[c + 1], line[c + 2], line[c], rates[0, c, l], rates[1, c, l],
                            [turn[0, t, c, l] for t in range(tracers)], 1, x_masks)
            values = y_step(values, c, l)
            for t in range(tracers):
                v = values[t] * factors[0, c, l]
                if l > 0:
                    v = v + factors[2, c, l] * carried[c][t]
                carried[c][t] = v
                outs[c][t, l] = v
    for l in range(levels - 1, -1, -1):
        for c in range(columns):
            if l < levels - 1:
                for t in range(tracers):
                    carried[c][t] = outs[c][t, l] - factors[1, c, l] * carried[c][t]
            values = y_step(carried[c], c, l)
            for t in range(tracers):
                outs[c][t, l] = values[t]


def post_kernel(col0, col1, col2, west_halo, east_halo, rates, turn, out):
    tracers, columns, levels = out.shape[0], out.shape[1], out.shape[2]
    line_refs = (west_halo, col0, col1, col2, east_halo)
    masks = tile_masks(1)
    for l in range(levels):
        line = [[ref[t, l] for t in range(tracers)] for ref in line_refs]
        for c in range(columns):
            values = advect(line[c + 1], line[c + 2], line[c], rates[0, c, l], rates[1, c, l],
                            [turn[0, t, c, l] for t in range(tracers)], 1, masks)
            for t in range(tracers):
                out[t, c, l] = values[t]


def body(state_adjoint, switches, flags, air_mass, x_flux, y_flux, vertical_mixing):
    state = state_view(state_adjoint)
    switch = pair_view(switches)
    flag = pair_view(flags[None])[0]
    tracers, columns, levels = state.shape[:3]
    order = lax.axis_index("trc").astype(jnp.int32).reshape(1)

    packed, face = call(
        pack_kernel,
        (f32(2, columns, levels, LANES), f32(levels // 2, LANES)),
        (), 10**5, 10**6, air_mass, x_flux, y_flux, vertical_mixing, flag)
    face = shifted(face, "lon", -1)
    edge = shifted(flag[0], "lon", -1)
    others = [swapped(packed, "trc", mask) for mask in (1, 2, 3)]
    east_halo = shifted(state[:, 0], "lon", -1)
    west_halo = shifted(state[:, columns - 1], "lon", 1)
    faces = [swapped(face, "trc", mask) for mask in (1, 2, 3)]

    rates, factors, turn = pl.pallas_call(
        pre_kernel,
        out_shape=(f32(4, columns, levels, 8, LANES), f32(3, columns, levels, 8, LANES),
                   f32(2, tracers, columns, levels, 8, LANES)),
        in_specs=[VMEM] * 11 + [pl.BlockSpec(memory_space=pltpu.SMEM)],
        out_specs=(VMEM,) * 3,
        scratch_shapes=[pltpu.VMEM((4, columns, 2, levels, LANES), jnp.float32),
                        pltpu.VMEM((2, 2, levels // 2, LANES), jnp.float32)],
        compiler_params=pltpu.CompilerParams(vmem_limit_bytes=24 * 1024 * 1024),
        cost_estimate=pl.CostEstimate(flops=10**7, bytes_accessed=10**7, transcendentals=0),
    )(packed, *others, face, *faces, flag, edge, switch, order)

    column = f32(tracers, levels, 8, LANES)
    col0, col1, col2 = call(mid_kernel, (column,) * 3, (), 10**7, 10**7,
                            state, west_halo, east_halo, rates, factors, turn)
    east_halo = shifted(col0, "lon", -1)
    west_halo = shifted(col2, "lon", 1)
    out = call(post_kernel, f32(*state.shape), (), 10**7, 10**6,
               col0, col1, col2, west_halo, east_halo, rates, turn)
    return state_back(out)


def solution(mesh):
    placed = (
        P("trc", None, "lon", None, None),
        P("trc", None, "lon", None, None),
        P(None, "lon", None, None),
        P("lon", None, "trc"),
        P("lon", None, "trc"),
        P("lon", None, "trc"),
        P("lon", None, "trc"),
    )
    return jax.shard_map(
        body,
        mesh=mesh,
        in_specs=placed,
        out_specs=P("trc", None, "lon", None, None),
        check_vma=False,
    )
```

```python
import jax
import jax.numpy as jnp
from jax import lax
from jax.experimental import pallas as pl
from jax.experimental.pallas import tpu as pltpu
from jax.sharding import PartitionSpec as P

LANES = 128
MOMENTS = 4
VMEM = pl.BlockSpec(memory_space=pltpu.VMEM)
SMEM = pl.BlockSpec(memory_space=pltpu.SMEM)
ANY = pl.BlockSpec(memory_space=pl.ANY)


def state_view(x):
    t, m, c, l, n = x.shape
    b = n // LANES
    x = x.reshape(t, m, c, l, b, LANES).transpose(0, 2, 3, 4, 1, 5)
    return x.reshape(t, c, l, b * m, LANES)


def pair_view(x):
    t, d, c, l, n = x.shape
    b = n // LANES
    x = x.reshape(t, d, c, l, b, LANES).transpose(0, 2, 3, 4, 1, 5)
    return x.reshape(t, c, l * b * d, LANES)


def state_back(y):
    t, c, l, rows, _ = y.shape
    b = rows // MOMENTS
    y = y.reshape(t, c, l, b, MOMENTS, LANES).transpose(0, 4, 1, 2, 3, 5)
    return y.reshape(t, MOMENTS, c, l, b * LANES)


def shifted(value, axis, by):
    count = lax.axis_size(axis)
    return lax.ppermute(value, axis, [(i, (i + by) % count) for i in range(count)])


def swapped(value, axis, mask):
    count = lax.axis_size(axis)
    return lax.ppermute(value, axis, [(i, i ^ mask) for i in range(count)])


def call(kernel, out, in_specs, scratch, flops, moved, *args):
    return pl.pallas_call(
        kernel,
        out_shape=out,
        in_specs=in_specs,
        out_specs=jax.tree.map(lambda _: VMEM, out),
        scratch_shapes=scratch,
        compiler_params=pltpu.CompilerParams(vmem_limit_bytes=24 * 1024 * 1024),
        cost_estimate=pl.CostEstimate(flops=flops, bytes_accessed=moved, transcendentals=0),
    )(*args)


def f32(*shape):
    return jax.ShapeDtypeStruct(shape, jnp.float32)


def tile_masks(slope):
    row = lax.broadcasted_iota(jnp.int32, (8, LANES), 0) % MOMENTS
    return row == 0, row == slope


def head_kernel(state, flags, xf, order, col0, col1, col2, face, sems):
    tracers, levels = state.shape[0], xf.shape[1]
    half = LANES // 2
    copies = [pltpu.make_async_copy(state.at[t, c], col.at[t], sems.at[c, t])
              for c, col in enumerate((col0, col1, col2)) for t in range(tracers)]
    for copy in copies:
        copy.start()
    odd, high = order[0] % 2 == 1, order[0] >= 2
    block0 = flags[0, pl.ds(0, levels, stride=4), :].astype(jnp.float32)
    block1 = flags[0, pl.ds(2, levels, stride=4), :].astype(jnp.float32)
    chosen = jnp.where(high, block1, block0)
    chosen = jnp.where(odd, pltpu.roll(chosen, half, 1), chosen)[:, :half]
    signed = (2.0 * chosen - 1.0) * xf[0]
    face[:, :half] = signed[: levels // 2]
    face[:, half:] = signed[levels // 2 :]
    for copy in copies:
        copy.wait()


def pack_kernel(mass, xf, yf, km, face, packed):
    half = LANES // 2
    columns, levels = mass.shape[:2]
    for c in range(columns):
        low, top = c * levels, (columns + c) * levels
        packed[low : low + levels, :half] = mass[c]
        packed[low : low + levels, half:] = xf[c]
        packed[top : top + levels, :half] = yf[c]
        packed[top : top + levels - 1, half:] = km[c]
        packed[top + levels - 1 : top + levels, half:] = jnp.zeros((1, half), jnp.float32)
    tail = 2 * columns * levels
    packed[tail : tail + levels // 2] = face[...]


def spread(upper_block, ref, *where):
    blocks = [jnp.broadcast_to(ref[(*index, pl.ds(r, 1), slice(None))], (8, LANES)) for index, r in where]
    return jnp.where(upper_block, blocks[1], blocks[0])


def turn_kernel(switches, turn):
    tracers, columns = switches.shape[:2]
    levels = switches.shape[2] // 4
    row = lax.broadcasted_iota(jnp.int32, (8, LANES), 0)
    moment = row % MOMENTS
    for t in range(tracers):
        for c in range(columns):
            for l in range(levels):
                for d in range(2):
                    base = l * 4 + d
                    sw = spread(row >= MOMENTS, switches, ((t, c), base), ((t, c), base + 2))
                    take = jnp.where(sw == 1, 1.0, jnp.where(sw == 2, -1.0, 0.0))
                    keep = jnp.where(sw == 0, 1.0, 0.0)
                    turn[d, t, c, l] = jnp.where(moment == 0, take, jnp.where(moment == 1 + d, keep, 1.0))


def pre_kernel(own, first, second, third, flags, order, rates, factors, fields, faces):
    columns, levels = rates.shape[1], rates.shape[2]
    half = LANES // 2
    odd = order[0] % 2 == 1
    high = order[0] >= 2
    lane = lax.broadcasted_iota(jnp.int32, (8, LANES), 1)
    row = lax.broadcasted_iota(jnp.int32, (8, LANES), 0)
    upper_block = row >= MOMENTS
    lane_low = lax.broadcasted_iota(jnp.int32, (levels, LANES), 1) < half

    def sorted_shards(start, count):
        a, b, c, d = (ref[start : start + count] for ref in (own, first, second, third))
        a, b, c, d = (jnp.where(odd, b, a), jnp.where(odd, a, b), jnp.where(odd, d, c), jnp.where(odd, c, d))
        return (jnp.where(high, c, a), jnp.where(high, d, b), jnp.where(high, a, c), jnp.where(high, b, d))

    for pair in range(2):
        for c in range(columns):
            shards = sorted_shards((pair * columns + c) * levels, levels)
            for b in range(2):
                lo, hi = shards[2 * b], shards[2 * b + 1]
                fields[2 * pair, c, b] = jnp.where(lane_low, lo, pltpu.roll(hi, half, 1))
                fields[2 * pair + 1, c, b] = jnp.where(lane_low, pltpu.roll(lo, half, 1), hi)
    shards = sorted_shards(2 * columns * levels, levels // 2)
    short = lane_low[: levels // 2]
    for b in range(2):
        lo, hi = shards[2 * b], shards[2 * b + 1]
        faces[0, b] = jnp.where(short, lo, pltpu.roll(hi, half, 1))
        faces[1, b] = jnp.where(short, pltpu.roll(lo, half, 1), hi)

    def field(f, c, l):
        return spread(upper_block, fields, ((f, c, 0), l), ((f, c, 1), l))

    def flag(c, l, d):
        base = l * 4 + d
        return spread(upper_block, flags, ((c,), base), ((c,), base + 2)).astype(jnp.float32)

    first_row = (lane == 0) & (row < MOMENTS)
    last_row = (lane == LANES - 1) & (row >= MOMENTS)
    for l in range(levels):
        flux_x = [field(1, c, l) for c in range(columns)]
        flag_x = [flag(c, l, 0) for c in range(columns)]
        east = [flag_x[c] * flux_x[c] for c in range(columns)]
        west = [flux_x[c] - east[c] for c in range(columns)]
        deep, level = divmod(l, levels // 2)
        east.append(jnp.maximum(spread(upper_block, faces, ((deep, 0), level), ((deep, 1), level)), 0.0))
        for c in range(columns):
            share = 1.0 / field(0, c, l)
            rates[0, c, l] = east[c + 1] * share
            rates[1, c, l] = west[c] * share
            flux_y = field(2, c, l)
            north = flag(c, l, 1) * flux_y
            south = pltpu.roll(flux_y - north, 1, 1)
            south = jnp.where(lane == 0, pltpu.roll(south, 4, 0), south)
            rates[2, c, l] = jnp.where(last_row, 0.0, north) * share
            rates[3, c, l] = jnp.where(first_row, 0.0, south) * share

    fixed = row % MOMENTS == 3
    zero = jnp.zeros((8, LANES), jnp.float32)
    below, upper = [None] * columns, [None] * columns
    for l in range(levels):
        for c in range(columns):
            diagonal = zero + 1.0
            if l > 0:
                diagonal = diagonal + below[c]
            if l < levels - 1:
                above = field(3, c, l)
                diagonal = diagonal + above
            if l > 0:
                diagonal = diagonal + below[c] * upper[c]
            inverse = 1.0 / diagonal
            factors[0, c, l] = jnp.where(fixed, 1.0, inverse)
            factors[2, c, l] = jnp.where(fixed, 0.0, below[c] * inverse) if l > 0 else zero
            if l < levels - 1:
                upper[c] = -above * inverse
                factors[1, c, l] = jnp.where(fixed, 0.0, upper[c])
                below[c] = above
            else:
                factors[1, c, l] = zero


def advect(own, east_side, west_side, east, west, turns, slope, masks):
    is_mass, is_slope = masks
    stay = 1.0 - (east + west)
    east_part = east * jnp.where(is_slope, east, 1.0)
    west_part = west * jnp.where(is_slope, west, 1.0)
    east_cross = east * (1.0 - east)
    west_cross = west * (1.0 - west)
    out = []
    for s, e, w, z in zip(own, east_side, west_side, turns):
        total = stay * s + east_part * e + west_part * w
        cross = east_cross * (e - s) - west_cross * (w - s)
        total = total + jnp.where(is_slope, pltpu.roll(cross, slope, 0), 0.0)
        slope_up = pltpu.roll(total, 8 - slope, 0)
        out.append(z * jnp.where(is_mass, slope_up, total) + jnp.where(is_mass, total, 0.0))
    return out


def middle(todo, line_refs, rates, factors, turn, outs):
    tracers, levels = outs[0].shape[0], outs[0].shape[1]
    lane = lax.broadcasted_iota(jnp.int32, (8, LANES), 1)
    at_first, at_last = lane == 0, lane == LANES - 1
    x_masks, y_masks = tile_masks(1), tile_masks(2)
    every = range(tracers)

    def prev(v):
        r = pltpu.roll(v, 1, 1)
        return jnp.where(at_first, pltpu.roll(r, 4, 0), r)

    def following(v):
        r = pltpu.roll(v, LANES - 1, 1)
        return jnp.where(at_last, pltpu.roll(r, 4, 0), r)

    def y_step(values, c, l):
        return advect(values, [following(v) for v in values], [prev(v) for v in values],
                      rates[2, c, l], rates[3, c, l], [turn[1, t, c, l] for t in every], 2, y_masks)

    carried = {c: [None] * tracers for c in todo}
    for l in range(levels):
        line = [None if ref is None else [ref[t, l] for t in every] for ref in line_refs]
        for c, out in zip(todo, outs):
            values = advect(line[c + 1], line[c + 2], line[c], rates[0, c, l], rates[1, c, l],
                            [turn[0, t, c, l] for t in every], 1, x_masks)
            values = y_step(values, c, l)
            for t in every:
                v = values[t] * factors[0, c, l]
                if l > 0:
                    v = v + factors[2, c, l] * carried[c][t]
                carried[c][t] = v
                out[t, l] = v
    for l in range(levels - 1, -1, -1):
        for c, out in zip(todo, outs):
            if l < levels - 1:
                for t in every:
                    carried[c][t] = out[t, l] - factors[1, c, l] * carried[c][t]
            values = y_step(carried[c], c, l)
            for t in every:
                out[t, l] = values[t]


def inner_kernel(col0, col1, col2, rates, factors, turn, out):
    middle((1,), (None, col0, col1, col2, None), rates, factors, turn, (out,))


def outer_kernel(col0, col1, col2, west_halo, east_halo, rates, factors, turn, out0, out2):
    middle((0, 2), (west_halo, col0, col1, col2, east_halo), rates, factors, turn, (out0, out2))


def post_kernel(col0, col1, col2, west_halo, east_halo, rates, turn, out):
    tracers, columns, levels = out.shape[0], out.shape[1], out.shape[2]
    line_refs = (west_halo, col0, col1, col2, east_halo)
    masks = tile_masks(1)
    for l in range(levels):
        line = [[ref[t, l] for t in range(tracers)] for ref in line_refs]
        for c in range(columns):
            values = advect(line[c + 1], line[c + 2], line[c], rates[0, c, l], rates[1, c, l],
                            [turn[0, t, c, l] for t in range(tracers)], 1, masks)
            for t in range(tracers):
                out[t, c, l] = values[t]


def body(state_adjoint, switches, flags, air_mass, x_flux, y_flux, vertical_mixing):
    state = state_view(state_adjoint)
    switch = pair_view(switches)
    flag = pair_view(flags[None])[0]
    tracers, columns, levels = state.shape[:3]
    order = lax.axis_index("trc").astype(jnp.int32).reshape(1)
    column = f32(tracers, levels, 8, LANES)
    face_shape = f32(levels // 2, LANES)

    col0, col1, col2, face = call(
        head_kernel, (column,) * 3 + (face_shape,), (ANY, VMEM, VMEM, SMEM),
        [pltpu.SemaphoreType.DMA((columns, tracers))], 10**5, 10**6, state, flag, x_flux, order)
    face = shifted(face, "lon", -1)
    east_halo = shifted(col0, "lon", -1)
    west_halo = shifted(col2, "lon", 1)
    rows = -(-(2 * columns * levels + levels // 2) // 8) * 8
    packed = call(pack_kernel, f32(rows, LANES), (VMEM,) * 5, (), 10**5, 10**6,
                  air_mass, x_flux, y_flux, vertical_mixing, face)
    others = [swapped(packed, "trc", mask) for mask in (1, 2, 3)]
    turn = call(turn_kernel, f32(2, tracers, columns, levels, 8, LANES), (VMEM,), (), 10**6, 10**6, switch)
    rates, factors = call(
        pre_kernel, (f32(4, columns, levels, 8, LANES), f32(3, columns, levels, 8, LANES)),
        (VMEM,) * 5 + (SMEM,),
        [pltpu.VMEM((4, columns, 2, levels, LANES), jnp.float32),
         pltpu.VMEM((2, 2, levels // 2, LANES), jnp.float32)],
        10**7, 10**7, packed, *others, flag, order)
    mid1 = call(inner_kernel, column, (VMEM,) * 6, (), 10**7, 10**7, col0, col1, col2, rates, factors, turn)
    mid0, mid2 = call(outer_kernel, (column,) * 2, (VMEM,) * 8, (), 10**7, 10**7,
                      col0, col1, col2, west_halo, east_halo, rates, factors, turn)
    east_halo = shifted(mid0, "lon", -1)
    west_halo = shifted(mid2, "lon", 1)
    out = call(post_kernel, f32(*state.shape), (VMEM,) * 7, (), 10**7, 10**6,
               mid0, mid1, mid2, west_halo, east_halo, rates, turn)
    return state_back(out)


def solution(mesh):
    placed = (
        P("trc", None, "lon", None, None),
        P("trc", None, "lon", None, None),
        P(None, "lon", None, None),
        P("lon", None, "trc"),
        P("lon", None, "trc"),
        P("lon", None, "trc"),
        P("lon", None, "trc"),
    )
    return jax.shard_map(
        body,
        mesh=mesh,
        in_specs=placed,
        out_specs=P("trc", None, "lon", None, None),
        check_vma=False,
    )
```

```python
import jax
import jax.numpy as jnp
from jax import lax
from jax.experimental import pallas as pl
from jax.experimental.pallas import tpu as pltpu
from jax.sharding import PartitionSpec as P

LANES = 128
MOMENTS = 4
VMEM = pl.BlockSpec(memory_space=pltpu.VMEM)
SMEM = pl.BlockSpec(memory_space=pltpu.SMEM)
HBM = pl.BlockSpec(memory_space=pltpu.HBM)


def state_view(x):
    t, m, c, l, n = x.shape
    b = n // LANES
    x = x.reshape(t, m, c, l, b, LANES).transpose(0, 2, 3, 4, 1, 5)
    return x.reshape(t, c, l, b * m, LANES)


def pair_view(x):
    t, d, c, l, n = x.shape
    b = n // LANES
    x = x.reshape(t, d, c, l, b, LANES).transpose(0, 2, 3, 4, 1, 5)
    return x.reshape(t, c, l * b * d, LANES)


def state_back(y):
    t, c, l, rows, _ = y.shape
    b = rows // MOMENTS
    y = y.reshape(t, c, l, b, MOMENTS, LANES).transpose(0, 4, 1, 2, 3, 5)
    return y.reshape(t, MOMENTS, c, l, b * LANES)


def shifted(value, axis, by):
    count = lax.axis_size(axis)
    return lax.ppermute(value, axis, [(i, (i + by) % count) for i in range(count)])


def swapped(value, axis, mask):
    count = lax.axis_size(axis)
    return lax.ppermute(value, axis, [(i, i ^ mask) for i in range(count)])


def call(kernel, out, in_specs, scratch, flops, moved, *args, out_specs=None, aliases=None):
    return pl.pallas_call(
        kernel,
        out_shape=out,
        in_specs=in_specs,
        out_specs=jax.tree.map(lambda _: VMEM, out) if out_specs is None else out_specs,
        scratch_shapes=scratch,
        input_output_aliases=aliases or {},
        compiler_params=pltpu.CompilerParams(vmem_limit_bytes=24 * 1024 * 1024),
        cost_estimate=pl.CostEstimate(flops=flops, bytes_accessed=moved, transcendentals=0),
    )(*args)


def stay(x):
    return pltpu.with_memory_space_constraint(x, pltpu.HBM)


def f32(*shape):
    return jax.ShapeDtypeStruct(shape, jnp.float32)


def tile_masks(slope):
    row = lax.broadcasted_iota(jnp.int32, (8, LANES), 0) % MOMENTS
    return row == 0, row == slope


def head_kernel(state, flags, mass, xf, yf, km, message, col1, col2, packed, flags_v, mass_v, xf_v, yf_v, km_v, sems, column_sems):
    tracers, columns, levels = state.shape[0], mass.shape[0], mass.shape[1]
    half = LANES // 2
    pairs = ((mass, mass_v), (xf, xf_v), (yf, yf_v), (km, km_v), (flags, flags_v))
    copies = [pltpu.make_async_copy(src, dst, sems.at[i]) for i, (src, dst) in enumerate(pairs)]
    for t in range(tracers):
        for c, place in ((2, col2.at[t]), (0, message.at[pl.ds(t * levels, levels)]), (1, col1.at[t])):
            copies.append(pltpu.make_async_copy(state.at[t, c], place, column_sems.at[c, t]))
    for copy in copies:
        copy.start()
    for copy in copies[:4]:
        copy.wait()
    for c in range(columns):
        low, top = c * levels, (columns + c) * levels
        packed[low : low + levels, :half] = mass_v[c]
        packed[low : low + levels, half:] = xf_v[c]
        packed[top : top + levels, :half] = yf_v[c]
        packed[top : top + levels - 1, half:] = km_v[c]
        packed[top + levels - 1 : top + levels, half:] = jnp.zeros((1, half), jnp.float32)
    for copy in copies[4:]:
        copy.wait()


def spread(upper_block, ref, *where):
    blocks = [jnp.broadcast_to(ref[(*index, pl.ds(r, 1), slice(None))], (8, LANES)) for index, r in where]
    return jnp.where(upper_block, blocks[1], blocks[0])


def face_row(rows, levels, b):
    return rows - -(-2 * levels // 8) * 8 + b * levels


def turn_kernel(switches, turn):
    tracers, columns = switches.shape[:2]
    levels = switches.shape[2] // 4
    row = lax.broadcasted_iota(jnp.int32, (8, LANES), 0)
    moment = row % MOMENTS
    for t in range(tracers):
        for c in range(columns):
            for l in range(levels):
                for d in range(2):
                    base = l * 4 + d
                    sw = spread(row >= MOMENTS, switches, ((t, c), base), ((t, c), base + 2))
                    take = jnp.where(sw == 1, 1.0, jnp.where(sw == 2, -1.0, 0.0))
                    keep = jnp.where(sw == 0, 1.0, 0.0)
                    turn[d, t, c, l] = jnp.where(moment == 0, take, jnp.where(moment == 1 + d, keep, 1.0))


def pre_kernel(own, first, second, third, flags, order, begun, before, also, rates, factors, message, fields):
    columns, levels = rates.shape[1], rates.shape[2]
    half = LANES // 2
    odd = order[0] % 2 == 1
    high = order[0] >= 2
    lane = lax.broadcasted_iota(jnp.int32, (8, LANES), 1)
    row = lax.broadcasted_iota(jnp.int32, (8, LANES), 0)
    upper_block = row >= MOMENTS
    lane_low = lax.broadcasted_iota(jnp.int32, (levels, LANES), 1) < half

    def sorted_shards(start, count):
        a, b, c, d = (ref[start : start + count] for ref in (own, first, second, third))
        a, b, c, d = (jnp.where(odd, b, a), jnp.where(odd, a, b), jnp.where(odd, d, c), jnp.where(odd, c, d))
        return (jnp.where(high, c, a), jnp.where(high, d, b), jnp.where(high, a, c), jnp.where(high, b, d))

    for pair in range(2):
        for c in range(columns):
            shards = sorted_shards((pair * columns + c) * levels, levels)
            for b in range(2):
                lo, hi = shards[2 * b], shards[2 * b + 1]
                fields[2 * pair, c, b] = jnp.where(lane_low, lo, pltpu.roll(hi, half, 1))
                flux = jnp.where(lane_low, pltpu.roll(lo, half, 1), hi)
                fields[2 * pair + 1, c, b] = flux
                if pair == 0 and c == 0:
                    eastward = flags[0, pl.ds(2 * b, levels, stride=4), :].astype(jnp.float32)
                    start = face_row(message.shape[0], levels, b)
                    message[start : start + levels] = (2.0 * eastward - 1.0) * flux

    def field(f, c, l):
        return spread(upper_block, fields, ((f, c, 0), l), ((f, c, 1), l))

    def flag(c, l, d):
        base = l * 4 + d
        return spread(upper_block, flags, ((c,), base), ((c,), base + 2)).astype(jnp.float32)

    first_row = (lane == 0) & (row < MOMENTS)
    last_row = (lane == LANES - 1) & (row >= MOMENTS)
    for l in range(levels):
        flux_x = [field(1, c, l) for c in range(columns)]
        flag_x = [flag(c, l, 0) for c in range(columns)]
        east = [flag_x[c] * flux_x[c] for c in range(columns)]
        west = [flux_x[c] - east[c] for c in range(columns)]
        east.append(1.0)
        for c in range(columns):
            share = 1.0 / field(0, c, l)
            rates[0, c, l] = east[c + 1] * share
            rates[1, c, l] = west[c] * share
            flux_y = field(2, c, l)
            north = flag(c, l, 1) * flux_y
            south = pltpu.roll(flux_y - north, 1, 1)
            south = jnp.where(lane == 0, pltpu.roll(south, 4, 0), south)
            rates[2, c, l] = jnp.where(last_row, 0.0, north) * share
            rates[3, c, l] = jnp.where(first_row, 0.0, south) * share

    fixed = row % MOMENTS == 3
    zero = jnp.zeros((8, LANES), jnp.float32)
    below, upper = [None] * columns, [None] * columns
    for l in range(levels):
        for c in range(columns):
            diagonal = zero + 1.0
            if l > 0:
                diagonal = diagonal + below[c]
            if l < levels - 1:
                above = field(3, c, l)
                diagonal = diagonal + above
            if l > 0:
                diagonal = diagonal + below[c] * upper[c]
            inverse = 1.0 / diagonal
            factors[0, c, l] = jnp.where(fixed, 1.0, inverse)
            factors[2, c, l] = jnp.where(fixed, 0.0, below[c] * inverse) if l > 0 else zero
            if l < levels - 1:
                upper[c] = -above * inverse
                factors[1, c, l] = jnp.where(fixed, 0.0, upper[c])
                below[c] = above
            else:
                factors[1, c, l] = zero


def advect(own, east_side, west_side, east, west, turns, slope, masks):
    is_mass, is_slope = masks
    stay = 1.0 - (east + west)
    east_part = east * jnp.where(is_slope, east, 1.0)
    west_part = west * jnp.where(is_slope, west, 1.0)
    east_cross = east * (1.0 - east)
    west_cross = west * (1.0 - west)
    out = []
    for s, e, w, z in zip(own, east_side, west_side, turns):
        total = stay * s + east_part * e + west_part * w
        cross = east_cross * (e - s) - west_cross * (w - s)
        total = total + jnp.where(is_slope, pltpu.roll(cross, slope, 0), 0.0)
        slope_up = pltpu.roll(total, 8 - slope, 0)
        out.append(z * jnp.where(is_mass, slope_up, total) + jnp.where(is_mass, total, 0.0))
    return out


def middle(todo, own, east_side, west_side, east_rate, rates, factors, turn, out):
    tracers, levels = out.shape[0], out.shape[1]
    lane = lax.broadcasted_iota(jnp.int32, (8, LANES), 1)
    at_first, at_last = lane == 0, lane == LANES - 1
    x_masks, y_masks = tile_masks(1), tile_masks(2)
    every = range(tracers)
    c = todo

    def prev(v):
        r = pltpu.roll(v, 1, 1)
        return jnp.where(at_first, pltpu.roll(r, 4, 0), r)

    def following(v):
        r = pltpu.roll(v, LANES - 1, 1)
        return jnp.where(at_last, pltpu.roll(r, 4, 0), r)

    def y_step(values, l):
        return advect(values, [following(v) for v in values], [prev(v) for v in values],
                      rates[2, c, l], rates[3, c, l], [turn[1, t, c, l] for t in every], 2, y_masks)

    carried = [None] * tracers
    for l in range(levels):
        sides = [[side(t, l) for t in every] for side in (own, east_side, west_side)]
        values = advect(*sides, east_rate(l), rates[1, c, l], [turn[0, t, c, l] for t in every], 1, x_masks)
        values = y_step(values, l)
        for t in every:
            v = values[t] * factors[0, c, l]
            if l > 0:
                v = v + factors[2, c, l] * carried[t]
            carried[t] = v
            out[t, l] = v
    for l in range(levels - 1, -1, -1):
        if l < levels - 1:
            for t in every:
                carried[t] = out[t, l] - factors[1, c, l] * carried[t]
        values = y_step(carried, l)
        for t in every:
            out[t, l] = values[t]


def tiles(ref, levels):
    if len(ref.shape) == 4:
        return lambda t, l: ref[t, l]
    return lambda t, l: ref[(t * levels + l) * 8 : (t * levels + l + 1) * 8]


def west_kernel(message, col1, west_halo, rates, factors, turn, out):
    levels = out.shape[1]
    middle(0, tiles(message, levels), tiles(col1, levels), tiles(west_halo, levels),
           lambda l: rates[0, 0, l], rates, factors, turn, out)


def inner_kernel(message, col1, col2, rates, factors, turn, out):
    levels = out.shape[1]
    middle(1, tiles(col1, levels), tiles(col2, levels), tiles(message, levels),
           lambda l: rates[0, 1, l], rates, factors, turn, out)


def east_kernel(col1, col2, halo, rates, factors, turn, before, out, east):
    levels = out.shape[1]
    upper_block = lax.broadcasted_iota(jnp.int32, (8, LANES), 0) >= MOMENTS
    rows = [face_row(halo.shape[0], levels, b) for b in range(2)]

    def east_rate(l):
        flux = spread(upper_block, halo, ((), rows[0] + l), ((), rows[1] + l))
        east[l] = jnp.maximum(flux, 0.0) * rates[0, 2, l]
        return east[l]

    middle(2, tiles(col2, levels), tiles(halo, levels), tiles(col1, levels), east_rate, rates, factors, turn, out)


def finish(c, own, east_side, west_side, east_rate, rates, turn, out, buf, sems):
    tracers, levels = buf.shape[0], buf.shape[1]
    masks = tile_masks(1)
    every = range(tracers)
    copies = []
    for part in range(2):
        low, high = part * levels // 2, (part + 1) * levels // 2
        for l in range(low, high):
            values = advect(*([side[t, l] for t in every] for side in (own, east_side, west_side)),
                            east_rate(l), rates[1, c, l], [turn[0, t, c, l] for t in every], 1, masks)
            for t in every:
                buf[t, l] = values[t]
        for t in every:
            span = pl.ds(low, high - low)
            copies.append(pltpu.make_async_copy(buf.at[t, span], out.at[t, c, span], sems.at[part, t]))
            copies[-1].start()
    for copy in copies:
        copy.wait()


def last_inner_kernel(mid0, mid1, mid2, rates, turn, out, buf, sems):
    finish(1, mid1, mid2, mid0, lambda l: rates[0, 1, l], rates, turn, out, buf, sems)


def last_east_kernel(begun, mid1, mid2, halo, east, rates, turn, out, buf, sems):
    finish(2, mid2, halo, mid1, lambda l: east[l], rates, turn, out, buf, sems)


def last_west_kernel(begun, mid0, mid1, halo, rates, turn, out, buf, sems):
    finish(0, mid0, mid1, halo, lambda l: rates[0, 0, l], rates, turn, out, buf, sems)


def body(state_adjoint, switches, flags, air_mass, x_flux, y_flux, vertical_mixing):
    state = state_view(state_adjoint)
    switch = pair_view(switches)
    flag = pair_view(flags[None])[0]
    tracers, columns, levels = state.shape[:3]
    order = lax.axis_index("trc").astype(jnp.int32).reshape(1)
    column = f32(tracers, levels, 8, LANES)
    rows = -(-2 * columns * levels // 8) * 8
    length = tracers * levels + -(-2 * levels // 8)
    dma = pltpu.SemaphoreType.DMA
    fields = tuple(stay(x) for x in (air_mass, x_flux, y_flux, vertical_mixing))

    message, col1, col2, packed, flag = call(
        head_kernel,
        (f32(length, 8, LANES), column, column, f32(rows, LANES), jax.ShapeDtypeStruct(flag.shape, flag.dtype)),
        (HBM,) * 6, [pltpu.VMEM(x.shape, x.dtype) for x in fields] + [dma((5,)), dma((columns, tracers))],
        10**5, 10**6, stay(state), stay(flag), *fields)
    west_halo = shifted(col2, "lon", 1)
    others = [swapped(packed, "trc", mask) for mask in (1, 2, 3)]
    turn = call(turn_kernel, f32(2, tracers, columns, levels, 8, LANES), (VMEM,), (), 10**6, 10**6, switch)
    rates, factors, message = call(
        pre_kernel,
        (f32(4, columns, levels, 8, LANES), f32(3, columns, levels, 8, LANES), f32(length * 8, LANES)),
        (VMEM,) * 5 + (SMEM, VMEM, VMEM, VMEM), [pltpu.VMEM((4, columns, 2, levels, LANES), jnp.float32)],
        10**6, 10**6, packed, *others, flag, order, message.reshape(length * 8, LANES), west_halo, turn, aliases={6: 2})
    east_message = shifted(message, "lon", -1)
    mid0 = call(west_kernel, column, (VMEM,) * 6, (), 10**6, 10**6, message, col1, west_halo, rates, factors, turn)
    east_halo = shifted(mid0, "lon", -1)
    mid1 = call(inner_kernel, column, (VMEM,) * 6, (), 10**6, 10**6, message, col1, col2, rates, factors, turn)
    mid2, east = call(east_kernel, (column, f32(levels, 8, LANES)), (VMEM,) * 7, (), 10**6, 10**6,
                      col1, col2, east_message, rates, factors, turn, mid0)
    west_halo = shifted(mid2, "lon", 1)

    def last(kernel, aliases, *args):
        first = (HBM,) * len(aliases)
        return call(kernel, f32(*state.shape), first + (VMEM,) * (len(args) - len(first)),
                    [pltpu.VMEM(column.shape, jnp.float32), dma((2, tracers))], 10**6, 10**6,
                    *args, out_specs=HBM, aliases=aliases)

    out = last(last_inner_kernel, {}, mid0, mid1, mid2, rates, turn)
    out = last(last_east_kernel, {0: 0}, out, mid1, mid2, east_halo, east, rates, turn)
    out = last(last_west_kernel, {0: 0}, out, mid0, mid1, west_halo, rates, turn)
    return state_back(out)


def solution(mesh):
    placed = (
        P("trc", None, "lon", None, None),
        P("trc", None, "lon", None, None),
        P(None, "lon", None, None),
        P("lon", None, "trc"),
        P("lon", None, "trc"),
        P("lon", None, "trc"),
        P("lon", None, "trc"),
    )
    return jax.shard_map(
        body,
        mesh=mesh,
        in_specs=placed,
        out_specs=P("trc", None, "lon", None, None),
        check_vma=False,
    )
```

```python
import jax
import jax.numpy as jnp
from jax import lax
from jax.experimental import pallas as pl
from jax.experimental.pallas import tpu as pltpu
from jax.sharding import PartitionSpec as P

LANES = 128
MOMENTS = 4
VMEM = pl.BlockSpec(memory_space=pltpu.VMEM)
SMEM = pl.BlockSpec(memory_space=pltpu.SMEM)
HBM = pl.BlockSpec(memory_space=pltpu.HBM)


def state_view(x):
    t, m, c, l, n = x.shape
    b = n // LANES
    x = x.reshape(t, m, c, l, b, LANES).transpose(0, 2, 3, 4, 1, 5)
    return x.reshape(t, c, l, b * m, LANES)


def pair_view(x):
    t, d, c, l, n = x.shape
    b = n // LANES
    x = x.reshape(t, d, c, l, b, LANES).transpose(0, 2, 3, 4, 1, 5)
    return x.reshape(t, c, l * b * d, LANES)


def state_back(y):
    t, c, l, rows, _ = y.shape
    b = rows // MOMENTS
    y = y.reshape(t, c, l, b, MOMENTS, LANES).transpose(0, 4, 1, 2, 3, 5)
    return y.reshape(t, MOMENTS, c, l, b * LANES)


def shifted(value, axis, by):
    count = lax.axis_size(axis)
    return lax.ppermute(value, axis, [(i, (i + by) % count) for i in range(count)])


def swapped(value, axis, mask):
    count = lax.axis_size(axis)
    return lax.ppermute(value, axis, [(i, i ^ mask) for i in range(count)])


def call(kernel, out, in_specs, scratch, flops, moved, *args, out_specs=None, aliases=None):
    return pl.pallas_call(
        kernel,
        out_shape=out,
        in_specs=in_specs,
        out_specs=jax.tree.map(lambda _: VMEM, out) if out_specs is None else out_specs,
        scratch_shapes=scratch,
        input_output_aliases=aliases or {},
        compiler_params=pltpu.CompilerParams(vmem_limit_bytes=24 * 1024 * 1024),
        cost_estimate=pl.CostEstimate(flops=flops, bytes_accessed=moved, transcendentals=0),
    )(*args)


def stay(x):
    return pltpu.with_memory_space_constraint(x, pltpu.HBM)


def f32(*shape):
    return jax.ShapeDtypeStruct(shape, jnp.float32)


def tile_masks(slope):
    row = lax.broadcasted_iota(jnp.int32, (8, LANES), 0) % MOMENTS
    return row == 0, row == slope


def head_kernel(state, flags, mass, xf, yf, km, message, col1, col2, packed, flags_v, mass_v, xf_v, yf_v, km_v, sems, column_sems):
    tracers, columns, levels = state.shape[0], mass.shape[0], mass.shape[1]
    half = LANES // 2
    pairs = ((mass, mass_v), (xf, xf_v), (yf, yf_v), (km, km_v), (flags, flags_v))
    copies = [pltpu.make_async_copy(src, dst, sems.at[i]) for i, (src, dst) in enumerate(pairs)]
    for t in range(tracers):
        for c, place in ((2, col2.at[t]), (0, message.at[pl.ds(t * levels, levels)]), (1, col1.at[t])):
            copies.append(pltpu.make_async_copy(state.at[t, c], place, column_sems.at[c, t]))
    for copy in copies:
        copy.start()
    for copy in copies[:4]:
        copy.wait()
    for c in range(columns):
        low, top = c * levels, (columns + c) * levels
        packed[low : low + levels, :half] = mass_v[c]
        packed[low : low + levels, half:] = xf_v[c]
        packed[top : top + levels, :half] = yf_v[c]
        packed[top : top + levels - 1, half:] = km_v[c]
        packed[top + levels - 1 : top + levels, half:] = jnp.zeros((1, half), jnp.float32)
    for copy in copies[4:]:
        copy.wait()


def spread(upper_block, ref, *where):
    blocks = [jnp.broadcast_to(ref[(*index, pl.ds(r, 1), slice(None))], (8, LANES)) for index, r in where]
    return jnp.where(upper_block, blocks[1], blocks[0])


def face_row(rows, levels, b):
    return rows - -(-2 * levels // 8) * 8 + b * levels


def turn_kernel(switches, turn):
    tracers, columns = switches.shape[:2]
    levels = switches.shape[2] // 4
    row = lax.broadcasted_iota(jnp.int32, (8, LANES), 0)
    moment = row % MOMENTS
    for t in range(tracers):
        for c in range(columns):
            for l in range(levels):
                for d in range(2):
                    base = l * 4 + d
                    sw = spread(row >= MOMENTS, switches, ((t, c), base), ((t, c), base + 2))
                    take = jnp.where(sw == 1, 1.0, jnp.where(sw == 2, -1.0, 0.0))
                    keep = jnp.where(sw == 0, 1.0, 0.0)
                    turn[d, t, c, l] = jnp.where(moment == 0, take, jnp.where(moment == 1 + d, keep, 1.0))


def pre_kernel(own, first, second, third, flags, order, begun, before, also, rates, factors, message, fields):
    columns, levels = rates.shape[1], rates.shape[2]
    half = LANES // 2
    odd = order[0] % 2 == 1
    high = order[0] >= 2
    lane = lax.broadcasted_iota(jnp.int32, (8, LANES), 1)
    row = lax.broadcasted_iota(jnp.int32, (8, LANES), 0)
    upper_block = row >= MOMENTS
    lane_low = lax.broadcasted_iota(jnp.int32, (levels, LANES), 1) < half

    def sorted_shards(start, count):
        a, b, c, d = (ref[start : start + count] for ref in (own, first, second, third))
        a, b, c, d = (jnp.where(odd, b, a), jnp.where(odd, a, b), jnp.where(odd, d, c), jnp.where(odd, c, d))
        return (jnp.where(high, c, a), jnp.where(high, d, b), jnp.where(high, a, c), jnp.where(high, b, d))

    for pair in range(2):
        for c in range(columns):
            shards = sorted_shards((pair * columns + c) * levels, levels)
            for b in range(2):
                lo, hi = shards[2 * b], shards[2 * b + 1]
                fields[2 * pair, c, b] = jnp.where(lane_low, lo, pltpu.roll(hi, half, 1))
                flux = jnp.where(lane_low, pltpu.roll(lo, half, 1), hi)
                fields[2 * pair + 1, c, b] = flux
                if pair == 0 and c == 0:
                    eastward = flags[0, pl.ds(2 * b, levels, stride=4), :].astype(jnp.float32)
                    start = face_row(message.shape[0], levels, b)
                    message[start : start + levels] = (2.0 * eastward - 1.0) * flux

    def field(f, c, l):
        return spread(upper_block, fields, ((f, c, 0), l), ((f, c, 1), l))

    def flag(c, l, d):
        base = l * 4 + d
        return spread(upper_block, flags, ((c,), base), ((c,), base + 2)).astype(jnp.float32)

    first_row = (lane == 0) & (row < MOMENTS)
    last_row = (lane == LANES - 1) & (row >= MOMENTS)
    for l in range(levels):
        flux_x = [field(1, c, l) for c in range(columns)]
        flag_x = [flag(c, l, 0) for c in range(columns)]
        east = [flag_x[c] * flux_x[c] for c in range(columns)]
        west = [flux_x[c] - east[c] for c in range(columns)]
        east.append(1.0)
        for c in range(columns):
            share = 1.0 / field(0, c, l)
            rates[0, c, l] = east[c + 1] * share
            rates[1, c, l] = west[c] * share
            flux_y = field(2, c, l)
            north = flag(c, l, 1) * flux_y
            south = pltpu.roll(flux_y - north, 1, 1)
            south = jnp.where(lane == 0, pltpu.roll(south, 4, 0), south)
            rates[2, c, l] = jnp.where(last_row, 0.0, north) * share
            rates[3, c, l] = jnp.where(first_row, 0.0, south) * share

    fixed = row % MOMENTS == 3
    zero = jnp.zeros((8, LANES), jnp.float32)
    below, upper = [None] * columns, [None] * columns
    for l in range(levels):
        for c in range(columns):
            diagonal = zero + 1.0
            if l > 0:
                diagonal = diagonal + below[c]
            if l < levels - 1:
                above = field(3, c, l)
                diagonal = diagonal + above
            if l > 0:
                diagonal = diagonal + below[c] * upper[c]
            inverse = 1.0 / diagonal
            factors[0, c, l] = jnp.where(fixed, 1.0, inverse)
            factors[2, c, l] = jnp.where(fixed, 0.0, below[c] * inverse) if l > 0 else zero
            if l < levels - 1:
                upper[c] = -above * inverse
                factors[1, c, l] = jnp.where(fixed, 0.0, upper[c])
                below[c] = above
            else:
                factors[1, c, l] = zero


def advect(own, east_side, west_side, east, west, turns, slope, masks):
    is_mass, is_slope = masks
    stay = 1.0 - (east + west)
    east_part = east * jnp.where(is_slope, east, 1.0)
    west_part = west * jnp.where(is_slope, west, 1.0)
    east_cross = east * (1.0 - east)
    west_cross = west * (1.0 - west)
    out = []
    for s, e, w, z in zip(own, east_side, west_side, turns):
        total = stay * s + east_part * e + west_part * w
        cross = east_cross * (e - s) - west_cross * (w - s)
        total = total + jnp.where(is_slope, pltpu.roll(cross, slope, 0), 0.0)
        slope_up = pltpu.roll(total, 8 - slope, 0)
        out.append(z * jnp.where(is_mass, slope_up, total) + jnp.where(is_mass, total, 0.0))
    return out


def middle(todo, own, east_side, west_side, east_rate, rates, factors, turn, out):
    tracers, levels = out.shape[0], out.shape[1]
    lane = lax.broadcasted_iota(jnp.int32, (8, LANES), 1)
    at_first, at_last = lane == 0, lane == LANES - 1
    x_masks, y_masks = tile_masks(1), tile_masks(2)
    every = range(tracers)
    c = todo

    def prev(v):
        r = pltpu.roll(v, 1, 1)
        return jnp.where(at_first, pltpu.roll(r, 4, 0), r)

    def following(v):
        r = pltpu.roll(v, LANES - 1, 1)
        return jnp.where(at_last, pltpu.roll(r, 4, 0), r)

    def y_step(values, l):
        return advect(values, [following(v) for v in values], [prev(v) for v in values],
                      rates[2, c, l], rates[3, c, l], [turn[1, t, c, l] for t in every], 2, y_masks)

    carried = [None] * tracers
    for l in range(levels):
        sides = [[side(t, l) for t in every] for side in (own, east_side, west_side)]
        values = advect(*sides, east_rate(l), rates[1, c, l], [turn[0, t, c, l] for t in every], 1, x_masks)
        values = y_step(values, l)
        for t in every:
            v = values[t] * factors[0, c, l]
            if l > 0:
                v = v + factors[2, c, l] * carried[t]
            carried[t] = v
            out[t, l] = v
    for l in range(levels - 1, -1, -1):
        if l < levels - 1:
            for t in every:
                carried[t] = out[t, l] - factors[1, c, l] * carried[t]
        values = y_step(carried, l)
        for t in every:
            out[t, l] = values[t]


def tiles(ref, levels):
    if len(ref.shape) == 4:
        return lambda t, l: ref[t, l]
    return lambda t, l: ref[(t * levels + l) * 8 : (t * levels + l + 1) * 8]


def west_kernel(message, col1, west_halo, rates, factors, turn, out):
    levels = out.shape[1]
    middle(0, tiles(message, levels), tiles(col1, levels), tiles(west_halo, levels),
           lambda l: rates[0, 0, l], rates, factors, turn, out)


def inner_kernel(message, col1, col2, rates, factors, turn, out):
    levels = out.shape[1]
    middle(1, tiles(col1, levels), tiles(col2, levels), tiles(message, levels),
           lambda l: rates[0, 1, l], rates, factors, turn, out)


def east_kernel(col1, col2, halo, rates, factors, turn, before, out, east):
    levels = out.shape[1]
    upper_block = lax.broadcasted_iota(jnp.int32, (8, LANES), 0) >= MOMENTS
    rows = [face_row(halo.shape[0], levels, b) for b in range(2)]

    def east_rate(l):
        flux = spread(upper_block, halo, ((), rows[0] + l), ((), rows[1] + l))
        east[l] = jnp.maximum(flux, 0.0) * rates[0, 2, l]
        return east[l]

    middle(2, tiles(col2, levels), tiles(halo, levels), tiles(col1, levels), east_rate, rates, factors, turn, out)


def finish(c, own, east_side, west_side, east_rate, rates, turn, out, buf, sems):
    tracers, levels = buf.shape[0], buf.shape[1]
    masks = tile_masks(1)
    every = range(tracers)
    copies = []
    for part in range(2):
        low, high = part * levels // 2, (part + 1) * levels // 2
        for l in range(low, high):
            values = advect(*([side[t, l] for t in every] for side in (own, east_side, west_side)),
                            east_rate(l), rates[1, c, l], [turn[0, t, c, l] for t in every], 1, masks)
            for t in every:
                buf[t, l] = values[t]
        for t in every:
            span = pl.ds(low, high - low)
            copies.append(pltpu.make_async_copy(buf.at[t, span], out.at[t, c, span], sems.at[part, t]))
            copies[-1].start()
    for copy in copies:
        copy.wait()


def last_inner_kernel(mid0, mid1, mid2, rates, turn, out, buf, sems):
    finish(1, mid1, mid2, mid0, lambda l: rates[0, 1, l], rates, turn, out, buf, sems)


def last_east_kernel(begun, mid1, mid2, halo, east, rates, turn, out, buf, sems):
    finish(2, mid2, halo, mid1, lambda l: east[l], rates, turn, out, buf, sems)


def last_west_kernel(begun, mid0, mid1, halo, rates, turn, out, buf, sems):
    finish(0, mid0, mid1, halo, lambda l: rates[0, 0, l], rates, turn, out, buf, sems)


def body(state_adjoint, switches, flags, air_mass, x_flux, y_flux, vertical_mixing):
    state = state_view(state_adjoint)
    switch = pair_view(switches)
    flag = pair_view(flags[None])[0]
    tracers, columns, levels = state.shape[:3]
    order = lax.axis_index("trc").astype(jnp.int32).reshape(1)
    column = f32(tracers, levels, 8, LANES)
    rows = -(-2 * columns * levels // 8) * 8
    length = tracers * levels + -(-2 * levels // 8)
    dma = pltpu.SemaphoreType.DMA
    fields = tuple(stay(x) for x in (air_mass, x_flux, y_flux, vertical_mixing))

    message, col1, col2, packed, flag = call(
        head_kernel,
        (f32(length, 8, LANES), column, column, f32(rows, LANES), jax.ShapeDtypeStruct(flag.shape, flag.dtype)),
        (HBM,) * 6, [pltpu.VMEM(x.shape, x.dtype) for x in fields] + [dma((5,)), dma((columns, tracers))],
        10**5, 10**6, stay(state), stay(flag), *fields)
    west_halo = shifted(col2, "lon", 1)
    across = swapped(packed, "trc", 2)
    others = [swapped(packed, "trc", 1), across, swapped(across, "trc", 1)]
    turn = call(turn_kernel, f32(2, tracers, columns, levels, 8, LANES), (VMEM,), (), 10**6, 10**6, switch)
    rates, factors, message = call(
        pre_kernel,
        (f32(4, columns, levels, 8, LANES), f32(3, columns, levels, 8, LANES), f32(length * 8, LANES)),
        (VMEM,) * 5 + (SMEM, VMEM, VMEM, VMEM), [pltpu.VMEM((4, columns, 2, levels, LANES), jnp.float32)],
        10**6, 10**6, packed, *others, flag, order, message.reshape(length * 8, LANES), west_halo, turn, aliases={6: 2})
    east_message = shifted(message, "lon", -1)
    mid0 = call(west_kernel, column, (VMEM,) * 6, (), 10**6, 10**6, message, col1, west_halo, rates, factors, turn)
    east_halo = shifted(mid0, "lon", -1)
    mid1 = call(inner_kernel, column, (VMEM,) * 6, (), 10**6, 10**6, message, col1, col2, rates, factors, turn)
    mid2, east = call(east_kernel, (column, f32(levels, 8, LANES)), (VMEM,) * 7, (), 10**6, 10**6,
                      col1, col2, east_message, rates, factors, turn, mid0)
    west_halo = shifted(mid2, "lon", 1)

    def last(kernel, aliases, *args):
        first = (HBM,) * len(aliases)
        return call(kernel, f32(*state.shape), first + (VMEM,) * (len(args) - len(first)),
                    [pltpu.VMEM(column.shape, jnp.float32), dma((2, tracers))], 10**6, 10**6,
                    *args, out_specs=HBM, aliases=aliases)

    out = last(last_inner_kernel, {}, mid0, mid1, mid2, rates, turn)
    out = last(last_east_kernel, {0: 0}, out, mid1, mid2, east_halo, east, rates, turn)
    out = last(last_west_kernel, {0: 0}, out, mid0, mid1, west_halo, rates, turn)
    return state_back(out)


def solution(mesh):
    placed = (
        P("trc", None, "lon", None, None),
        P("trc", None, "lon", None, None),
        P(None, "lon", None, None),
        P("lon", None, "trc"),
        P("lon", None, "trc"),
        P("lon", None, "trc"),
        P("lon", None, "trc"),
    )
    return jax.shard_map(
        body,
        mesh=mesh,
        in_specs=placed,
        out_specs=P("trc", None, "lon", None, None),
        check_vma=False,
    )
```

```python
import jax
import jax.numpy as jnp
from jax import lax
from jax.experimental import pallas as pl
from jax.experimental.pallas import tpu as pltpu
from jax.sharding import PartitionSpec as P

LANES = 128
MOMENTS = 4
VMEM = pl.BlockSpec(memory_space=pltpu.VMEM)
SMEM = pl.BlockSpec(memory_space=pltpu.SMEM)
HBM = pl.BlockSpec(memory_space=pltpu.HBM)


def state_view(x):
    t, m, c, l, n = x.shape
    b = n // LANES
    x = x.reshape(t, m, c, l, b, LANES).transpose(0, 2, 3, 4, 1, 5)
    return x.reshape(t, c, l, b * m, LANES)


def pair_view(x):
    t, d, c, l, n = x.shape
    b = n // LANES
    x = x.reshape(t, d, c, l, b, LANES).transpose(0, 2, 3, 4, 1, 5)
    return x.reshape(t, c, l * b * d, LANES)


def state_back(y):
    t, c, l, rows, _ = y.shape
    b = rows // MOMENTS
    y = y.reshape(t, c, l, b, MOMENTS, LANES).transpose(0, 4, 1, 2, 3, 5)
    return y.reshape(t, MOMENTS, c, l, b * LANES)


def shifted(value, axis, by):
    count = lax.axis_size(axis)
    return lax.ppermute(value, axis, [(i, (i + by) % count) for i in range(count)])


def swapped(value, axis, mask):
    count = lax.axis_size(axis)
    return lax.ppermute(value, axis, [(i, i ^ mask) for i in range(count)])


def call(kernel, out, in_specs, scratch, flops, moved, *args, out_specs=None, aliases=None):
    return pl.pallas_call(
        kernel,
        out_shape=out,
        in_specs=in_specs,
        out_specs=jax.tree.map(lambda _: VMEM, out) if out_specs is None else out_specs,
        scratch_shapes=scratch,
        input_output_aliases=aliases or {},
        compiler_params=pltpu.CompilerParams(vmem_limit_bytes=24 * 1024 * 1024),
        cost_estimate=pl.CostEstimate(flops=flops, bytes_accessed=moved, transcendentals=0),
    )(*args)


def stay(x):
    return pltpu.with_memory_space_constraint(x, pltpu.HBM)


def f32(*shape):
    return jax.ShapeDtypeStruct(shape, jnp.float32)


def tile_masks(slope):
    row = lax.broadcasted_iota(jnp.int32, (8, LANES), 0) % MOMENTS
    return row == 0, row == slope


def head_kernel(state, flags, mass, xf, yf, km, col0, col1, col2, packed, flags_v, mass_v, xf_v, yf_v, km_v, sems, column_sems):
    tracers, columns, levels = state.shape[0], mass.shape[0], mass.shape[1]
    half = LANES // 2
    pairs = ((mass, mass_v), (xf, xf_v), (yf, yf_v), (km, km_v), (flags, flags_v))
    copies = [pltpu.make_async_copy(src, dst, sems.at[i]) for i, (src, dst) in enumerate(pairs)]
    for t in range(tracers):
        for c, place in ((2, col2.at[t]), (0, col0.at[t]), (1, col1.at[t])):
            copies.append(pltpu.make_async_copy(state.at[t, c], place, column_sems.at[c, t]))
    for copy in copies:
        copy.start()
    for copy in copies[:4]:
        copy.wait()
    for c in range(columns):
        low, top = c * levels, (columns + c) * levels
        packed[low : low + levels, :half] = mass_v[c]
        packed[low : low + levels, half:] = xf_v[c]
        packed[top : top + levels, :half] = yf_v[c]
        packed[top : top + levels - 1, half:] = km_v[c]
        packed[top + levels - 1 : top + levels, half:] = jnp.zeros((1, half), jnp.float32)
    for copy in copies[4:]:
        copy.wait()


def spread(upper_block, ref, *where):
    blocks = [jnp.broadcast_to(ref[(*index, pl.ds(r, 1), slice(None))], (8, LANES)) for index, r in where]
    return jnp.where(upper_block, blocks[1], blocks[0])


def turn_kernel(switches, turn):
    tracers, columns = switches.shape[:2]
    levels = switches.shape[2] // 4
    row = lax.broadcasted_iota(jnp.int32, (8, LANES), 0)
    moment = row % MOMENTS
    for t in range(tracers):
        for c in range(columns):
            for l in range(levels):
                for d in range(2):
                    base = l * 4 + d
                    sw = spread(row >= MOMENTS, switches, ((t, c), base), ((t, c), base + 2))
                    take = jnp.where(sw == 1, 1.0, jnp.where(sw == 2, -1.0, 0.0))
                    keep = jnp.where(sw == 0, 1.0, 0.0)
                    turn[d, t, c, l] = jnp.where(moment == 0, take, jnp.where(moment == 1 + d, keep, 1.0))


def pre_kernel(own, first, second, third, flags, order, before, also, rates, factors, face, fields):
    columns, levels = rates.shape[1], rates.shape[2]
    half = LANES // 2
    odd = order[0] % 2 == 1
    high = order[0] >= 2
    lane = lax.broadcasted_iota(jnp.int32, (8, LANES), 1)
    row = lax.broadcasted_iota(jnp.int32, (8, LANES), 0)
    upper_block = row >= MOMENTS
    lane_low = lax.broadcasted_iota(jnp.int32, (levels, LANES), 1) < half

    def sorted_shards(start, count):
        a, b, c, d = (ref[start : start + count] for ref in (own, first, second, third))
        a, b, c, d = (jnp.where(odd, b, a), jnp.where(odd, a, b), jnp.where(odd, d, c), jnp.where(odd, c, d))
        return (jnp.where(high, c, a), jnp.where(high, d, b), jnp.where(high, a, c), jnp.where(high, b, d))

    for pair in range(2):
        for c in range(columns):
            shards = sorted_shards((pair * columns + c) * levels, levels)
            for b in range(2):
                lo, hi = shards[2 * b], shards[2 * b + 1]
                fields[2 * pair, c, b] = jnp.where(lane_low, lo, pltpu.roll(hi, half, 1))
                flux = jnp.where(lane_low, pltpu.roll(lo, half, 1), hi)
                fields[2 * pair + 1, c, b] = flux
                if pair == 0 and c == 0:
                    eastward = flags[0, pl.ds(2 * b, levels, stride=4), :].astype(jnp.float32)
                    face[b * levels : (b + 1) * levels] = (2.0 * eastward - 1.0) * flux

    def field(f, c, l):
        return spread(upper_block, fields, ((f, c, 0), l), ((f, c, 1), l))

    def flag(c, l, d):
        base = l * 4 + d
        return spread(upper_block, flags, ((c,), base), ((c,), base + 2)).astype(jnp.float32)

    first_row = (lane == 0) & (row < MOMENTS)
    last_row = (lane == LANES - 1) & (row >= MOMENTS)
    for l in range(levels):
        flux_x = [field(1, c, l) for c in range(columns)]
        flag_x = [flag(c, l, 0) for c in range(columns)]
        east = [flag_x[c] * flux_x[c] for c in range(columns)]
        west = [flux_x[c] - east[c] for c in range(columns)]
        east.append(1.0)
        for c in range(columns):
            share = 1.0 / field(0, c, l)
            rates[0, c, l] = east[c + 1] * share
            rates[1, c, l] = west[c] * share
            flux_y = field(2, c, l)
            north = flag(c, l, 1) * flux_y
            south = pltpu.roll(flux_y - north, 1, 1)
            south = jnp.where(lane == 0, pltpu.roll(south, 4, 0), south)
            rates[2, c, l] = jnp.where(last_row, 0.0, north) * share
            rates[3, c, l] = jnp.where(first_row, 0.0, south) * share

    fixed = row % MOMENTS == 3
    zero = jnp.zeros((8, LANES), jnp.float32)
    below, upper = [None] * columns, [None] * columns
    for l in range(levels):
        for c in range(columns):
            diagonal = zero + 1.0
            if l > 0:
                diagonal = diagonal + below[c]
            if l < levels - 1:
                above = field(3, c, l)
                diagonal = diagonal + above
            if l > 0:
                diagonal = diagonal + below[c] * upper[c]
            inverse = 1.0 / diagonal
            factors[0, c, l] = jnp.where(fixed, 1.0, inverse)
            factors[2, c, l] = jnp.where(fixed, 0.0, below[c] * inverse) if l > 0 else zero
            if l < levels - 1:
                upper[c] = -above * inverse
                factors[1, c, l] = jnp.where(fixed, 0.0, upper[c])
                below[c] = above
            else:
                factors[1, c, l] = zero


def advect(own, east_side, west_side, east, west, turns, slope, masks):
    is_mass, is_slope = masks
    stay = 1.0 - (east + west)
    east_part = east * jnp.where(is_slope, east, 1.0)
    west_part = west * jnp.where(is_slope, west, 1.0)
    east_cross = east * (1.0 - east)
    west_cross = west * (1.0 - west)
    out = []
    for s, e, w, z in zip(own, east_side, west_side, turns):
        total = stay * s + east_part * e + west_part * w
        cross = east_cross * (e - s) - west_cross * (w - s)
        total = total + jnp.where(is_slope, pltpu.roll(cross, slope, 0), 0.0)
        slope_up = pltpu.roll(total, 8 - slope, 0)
        out.append(z * jnp.where(is_mass, slope_up, total) + jnp.where(is_mass, total, 0.0))
    return out


def middle(todo, own, east_side, west_side, east_rate, rates, factors, turn, out):
    tracers, levels = out.shape[0], out.shape[1]
    lane = lax.broadcasted_iota(jnp.int32, (8, LANES), 1)
    at_first, at_last = lane == 0, lane == LANES - 1
    x_masks, y_masks = tile_masks(1), tile_masks(2)
    every = range(tracers)
    c = todo

    def prev(v):
        r = pltpu.roll(v, 1, 1)
        return jnp.where(at_first, pltpu.roll(r, 4, 0), r)

    def following(v):
        r = pltpu.roll(v, LANES - 1, 1)
        return jnp.where(at_last, pltpu.roll(r, 4, 0), r)

    def y_step(values, l):
        return advect(values, [following(v) for v in values], [prev(v) for v in values],
                      rates[2, c, l], rates[3, c, l], [turn[1, t, c, l] for t in every], 2, y_masks)

    carried = [None] * tracers
    for l in range(levels):
        sides = [[side(t, l) for t in every] for side in (own, east_side, west_side)]
        values = advect(*sides, east_rate(l), rates[1, c, l], [turn[0, t, c, l] for t in every], 1, x_masks)
        values = y_step(values, l)
        for t in every:
            v = values[t] * factors[0, c, l]
            if l > 0:
                v = v + factors[2, c, l] * carried[t]
            carried[t] = v
            out[t, l] = v
    for l in range(levels - 1, -1, -1):
        if l < levels - 1:
            for t in every:
                carried[t] = out[t, l] - factors[1, c, l] * carried[t]
        values = y_step(carried, l)
        for t in every:
            out[t, l] = values[t]


def tiles(ref):
    return lambda t, l: ref[t, l]


def west_kernel(col0, col1, west_halo, rates, factors, turn, out):
    middle(0, tiles(col0), tiles(col1), tiles(west_halo), lambda l: rates[0, 0, l], rates, factors, turn, out)


def inner_kernel(col0, col1, col2, rates, factors, turn, out):
    middle(1, tiles(col1), tiles(col2), tiles(col0), lambda l: rates[0, 1, l], rates, factors, turn, out)


def east_kernel(col1, col2, east_halo, face, rates, factors, turn, before, out, east):
    levels = out.shape[1]
    upper_block = lax.broadcasted_iota(jnp.int32, (8, LANES), 0) >= MOMENTS

    def east_rate(l):
        flux = spread(upper_block, face, ((), l), ((), levels + l))
        east[l] = jnp.maximum(flux, 0.0) * rates[0, 2, l]
        return east[l]

    middle(2, tiles(col2), tiles(east_halo), tiles(col1), east_rate, rates, factors, turn, out)


def finish(c, own, east_side, west_side, east_rate, rates, turn, out, buf, sems):
    tracers, levels = buf.shape[0], buf.shape[1]
    masks = tile_masks(1)
    every = range(tracers)
    copies = []
    for part in range(2):
        low, high = part * levels // 2, (part + 1) * levels // 2
        for l in range(low, high):
            values = advect(*([side[t, l] for t in every] for side in (own, east_side, west_side)),
                            east_rate(l), rates[1, c, l], [turn[0, t, c, l] for t in every], 1, masks)
            for t in every:
                buf[t, l] = values[t]
        for t in every:
            span = pl.ds(low, high - low)
            copies.append(pltpu.make_async_copy(buf.at[t, span], out.at[t, c, span], sems.at[part, t]))
            copies[-1].start()
    for copy in copies:
        copy.wait()


def last_inner_kernel(mid0, mid1, mid2, rates, turn, out, buf, sems):
    finish(1, mid1, mid2, mid0, lambda l: rates[0, 1, l], rates, turn, out, buf, sems)


def last_east_kernel(begun, mid1, mid2, halo, east, rates, turn, out, buf, sems):
    finish(2, mid2, halo, mid1, lambda l: east[l], rates, turn, out, buf, sems)


def last_west_kernel(begun, mid0, mid1, halo, rates, turn, out, buf, sems):
    finish(0, mid0, mid1, halo, lambda l: rates[0, 0, l], rates, turn, out, buf, sems)


def body(state_adjoint, switches, flags, air_mass, x_flux, y_flux, vertical_mixing):
    state = state_view(state_adjoint)
    switch = pair_view(switches)
    flag = pair_view(flags[None])[0]
    tracers, columns, levels = state.shape[:3]
    order = lax.axis_index("trc").astype(jnp.int32).reshape(1)
    column = f32(tracers, levels, 8, LANES)
    rows = -(-2 * columns * levels // 8) * 8
    dma = pltpu.SemaphoreType.DMA
    fields = tuple(stay(x) for x in (air_mass, x_flux, y_flux, vertical_mixing))

    col0, col1, col2, packed, flag = call(
        head_kernel,
        (column, column, column, f32(rows, LANES), jax.ShapeDtypeStruct(flag.shape, flag.dtype)),
        (HBM,) * 6, [pltpu.VMEM(x.shape, x.dtype) for x in fields] + [dma((5,)), dma((columns, tracers))],
        10**5, 10**6, stay(state), stay(flag), *fields)
    west_halo = shifted(col2, "lon", 1)
    east_halo = shifted(col0, "lon", -1)
    across = swapped(packed, "trc", 2)
    others = [swapped(packed, "trc", 1), across, swapped(across, "trc", 1)]
    turn = call(turn_kernel, f32(2, tracers, columns, levels, 8, LANES), (VMEM,), (), 10**6, 10**6, switch)
    rates, factors, face = call(
        pre_kernel,
        (f32(4, columns, levels, 8, LANES), f32(3, columns, levels, 8, LANES), f32(2 * levels, LANES)),
        (VMEM,) * 5 + (SMEM, VMEM, VMEM), [pltpu.VMEM((4, columns, 2, levels, LANES), jnp.float32)],
        10**6, 10**6, packed, *others, flag, order, west_halo, turn)
    face = shifted(face, "lon", -1)
    mid0 = call(west_kernel, column, (VMEM,) * 6, (), 10**6, 10**6, col0, col1, west_halo, rates, factors, turn)
    east_mid = shifted(mid0, "lon", -1)
    mid1 = call(inner_kernel, column, (VMEM,) * 6, (), 10**6, 10**6, col0, col1, col2, rates, factors, turn)
    mid2, east = call(east_kernel, (column, f32(levels, 8, LANES)), (VMEM,) * 8, (), 10**6, 10**6,
                      col1, col2, east_halo, face, rates, factors, turn, mid0)
    west_mid = shifted(mid2, "lon", 1)

    def last(kernel, aliases, *args):
        first = (HBM,) * len(aliases)
        return call(kernel, f32(*state.shape), first + (VMEM,) * (len(args) - len(first)),
                    [pltpu.VMEM(column.shape, jnp.float32), dma((2, tracers))], 10**6, 10**6,
                    *args, out_specs=HBM, aliases=aliases)

    out = last(last_inner_kernel, {}, mid0, mid1, mid2, rates, turn)
    out = last(last_east_kernel, {0: 0}, out, mid1, mid2, east_mid, east, rates, turn)
    out = last(last_west_kernel, {0: 0}, out, mid0, mid1, west_mid, rates, turn)
    return state_back(out)


def solution(mesh):
    placed = (
        P("trc", None, "lon", None, None),
        P("trc", None, "lon", None, None),
        P(None, "lon", None, None),
        P("lon", None, "trc"),
        P("lon", None, "trc"),
        P("lon", None, "trc"),
        P("lon", None, "trc"),
    )
    return jax.shard_map(
        body,
        mesh=mesh,
        in_specs=placed,
        out_specs=P("trc", None, "lon", None, None),
        check_vma=False,
    )
```

```python
import jax
import jax.numpy as jnp
from jax import lax
from jax.experimental import pallas as pl
from jax.experimental.pallas import tpu as pltpu
from jax.sharding import PartitionSpec as P

LANES = 128
MOMENTS = 4
VMEM = pl.BlockSpec(memory_space=pltpu.VMEM)
SMEM = pl.BlockSpec(memory_space=pltpu.SMEM)
HBM = pl.BlockSpec(memory_space=pltpu.HBM)


def state_view(x):
    t, m, c, l, n = x.shape
    b = n // LANES
    x = x.reshape(t, m, c, l, b, LANES).transpose(0, 2, 3, 4, 1, 5)
    return x.reshape(t, c, l, b * m, LANES)


def pair_view(x):
    t, d, c, l, n = x.shape
    b = n // LANES
    x = x.reshape(t, d, c, l, b, LANES).transpose(0, 2, 3, 4, 1, 5)
    return x.reshape(t, c, l * b * d, LANES)


def state_back(y):
    t, c, l, rows, _ = y.shape
    b = rows // MOMENTS
    y = y.reshape(t, c, l, b, MOMENTS, LANES).transpose(0, 4, 1, 2, 3, 5)
    return y.reshape(t, MOMENTS, c, l, b * LANES)


def shifted(value, axis, by):
    count = lax.axis_size(axis)
    return lax.ppermute(value, axis, [(i, (i + by) % count) for i in range(count)])


def swapped(value, axis, mask):
    count = lax.axis_size(axis)
    return lax.ppermute(value, axis, [(i, i ^ mask) for i in range(count)])


def call(kernel, out, in_specs, scratch, flops, moved, *args, out_specs=None, aliases=None):
    return pl.pallas_call(
        kernel,
        out_shape=out,
        in_specs=in_specs,
        out_specs=jax.tree.map(lambda _: VMEM, out) if out_specs is None else out_specs,
        scratch_shapes=scratch,
        input_output_aliases=aliases or {},
        compiler_params=pltpu.CompilerParams(vmem_limit_bytes=24 * 1024 * 1024),
        cost_estimate=pl.CostEstimate(flops=flops, bytes_accessed=moved, transcendentals=0),
    )(*args)


def stay(x):
    return pltpu.with_memory_space_constraint(x, pltpu.HBM)


def f32(*shape):
    return jax.ShapeDtypeStruct(shape, jnp.float32)


def tile_masks(slope):
    row = lax.broadcasted_iota(jnp.int32, (8, LANES), 0) % MOMENTS
    return row == 0, row == slope


def head_kernel(state, flags, mass, xf, yf, km, col0, message, col1, col2, packed, flags_v, mass_v, xf_v, yf_v, km_v, sems, column_sems):
    tracers, columns, levels = state.shape[0], mass.shape[0], mass.shape[1]
    half = LANES // 2
    pairs = ((mass, mass_v), (xf, xf_v), (yf, yf_v), (km, km_v), (flags, flags_v))
    copies = [pltpu.make_async_copy(src, dst, sems.at[i]) for i, (src, dst) in enumerate(pairs)]
    for t in range(tracers):
        first = message.at[pl.ds((t - 1) * levels, levels)] if t else col0.at[t]
        for c, place in ((2, col2.at[t]), (0, first), (1, col1.at[t])):
            copies.append(pltpu.make_async_copy(state.at[t, c], place, column_sems.at[c, t]))
    for copy in copies:
        copy.start()
    for copy in copies[:4]:
        copy.wait()
    for c in range(columns):
        low, top = c * levels, (columns + c) * levels
        packed[low : low + levels, :half] = mass_v[c]
        packed[low : low + levels, half:] = xf_v[c]
        packed[top : top + levels, :half] = yf_v[c]
        packed[top : top + levels - 1, half:] = km_v[c]
        packed[top + levels - 1 : top + levels, half:] = jnp.zeros((1, half), jnp.float32)
    for copy in copies[4:]:
        copy.wait()


def spread(upper_block, ref, *where):
    blocks = [jnp.broadcast_to(ref[(*index, pl.ds(r, 1), slice(None))], (8, LANES)) for index, r in where]
    return jnp.where(upper_block, blocks[1], blocks[0])


def face_row(rows, levels, b):
    return rows - -(-2 * levels // 8) * 8 + b * levels


def turn_kernel(switches, turn):
    tracers, columns = switches.shape[:2]
    levels = switches.shape[2] // 4
    row = lax.broadcasted_iota(jnp.int32, (8, LANES), 0)
    moment = row % MOMENTS
    for t in range(tracers):
        for c in range(columns):
            for l in range(levels):
                for d in range(2):
                    base = l * 4 + d
                    sw = spread(row >= MOMENTS, switches, ((t, c), base), ((t, c), base + 2))
                    take = jnp.where(sw == 1, 1.0, jnp.where(sw == 2, -1.0, 0.0))
                    keep = jnp.where(sw == 0, 1.0, 0.0)
                    turn[d, t, c, l] = jnp.where(moment == 0, take, jnp.where(moment == 1 + d, keep, 1.0))


def pre_kernel(own, first, second, third, flags, order, begun, before, also, rates, factors, message, fields):
    columns, levels = rates.shape[1], rates.shape[2]
    half = LANES // 2
    odd = order[0] % 2 == 1
    high = order[0] >= 2
    lane = lax.broadcasted_iota(jnp.int32, (8, LANES), 1)
    row = lax.broadcasted_iota(jnp.int32, (8, LANES), 0)
    upper_block = row >= MOMENTS
    lane_low = lax.broadcasted_iota(jnp.int32, (levels, LANES), 1) < half

    def sorted_shards(start, count):
        a, b, c, d = (ref[start : start + count] for ref in (own, first, second, third))
        a, b, c, d = (jnp.where(odd, b, a), jnp.where(odd, a, b), jnp.where(odd, d, c), jnp.where(odd, c, d))
        return (jnp.where(high, c, a), jnp.where(high, d, b), jnp.where(high, a, c), jnp.where(high, b, d))

    for pair in range(2):
        for c in range(columns):
            shards = sorted_shards((pair * columns + c) * levels, levels)
            for b in range(2):
                lo, hi = shards[2 * b], shards[2 * b + 1]
                fields[2 * pair, c, b] = jnp.where(lane_low, lo, pltpu.roll(hi, half, 1))
                flux = jnp.where(lane_low, pltpu.roll(lo, half, 1), hi)
                fields[2 * pair + 1, c, b] = flux
                if pair == 0 and c == 0:
                    eastward = flags[0, pl.ds(2 * b, levels, stride=4), :].astype(jnp.float32)
                    start = face_row(message.shape[0], levels, b)
                    message[start : start + levels] = (2.0 * eastward - 1.0) * flux

    def field(f, c, l):
        return spread(upper_block, fields, ((f, c, 0), l), ((f, c, 1), l))

    def flag(c, l, d):
        base = l * 4 + d
        return spread(upper_block, flags, ((c,), base), ((c,), base + 2)).astype(jnp.float32)

    first_row = (lane == 0) & (row < MOMENTS)
    last_row = (lane == LANES - 1) & (row >= MOMENTS)
    for l in range(levels):
        flux_x = [field(1, c, l) for c in range(columns)]
        flag_x = [flag(c, l, 0) for c in range(columns)]
        east = [flag_x[c] * flux_x[c] for c in range(columns)]
        west = [flux_x[c] - east[c] for c in range(columns)]
        east.append(1.0)
        for c in range(columns):
            share = 1.0 / field(0, c, l)
            rates[0, c, l] = east[c + 1] * share
            rates[1, c, l] = west[c] * share
            flux_y = field(2, c, l)
            north = flag(c, l, 1) * flux_y
            south = pltpu.roll(flux_y - north, 1, 1)
            south = jnp.where(lane == 0, pltpu.roll(south, 4, 0), south)
            rates[2, c, l] = jnp.where(last_row, 0.0, north) * share
            rates[3, c, l] = jnp.where(first_row, 0.0, south) * share

    fixed = row % MOMENTS == 3
    zero = jnp.zeros((8, LANES), jnp.float32)
    below, upper = [None] * columns, [None] * columns
    for l in range(levels):
        for c in range(columns):
            diagonal = zero + 1.0
            if l > 0:
                diagonal = diagonal + below[c]
            if l < levels - 1:
                above = field(3, c, l)
                diagonal = diagonal + above
            if l > 0:
                diagonal = diagonal + below[c] * upper[c]
            inverse = 1.0 / diagonal
            factors[0, c, l] = jnp.where(fixed, 1.0, inverse)
            factors[2, c, l] = jnp.where(fixed, 0.0, below[c] * inverse) if l > 0 else zero
            if l < levels - 1:
                upper[c] = -above * inverse
                factors[1, c, l] = jnp.where(fixed, 0.0, upper[c])
                below[c] = above
            else:
                factors[1, c, l] = zero


def advect(own, east_side, west_side, east, west, turns, slope, masks):
    is_mass, is_slope = masks
    stay = 1.0 - (east + west)
    east_part = east * jnp.where(is_slope, east, 1.0)
    west_part = west * jnp.where(is_slope, west, 1.0)
    east_cross = east * (1.0 - east)
    west_cross = west * (1.0 - west)
    out = []
    for s, e, w, z in zip(own, east_side, west_side, turns):
        total = stay * s + east_part * e + west_part * w
        cross = east_cross * (e - s) - west_cross * (w - s)
        total = total + jnp.where(is_slope, pltpu.roll(cross, slope, 0), 0.0)
        slope_up = pltpu.roll(total, 8 - slope, 0)
        out.append(z * jnp.where(is_mass, slope_up, total) + jnp.where(is_mass, total, 0.0))
    return out


def middle(todo, own, east_side, west_side, east_rate, rates, factors, turn, out):
    tracers, levels = out.shape[0], out.shape[1]
    lane = lax.broadcasted_iota(jnp.int32, (8, LANES), 1)
    at_first, at_last = lane == 0, lane == LANES - 1
    x_masks, y_masks = tile_masks(1), tile_masks(2)
    every = range(tracers)
    c = todo

    def prev(v):
        r = pltpu.roll(v, 1, 1)
        return jnp.where(at_first, pltpu.roll(r, 4, 0), r)

    def following(v):
        r = pltpu.roll(v, LANES - 1, 1)
        return jnp.where(at_last, pltpu.roll(r, 4, 0), r)

    def y_step(values, l):
        return advect(values, [following(v) for v in values], [prev(v) for v in values],
                      rates[2, c, l], rates[3, c, l], [turn[1, t, c, l] for t in every], 2, y_masks)

    carried = [None] * tracers
    for l in range(levels):
        sides = [[side(t, l) for t in every] for side in (own, east_side, west_side)]
        values = advect(*sides, east_rate(l), rates[1, c, l], [turn[0, t, c, l] for t in every], 1, x_masks)
        values = y_step(values, l)
        for t in every:
            v = values[t] * factors[0, c, l]
            if l > 0:
                v = v + factors[2, c, l] * carried[t]
            carried[t] = v
            out[t, l] = v
    for l in range(levels - 1, -1, -1):
        if l < levels - 1:
            for t in every:
                carried[t] = out[t, l] - factors[1, c, l] * carried[t]
        values = y_step(carried, l)
        for t in every:
            out[t, l] = values[t]


def tiles(ref, message=None):
    if message is None:
        return lambda t, l: ref[t, l]
    levels = ref.shape[1]
    start = lambda t, l: ((t - 1) * levels + l) * 8
    return lambda t, l: message[start(t, l) : start(t, l) + 8] if t else ref[0, l]


def west_kernel(col0, message, col1, west_halo, rates, factors, turn, out):
    middle(0, tiles(col0, message), tiles(col1), tiles(west_halo), lambda l: rates[0, 0, l], rates, factors, turn, out)


def inner_kernel(col0, message, col1, col2, rates, factors, turn, out):
    middle(1, tiles(col1), tiles(col2), tiles(col0, message), lambda l: rates[0, 1, l], rates, factors, turn, out)


def east_kernel(col1, col2, halo0, halo, rates, factors, turn, before, out, east):
    levels = out.shape[1]
    upper_block = lax.broadcasted_iota(jnp.int32, (8, LANES), 0) >= MOMENTS
    rows = [face_row(halo.shape[0], levels, b) for b in range(2)]

    def east_rate(l):
        flux = spread(upper_block, halo, ((), rows[0] + l), ((), rows[1] + l))
        east[l] = jnp.maximum(flux, 0.0) * rates[0, 2, l]
        return east[l]

    middle(2, tiles(col2), tiles(halo0, halo), tiles(col1), east_rate, rates, factors, turn, out)


def finish(c, own, east_side, west_side, east_rate, rates, turn, out, buf, sems):
    tracers, levels = buf.shape[0], buf.shape[1]
    masks = tile_masks(1)
    every = range(tracers)
    copies = []
    for part in range(2):
        low, high = part * levels // 2, (part + 1) * levels // 2
        for l in range(low, high):
            values = advect(*([side[t, l] for t in every] for side in (own, east_side, west_side)),
                            east_rate(l), rates[1, c, l], [turn[0, t, c, l] for t in every], 1, masks)
            for t in every:
                buf[t, l] = values[t]
        for t in every:
            span = pl.ds(low, high - low)
            copies.append(pltpu.make_async_copy(buf.at[t, span], out.at[t, c, span], sems.at[part, t]))
            copies[-1].start()
    for copy in copies:
        copy.wait()


def last_inner_kernel(mid0, mid1, mid2, rates, turn, out, buf, sems):
    finish(1, mid1, mid2, mid0, lambda l: rates[0, 1, l], rates, turn, out, buf, sems)


def last_east_kernel(begun, mid1, mid2, halo, east, rates, turn, out, buf, sems):
    finish(2, mid2, halo, mid1, lambda l: east[l], rates, turn, out, buf, sems)


def last_west_kernel(begun, mid0, mid1, halo, rates, turn, out, buf, sems):
    finish(0, mid0, mid1, halo, lambda l: rates[0, 0, l], rates, turn, out, buf, sems)


def body(state_adjoint, switches, flags, air_mass, x_flux, y_flux, vertical_mixing):
    state = state_view(state_adjoint)
    switch = pair_view(switches)
    flag = pair_view(flags[None])[0]
    tracers, columns, levels = state.shape[:3]
    order = lax.axis_index("trc").astype(jnp.int32).reshape(1)
    column = f32(tracers, levels, 8, LANES)
    rows = -(-2 * columns * levels // 8) * 8
    length = (tracers - 1) * levels + -(-2 * levels // 8)
    dma = pltpu.SemaphoreType.DMA
    fields = tuple(stay(x) for x in (air_mass, x_flux, y_flux, vertical_mixing))

    col0, message, col1, col2, packed, flag = call(
        head_kernel,
        (f32(1, levels, 8, LANES), f32(length, 8, LANES), column, column, f32(rows, LANES), jax.ShapeDtypeStruct(flag.shape, flag.dtype)),
        (HBM,) * 6, [pltpu.VMEM(x.shape, x.dtype) for x in fields] + [dma((5,)), dma((columns, tracers))],
        10**5, 10**6, stay(state), stay(flag), *fields)
    west_halo = shifted(col2, "lon", 1)
    east_halo = shifted(col0, "lon", -1)
    across = swapped(packed, "trc", 2)
    others = [swapped(packed, "trc", 1), across, swapped(across, "trc", 1)]
    turn = call(turn_kernel, f32(2, tracers, columns, levels, 8, LANES), (VMEM,), (), 10**6, 10**6, switch)
    rates, factors, message = call(
        pre_kernel,
        (f32(4, columns, levels, 8, LANES), f32(3, columns, levels, 8, LANES), f32(length * 8, LANES)),
        (VMEM,) * 5 + (SMEM, VMEM, VMEM, VMEM), [pltpu.VMEM((4, columns, 2, levels, LANES), jnp.float32)],
        10**6, 10**6, packed, *others, flag, order, message.reshape(length * 8, LANES), east_halo, turn, aliases={6: 2})
    east_message = shifted(message, "lon", -1)
    mid0 = call(west_kernel, column, (VMEM,) * 7, (), 10**6, 10**6, col0, message, col1, west_halo, rates, factors, turn)
    east_mid = shifted(mid0, "lon", -1)
    mid1 = call(inner_kernel, column, (VMEM,) * 7, (), 10**6, 10**6, col0, message, col1, col2, rates, factors, turn)
    mid2, east = call(east_kernel, (column, f32(levels, 8, LANES)), (VMEM,) * 8, (), 10**6, 10**6,
                      col1, col2, east_halo, east_message, rates, factors, turn, mid0)
    west_mid = shifted(mid2, "lon", 1)

    def last(kernel, aliases, *args):
        first = (HBM,) * len(aliases)
        return call(kernel, f32(*state.shape), first + (VMEM,) * (len(args) - len(first)),
                    [pltpu.VMEM(column.shape, jnp.float32), dma((2, tracers))], 10**6, 10**6,
                    *args, out_specs=HBM, aliases=aliases)

    out = last(last_inner_kernel, {}, mid0, mid1, mid2, rates, turn)
    out = last(last_east_kernel, {0: 0}, out, mid1, mid2, east_mid, east, rates, turn)
    out = last(last_west_kernel, {0: 0}, out, mid0, mid1, west_mid, rates, turn)
    return state_back(out)


def solution(mesh):
    placed = (
        P("trc", None, "lon", None, None),
        P("trc", None, "lon", None, None),
        P(None, "lon", None, None),
        P("lon", None, "trc"),
        P("lon", None, "trc"),
        P("lon", None, "trc"),
        P("lon", None, "trc"),
    )
    return jax.shard_map(
        body,
        mesh=mesh,
        in_specs=placed,
        out_specs=P("trc", None, "lon", None, None),
        check_vma=False,
    )
```

```python
import jax
import jax.numpy as jnp
from jax import lax
from jax.experimental import pallas as pl
from jax.experimental.pallas import tpu as pltpu
from jax.sharding import PartitionSpec as P

LANES = 128
MOMENTS = 4
PARTS = 4
VMEM = pl.BlockSpec(memory_space=pltpu.VMEM)
SMEM = pl.BlockSpec(memory_space=pltpu.SMEM)
HBM = pl.BlockSpec(memory_space=pltpu.HBM)


def state_view(x):
    t, m, c, l, n = x.shape
    b = n // LANES
    x = x.reshape(t, m, c, l, b, LANES).transpose(0, 2, 3, 4, 1, 5)
    return x.reshape(t, c, l, b * m, LANES)


def pair_view(x):
    t, d, c, l, n = x.shape
    b = n // LANES
    x = x.reshape(t, d, c, l, b, LANES).transpose(0, 2, 3, 4, 1, 5)
    return x.reshape(t, c, l * b * d, LANES)


def state_back(y):
    t, c, l, rows, _ = y.shape
    b = rows // MOMENTS
    y = y.reshape(t, c, l, b, MOMENTS, LANES).transpose(0, 4, 1, 2, 3, 5)
    return y.reshape(t, MOMENTS, c, l, b * LANES)


def shifted(value, axis, by):
    count = lax.axis_size(axis)
    return lax.ppermute(value, axis, [(i, (i + by) % count) for i in range(count)])


def swapped(value, axis, mask):
    count = lax.axis_size(axis)
    return lax.ppermute(value, axis, [(i, i ^ mask) for i in range(count)])


def call(kernel, out, in_specs, scratch, flops, moved, *args, out_specs=None, aliases=None):
    return pl.pallas_call(
        kernel,
        out_shape=out,
        in_specs=in_specs,
        out_specs=jax.tree.map(lambda _: VMEM, out) if out_specs is None else out_specs,
        scratch_shapes=scratch,
        input_output_aliases=aliases or {},
        compiler_params=pltpu.CompilerParams(vmem_limit_bytes=24 * 1024 * 1024),
        cost_estimate=pl.CostEstimate(flops=flops, bytes_accessed=moved, transcendentals=0),
    )(*args)


def stay(x):
    return pltpu.with_memory_space_constraint(x, pltpu.HBM)


def f32(*shape):
    return jax.ShapeDtypeStruct(shape, jnp.float32)


def tile_masks(slope):
    row = lax.broadcasted_iota(jnp.int32, (8, LANES), 0) % MOMENTS
    return row == 0, row == slope


def head_kernel(state, flags, mass, xf, yf, km, message, col1, col2, packed, flags_v, mass_v, xf_v, yf_v, km_v, sems, column_sems):
    tracers, columns, levels = state.shape[0], mass.shape[0], mass.shape[1]
    half = LANES // 2
    pairs = ((mass, mass_v), (xf, xf_v), (yf, yf_v), (km, km_v), (flags, flags_v))
    copies = [pltpu.make_async_copy(src, dst, sems.at[i]) for i, (src, dst) in enumerate(pairs)]
    for t in range(tracers):
        for c, place in ((2, col2.at[t]), (0, message.at[pl.ds(t * levels, levels)]), (1, col1.at[t])):
            copies.append(pltpu.make_async_copy(state.at[t, c], place, column_sems.at[c, t]))
    for copy in copies:
        copy.start()
    for copy in copies[:4]:
        copy.wait()
    for c in range(columns):
        low, top = c * levels, (columns + c) * levels
        packed[low : low + levels, :half] = mass_v[c]
        packed[low : low + levels, half:] = xf_v[c]
        packed[top : top + levels, :half] = yf_v[c]
        packed[top : top + levels - 1, half:] = km_v[c]
        packed[top + levels - 1 : top + levels, half:] = jnp.zeros((1, half), jnp.float32)
    for copy in copies[4:]:
        copy.wait()


def spread(upper_block, ref, *where):
    blocks = [jnp.broadcast_to(ref[(*index, pl.ds(r, 1), slice(None))], (8, LANES)) for index, r in where]
    return jnp.where(upper_block, blocks[1], blocks[0])


def face_row(rows, levels, b):
    return rows - -(-2 * levels // 8) * 8 + b * levels


def turn_kernel(switches, turn):
    tracers, columns = switches.shape[:2]
    levels = switches.shape[2] // 4
    row = lax.broadcasted_iota(jnp.int32, (8, LANES), 0)
    moment = row % MOMENTS
    for t in range(tracers):
        for c in range(columns):
            for l in range(levels):
                for d in range(2):
                    base = l * 4 + d
                    sw = spread(row >= MOMENTS, switches, ((t, c), base), ((t, c), base + 2))
                    take = jnp.where(sw == 1, 1.0, jnp.where(sw == 2, -1.0, 0.0))
                    keep = jnp.where(sw == 0, 1.0, 0.0)
                    turn[d, t, c, l] = jnp.where(moment == 0, take, jnp.where(moment == 1 + d, keep, 1.0))


def sorted_shards(refs, order, start, count):
    odd, high = order[0] % 2 == 1, order[0] >= 2
    a, b, c, d = (ref[start : start + count] for ref in refs)
    a, b, c, d = (jnp.where(odd, b, a), jnp.where(odd, a, b), jnp.where(odd, d, c), jnp.where(odd, c, d))
    return (jnp.where(high, c, a), jnp.where(high, d, b), jnp.where(high, a, c), jnp.where(high, b, d))


def gate_kernel(message, before, out):
    pass


def pre_kernel(own, first, second, third, flags, order, begun, also, rates, factors, message, fields):
    columns, levels = rates.shape[1], rates.shape[2]
    half = LANES // 2
    lane = lax.broadcasted_iota(jnp.int32, (8, LANES), 1)
    row = lax.broadcasted_iota(jnp.int32, (8, LANES), 0)
    upper_block = row >= MOMENTS
    lane_low = lax.broadcasted_iota(jnp.int32, (levels, LANES), 1) < half
    for pair in range(2):
        for c in range(columns):
            shards = sorted_shards((own, first, second, third), order, (pair * columns + c) * levels, levels)
            for b in range(2):
                lo, hi = shards[2 * b], shards[2 * b + 1]
                fields[2 * pair, c, b] = jnp.where(lane_low, lo, pltpu.roll(hi, half, 1))
                flux = jnp.where(lane_low, pltpu.roll(lo, half, 1), hi)
                fields[2 * pair + 1, c, b] = flux
                if pair == 0 and c == 0:
                    eastward = flags[0, pl.ds(2 * b, levels, stride=4), :].astype(jnp.float32)
                    start = face_row(message.shape[0], levels, b)
                    message[start : start + levels] = (2.0 * eastward - 1.0) * flux

    def field(f, c, l):
        return spread(upper_block, fields, ((f, c, 0), l), ((f, c, 1), l))

    def flag(c, l, d):
        base = l * 4 + d
        return spread(upper_block, flags, ((c,), base), ((c,), base + 2)).astype(jnp.float32)

    first_row = (lane == 0) & (row < MOMENTS)
    last_row = (lane == LANES - 1) & (row >= MOMENTS)
    for l in range(levels):
        flux_x = [field(1, c, l) for c in range(columns)]
        flag_x = [flag(c, l, 0) for c in range(columns)]
        east = [flag_x[c] * flux_x[c] for c in range(columns)]
        west = [flux_x[c] - east[c] for c in range(columns)]
        east.append(1.0)
        for c in range(columns):
            share = 1.0 / field(0, c, l)
            rates[0, c, l] = east[c + 1] * share
            rates[1, c, l] = west[c] * share
            flux_y = field(2, c, l)
            north = flag(c, l, 1) * flux_y
            south = pltpu.roll(flux_y - north, 1, 1)
            south = jnp.where(lane == 0, pltpu.roll(south, 4, 0), south)
            rates[2, c, l] = jnp.where(last_row, 0.0, north) * share
            rates[3, c, l] = jnp.where(first_row, 0.0, south) * share

    fixed = row % MOMENTS == 3
    zero = jnp.zeros((8, LANES), jnp.float32)
    below, upper = [None] * columns, [None] * columns
    for l in range(levels):
        for c in range(columns):
            diagonal = zero + 1.0
            if l > 0:
                diagonal = diagonal + below[c]
            if l < levels - 1:
                above = field(3, c, l)
                diagonal = diagonal + above
            if l > 0:
                diagonal = diagonal + below[c] * upper[c]
            inverse = 1.0 / diagonal
            factors[0, c, l] = jnp.where(fixed, 1.0, inverse)
            factors[2, c, l] = jnp.where(fixed, 0.0, below[c] * inverse) if l > 0 else zero
            if l < levels - 1:
                upper[c] = -above * inverse
                factors[1, c, l] = jnp.where(fixed, 0.0, upper[c])
                below[c] = above
            else:
                factors[1, c, l] = zero


def advect(own, east_side, west_side, east, west, turns, slope, masks):
    is_mass, is_slope = masks
    stay = 1.0 - (east + west)
    east_part = east * jnp.where(is_slope, east, 1.0)
    west_part = west * jnp.where(is_slope, west, 1.0)
    east_cross = east * (1.0 - east)
    west_cross = west * (1.0 - west)
    out = []
    for s, e, w, z in zip(own, east_side, west_side, turns):
        total = stay * s + east_part * e + west_part * w
        cross = east_cross * (e - s) - west_cross * (w - s)
        total = total + jnp.where(is_slope, pltpu.roll(cross, slope, 0), 0.0)
        slope_up = pltpu.roll(total, 8 - slope, 0)
        out.append(z * jnp.where(is_mass, slope_up, total) + jnp.where(is_mass, total, 0.0))
    return out


def middle(todo, own, east_side, west_side, east_rate, rates, factors, turn, out):
    tracers, levels = out.shape[0], out.shape[1]
    lane = lax.broadcasted_iota(jnp.int32, (8, LANES), 1)
    at_first, at_last = lane == 0, lane == LANES - 1
    x_masks, y_masks = tile_masks(1), tile_masks(2)
    every = range(tracers)
    c = todo

    def prev(v):
        r = pltpu.roll(v, 1, 1)
        return jnp.where(at_first, pltpu.roll(r, 4, 0), r)

    def following(v):
        r = pltpu.roll(v, LANES - 1, 1)
        return jnp.where(at_last, pltpu.roll(r, 4, 0), r)

    def y_step(values, l):
        return advect(values, [following(v) for v in values], [prev(v) for v in values],
                      rates[2, c, l], rates[3, c, l], [turn[1, t, c, l] for t in every], 2, y_masks)

    carried = [None] * tracers
    for l in range(levels):
        sides = [[side(t, l) for t in every] for side in (own, east_side, west_side)]
        values = advect(*sides, east_rate(l), rates[1, c, l], [turn[0, t, c, l] for t in every], 1, x_masks)
        values = y_step(values, l)
        for t in every:
            v = values[t] * factors[0, c, l]
            if l > 0:
                v = v + factors[2, c, l] * carried[t]
            carried[t] = v
            out[t, l] = v
    for l in range(levels - 1, -1, -1):
        if l < levels - 1:
            for t in every:
                carried[t] = out[t, l] - factors[1, c, l] * carried[t]
        values = y_step(carried, l)
        for t in every:
            out[t, l] = values[t]


def tiles(ref, levels):
    if len(ref.shape) == 4:
        return lambda t, l: ref[t, l]
    return lambda t, l: ref[(t * levels + l) * 8 : (t * levels + l + 1) * 8]


def west_kernel(message, col1, west_halo, rates, factors, turn, out):
    levels = out.shape[1]
    middle(0, tiles(message, levels), tiles(col1, levels), tiles(west_halo, levels),
           lambda l: rates[0, 0, l], rates, factors, turn, out)


def inner_kernel(message, col1, col2, rates, factors, turn, out):
    levels = out.shape[1]
    middle(1, tiles(col1, levels), tiles(col2, levels), tiles(message, levels),
           lambda l: rates[0, 1, l], rates, factors, turn, out)


def east_kernel(col1, col2, halo, rates, factors, turn, before, out, east):
    levels = out.shape[1]
    upper_block = lax.broadcasted_iota(jnp.int32, (8, LANES), 0) >= MOMENTS
    rows = [face_row(halo.shape[0], levels, b) for b in range(2)]

    def east_rate(l):
        flux = spread(upper_block, halo, ((), rows[0] + l), ((), rows[1] + l))
        east[l] = jnp.maximum(flux, 0.0) * rates[0, 2, l]
        return east[l]

    middle(2, tiles(col2, levels), tiles(halo, levels), tiles(col1, levels), east_rate, rates, factors, turn, out)


def finish(c, own, east_side, west_side, east_rate, rates, turn, out, buf, sems):
    tracers, levels = buf.shape[0], buf.shape[1]
    masks = tile_masks(1)
    every = range(tracers)
    copies = []
    for part in range(PARTS):
        low, high = part * levels // PARTS, (part + 1) * levels // PARTS
        for l in range(low, high):
            values = advect(*([side[t, l] for t in every] for side in (own, east_side, west_side)),
                            east_rate(l), rates[1, c, l], [turn[0, t, c, l] for t in every], 1, masks)
            for t in every:
                buf[t, l] = values[t]
        for t in every:
            span = pl.ds(low, high - low)
            copies.append(pltpu.make_async_copy(buf.at[t, span], out.at[t, c, span], sems.at[part, t]))
            copies[-1].start()
    for copy in copies:
        copy.wait()


def last_inner_kernel(mid0, mid1, mid2, rates, turn, out, buf, sems):
    finish(1, mid1, mid2, mid0, lambda l: rates[0, 1, l], rates, turn, out, buf, sems)


def last_east_kernel(begun, mid1, mid2, halo, east, rates, turn, out, buf, sems):
    finish(2, mid2, halo, mid1, lambda l: east[l], rates, turn, out, buf, sems)


def last_west_kernel(begun, mid0, mid1, halo, rates, turn, out, buf, sems):
    finish(0, mid0, mid1, halo, lambda l: rates[0, 0, l], rates, turn, out, buf, sems)


def body(state_adjoint, switches, flags, air_mass, x_flux, y_flux, vertical_mixing):
    state = state_view(state_adjoint)
    switch = pair_view(switches)
    flag = pair_view(flags[None])[0]
    tracers, columns, levels = state.shape[:3]
    order = lax.axis_index("trc").astype(jnp.int32).reshape(1)
    column = f32(tracers, levels, 8, LANES)
    rows = -(-2 * columns * levels // 8) * 8
    length = tracers * levels + -(-2 * levels // 8)
    dma = pltpu.SemaphoreType.DMA
    fields = tuple(stay(x) for x in (air_mass, x_flux, y_flux, vertical_mixing))

    message, col1, col2, packed, flag = call(
        head_kernel,
        (f32(length, 8, LANES), column, column, f32(rows, LANES), jax.ShapeDtypeStruct(flag.shape, flag.dtype)),
        (HBM,) * 6, [pltpu.VMEM(x.shape, x.dtype) for x in fields] + [dma((5,)), dma((columns, tracers))],
        10**5, 10**6, stay(state), stay(flag), *fields)
    west_halo = shifted(col2, "lon", 1)
    across = swapped(packed, "trc", 2)
    others = [swapped(packed, "trc", 1), across, swapped(across, "trc", 1)]
    turn = call(turn_kernel, f32(2, tracers, columns, levels, 8, LANES), (VMEM,), (), 10**6, 10**6, switch)
    rates, factors, message = call(
        pre_kernel,
        (f32(4, columns, levels, 8, LANES), f32(3, columns, levels, 8, LANES), f32(length * 8, LANES)),
        (VMEM,) * 5 + (SMEM,) + (VMEM,) * 2, [pltpu.VMEM((4, columns, 2, levels, LANES), jnp.float32)], 1, 1,
        packed, *others, flag, order, message.reshape(length * 8, LANES), turn, aliases={6: 2})
    message = call(gate_kernel, f32(length * 8, LANES), (VMEM,) * 2, (), 1, 1, message, west_halo, aliases={0: 0})
    east_message = shifted(message, "lon", -1)
    mid0 = call(west_kernel, column, (VMEM,) * 6, (), 10**6, 10**6, message, col1, west_halo, rates, factors, turn)
    east_halo = shifted(mid0, "lon", -1)
    mid1 = call(inner_kernel, column, (VMEM,) * 6, (), 10**6, 10**6, message, col1, col2, rates, factors, turn)
    mid2, east = call(east_kernel, (column, f32(levels, 8, LANES)), (VMEM,) * 7, (), 10**6, 10**6,
                      col1, col2, east_message, rates, factors, turn, mid0)
    west_halo = shifted(mid2, "lon", 1)

    def last(kernel, aliases, *args):
        first = (HBM,) * len(aliases)
        return call(kernel, f32(*state.shape), first + (VMEM,) * (len(args) - len(first)),
                    [pltpu.VMEM(column.shape, jnp.float32), dma((PARTS, tracers))], 10**6, 10**6,
                    *args, out_specs=HBM, aliases=aliases)

    out = last(last_inner_kernel, {}, mid0, mid1, mid2, rates, turn)
    out = last(last_east_kernel, {0: 0}, out, mid1, mid2, east_halo, east, rates, turn)
    out = last(last_west_kernel, {0: 0}, out, mid0, mid1, west_halo, rates, turn)
    return state_back(out)


def solution(mesh):
    placed = (
        P("trc", None, "lon", None, None),
        P("trc", None, "lon", None, None),
        P(None, "lon", None, None),
        P("lon", None, "trc"),
        P("lon", None, "trc"),
        P("lon", None, "trc"),
        P("lon", None, "trc"),
    )
    return jax.shard_map(
        body,
        mesh=mesh,
        in_specs=placed,
        out_specs=P("trc", None, "lon", None, None),
        check_vma=False,
    )
```

```python
import jax
import jax.numpy as jnp
from jax import lax
from jax.experimental import pallas as pl
from jax.experimental.pallas import tpu as pltpu
from jax.sharding import PartitionSpec as P

LANES = 128
MOMENTS = 4
VMEM = pl.BlockSpec(memory_space=pltpu.VMEM)
SMEM = pl.BlockSpec(memory_space=pltpu.SMEM)
HBM = pl.BlockSpec(memory_space=pltpu.HBM)


def state_view(x):
    t, m, c, l, n = x.shape
    b = n // LANES
    x = x.reshape(t, m, c, l, b, LANES).transpose(0, 2, 3, 4, 1, 5)
    return x.reshape(t, c, l, b * m, LANES)


def pair_view(x):
    t, d, c, l, n = x.shape
    b = n // LANES
    x = x.reshape(t, d, c, l, b, LANES).transpose(0, 2, 3, 4, 1, 5)
    return x.reshape(t, c, l * b * d, LANES)


def state_back(y):
    t, c, l, rows, _ = y.shape
    b = rows // MOMENTS
    y = y.reshape(t, c, l, b, MOMENTS, LANES).transpose(0, 4, 1, 2, 3, 5)
    return y.reshape(t, MOMENTS, c, l, b * LANES)


def shifted(value, axis, by):
    count = lax.axis_size(axis)
    return lax.ppermute(value, axis, [(i, (i + by) % count) for i in range(count)])


def swapped(value, axis, mask):
    count = lax.axis_size(axis)
    return lax.ppermute(value, axis, [(i, i ^ mask) for i in range(count)])


def call(kernel, out, in_specs, scratch, flops, moved, *args, out_specs=None, aliases=None):
    return pl.pallas_call(
        kernel,
        out_shape=out,
        in_specs=in_specs,
        out_specs=jax.tree.map(lambda _: VMEM, out) if out_specs is None else out_specs,
        scratch_shapes=scratch,
        input_output_aliases=aliases or {},
        compiler_params=pltpu.CompilerParams(vmem_limit_bytes=24 * 1024 * 1024),
        cost_estimate=pl.CostEstimate(flops=flops, bytes_accessed=moved, transcendentals=0),
    )(*args)


def stay(x):
    return pltpu.with_memory_space_constraint(x, pltpu.HBM)


def f32(*shape):
    return jax.ShapeDtypeStruct(shape, jnp.float32)


def tile_masks(slope):
    row = lax.broadcasted_iota(jnp.int32, (8, LANES), 0) % MOMENTS
    return row == 0, row == slope


def head_kernel(state, flags, mass, xf, yf, km, col0, col1, col2, packed, flags_v, mass_v, xf_v, yf_v, km_v, sems, column_sems):
    tracers, columns, levels = state.shape[0], mass.shape[0], mass.shape[1]
    half = LANES // 2
    pairs = ((mass, mass_v), (xf, xf_v), (yf, yf_v), (km, km_v), (flags, flags_v))
    copies = [pltpu.make_async_copy(src, dst, sems.at[i]) for i, (src, dst) in enumerate(pairs)]
    for t in range(tracers):
        for c, place in ((2, col2.at[t]), (0, col0.at[t]), (1, col1.at[t])):
            copies.append(pltpu.make_async_copy(state.at[t, c], place, column_sems.at[c, t]))
    for copy in copies:
        copy.start()
    for copy in copies[:4]:
        copy.wait()
    for c in range(columns):
        low, top = c * levels, (columns + c) * levels
        packed[low : low + levels, :half] = mass_v[c]
        packed[low : low + levels, half:] = xf_v[c]
        packed[top : top + levels, :half] = yf_v[c]
        packed[top : top + levels - 1, half:] = km_v[c]
        packed[top + levels - 1 : top + levels, half:] = jnp.zeros((1, half), jnp.float32)
    for copy in copies[4:]:
        copy.wait()


def gate_kernel(message, before, out):
    pass


def spread(upper_block, ref, *where):
    blocks = [jnp.broadcast_to(ref[(*index, pl.ds(r, 1), slice(None))], (8, LANES)) for index, r in where]
    return jnp.where(upper_block, blocks[1], blocks[0])


def turn_kernel(switches, turn):
    tracers, columns = switches.shape[:2]
    levels = switches.shape[2] // 4
    row = lax.broadcasted_iota(jnp.int32, (8, LANES), 0)
    moment = row % MOMENTS
    for t in range(tracers):
        for c in range(columns):
            for l in range(levels):
                for d in range(2):
                    base = l * 4 + d
                    sw = spread(row >= MOMENTS, switches, ((t, c), base), ((t, c), base + 2))
                    take = jnp.where(sw == 1, 1.0, jnp.where(sw == 2, -1.0, 0.0))
                    keep = jnp.where(sw == 0, 1.0, 0.0)
                    turn[d, t, c, l] = jnp.where(moment == 0, take, jnp.where(moment == 1 + d, keep, 1.0))


def pre_kernel(own, first, second, third, flags, order, also, rates, factors, face, fields):
    columns, levels = rates.shape[1], rates.shape[2]
    half = LANES // 2
    odd = order[0] % 2 == 1
    high = order[0] >= 2
    lane = lax.broadcasted_iota(jnp.int32, (8, LANES), 1)
    row = lax.broadcasted_iota(jnp.int32, (8, LANES), 0)
    upper_block = row >= MOMENTS
    lane_low = lax.broadcasted_iota(jnp.int32, (levels, LANES), 1) < half

    def sorted_shards(start, count):
        a, b, c, d = (ref[start : start + count] for ref in (own, first, second, third))
        a, b, c, d = (jnp.where(odd, b, a), jnp.where(odd, a, b), jnp.where(odd, d, c), jnp.where(odd, c, d))
        return (jnp.where(high, c, a), jnp.where(high, d, b), jnp.where(high, a, c), jnp.where(high, b, d))

    for pair in range(2):
        for c in range(columns):
            shards = sorted_shards((pair * columns + c) * levels, levels)
            for b in range(2):
                lo, hi = shards[2 * b], shards[2 * b + 1]
                fields[2 * pair, c, b] = jnp.where(lane_low, lo, pltpu.roll(hi, half, 1))
                flux = jnp.where(lane_low, pltpu.roll(lo, half, 1), hi)
                fields[2 * pair + 1, c, b] = flux
                if pair == 0 and c == 0:
                    eastward = flags[0, pl.ds(2 * b, levels, stride=4), :].astype(jnp.float32)
                    face[b * levels : (b + 1) * levels] = (2.0 * eastward - 1.0) * flux

    def field(f, c, l):
        return spread(upper_block, fields, ((f, c, 0), l), ((f, c, 1), l))

    def flag(c, l, d):
        base = l * 4 + d
        return spread(upper_block, flags, ((c,), base), ((c,), base + 2)).astype(jnp.float32)

    first_row = (lane == 0) & (row < MOMENTS)
    last_row = (lane == LANES - 1) & (row >= MOMENTS)
    for l in range(levels):
        flux_x = [field(1, c, l) for c in range(columns)]
        flag_x = [flag(c, l, 0) for c in range(columns)]
        east = [flag_x[c] * flux_x[c] for c in range(columns)]
        west = [flux_x[c] - east[c] for c in range(columns)]
        east.append(1.0)
        for c in range(columns):
            share = 1.0 / field(0, c, l)
            rates[0, c, l] = east[c + 1] * share
            rates[1, c, l] = west[c] * share
            flux_y = field(2, c, l)
            north = flag(c, l, 1) * flux_y
            south = pltpu.roll(flux_y - north, 1, 1)
            south = jnp.where(lane == 0, pltpu.roll(south, 4, 0), south)
            rates[2, c, l] = jnp.where(last_row, 0.0, north) * share
            rates[3, c, l] = jnp.where(first_row, 0.0, south) * share

    fixed = row % MOMENTS == 3
    zero = jnp.zeros((8, LANES), jnp.float32)
    below, upper = [None] * columns, [None] * columns
    for l in range(levels):
        for c in range(columns):
            diagonal = zero + 1.0
            if l > 0:
                diagonal = diagonal + below[c]
            if l < levels - 1:
                above = field(3, c, l)
                diagonal = diagonal + above
            if l > 0:
                diagonal = diagonal + below[c] * upper[c]
            inverse = 1.0 / diagonal
            factors[0, c, l] = jnp.where(fixed, 1.0, inverse)
            factors[2, c, l] = jnp.where(fixed, 0.0, below[c] * inverse) if l > 0 else zero
            if l < levels - 1:
                upper[c] = -above * inverse
                factors[1, c, l] = jnp.where(fixed, 0.0, upper[c])
                below[c] = above
            else:
                factors[1, c, l] = zero


def advect(own, east_side, west_side, east, west, turns, slope, masks):
    is_mass, is_slope = masks
    stay = 1.0 - (east + west)
    east_part = east * jnp.where(is_slope, east, 1.0)
    west_part = west * jnp.where(is_slope, west, 1.0)
    east_cross = east * (1.0 - east)
    west_cross = west * (1.0 - west)
    out = []
    for s, e, w, z in zip(own, east_side, west_side, turns):
        total = stay * s + east_part * e + west_part * w
        cross = east_cross * (e - s) - west_cross * (w - s)
        total = total + jnp.where(is_slope, pltpu.roll(cross, slope, 0), 0.0)
        slope_up = pltpu.roll(total, 8 - slope, 0)
        out.append(z * jnp.where(is_mass, slope_up, total) + jnp.where(is_mass, total, 0.0))
    return out


def middle(todo, own, east_side, west_side, east_rate, rates, factors, turn, out):
    tracers, levels = out.shape[0], out.shape[1]
    lane = lax.broadcasted_iota(jnp.int32, (8, LANES), 1)
    at_first, at_last = lane == 0, lane == LANES - 1
    x_masks, y_masks = tile_masks(1), tile_masks(2)
    every = range(tracers)
    c = todo

    def prev(v):
        r = pltpu.roll(v, 1, 1)
        return jnp.where(at_first, pltpu.roll(r, 4, 0), r)

    def following(v):
        r = pltpu.roll(v, LANES - 1, 1)
        return jnp.where(at_last, pltpu.roll(r, 4, 0), r)

    def y_step(values, l):
        return advect(values, [following(v) for v in values], [prev(v) for v in values],
                      rates[2, c, l], rates[3, c, l], [turn[1, t, c, l] for t in every], 2, y_masks)

    carried = [None] * tracers
    for l in range(levels):
        sides = [[side(t, l) for t in every] for side in (own, east_side, west_side)]
        values = advect(*sides, east_rate(l), rates[1, c, l], [turn[0, t, c, l] for t in every], 1, x_masks)
        values = y_step(values, l)
        for t in every:
            v = values[t] * factors[0, c, l]
            if l > 0:
                v = v + factors[2, c, l] * carried[t]
            carried[t] = v
            out[t, l] = v
    for l in range(levels - 1, -1, -1):
        if l < levels - 1:
            for t in every:
                carried[t] = out[t, l] - factors[1, c, l] * carried[t]
        values = y_step(carried, l)
        for t in every:
            out[t, l] = values[t]


def tiles(ref):
    return lambda t, l: ref[t, l]


def west_kernel(col0, col1, west_halo, rates, factors, turn, out):
    middle(0, tiles(col0), tiles(col1), tiles(west_halo), lambda l: rates[0, 0, l], rates, factors, turn, out)


def inner_kernel(col0, col1, col2, rates, factors, turn, out):
    middle(1, tiles(col1), tiles(col2), tiles(col0), lambda l: rates[0, 1, l], rates, factors, turn, out)


def east_kernel(col1, col2, east_halo, face, rates, factors, turn, before, out, east):
    levels = out.shape[1]
    upper_block = lax.broadcasted_iota(jnp.int32, (8, LANES), 0) >= MOMENTS

    def east_rate(l):
        flux = spread(upper_block, face, ((), l), ((), levels + l))
        east[l] = jnp.maximum(flux, 0.0) * rates[0, 2, l]
        return east[l]

    middle(2, tiles(col2), tiles(east_halo), tiles(col1), east_rate, rates, factors, turn, out)


def finish(c, own, east_side, west_side, east_rate, rates, turn, out, buf, sems):
    tracers, levels = buf.shape[0], buf.shape[1]
    masks = tile_masks(1)
    every = range(tracers)
    copies = []
    for part in range(2):
        low, high = part * levels // 2, (part + 1) * levels // 2
        for l in range(low, high):
            values = advect(*([side[t, l] for t in every] for side in (own, east_side, west_side)),
                            east_rate(l), rates[1, c, l], [turn[0, t, c, l] for t in every], 1, masks)
            for t in every:
                buf[t, l] = values[t]
        for t in every:
            span = pl.ds(low, high - low)
            copies.append(pltpu.make_async_copy(buf.at[t, span], out.at[t, c, span], sems.at[part, t]))
            copies[-1].start()
    for copy in copies:
        copy.wait()


def last_inner_kernel(mid0, mid1, mid2, rates, turn, out, buf, sems):
    finish(1, mid1, mid2, mid0, lambda l: rates[0, 1, l], rates, turn, out, buf, sems)


def last_east_kernel(begun, mid1, mid2, halo, east, rates, turn, out, buf, sems):
    finish(2, mid2, halo, mid1, lambda l: east[l], rates, turn, out, buf, sems)


def last_west_kernel(begun, mid0, mid1, halo, rates, turn, out, buf, sems):
    finish(0, mid0, mid1, halo, lambda l: rates[0, 0, l], rates, turn, out, buf, sems)


def body(state_adjoint, switches, flags, air_mass, x_flux, y_flux, vertical_mixing):
    state = state_view(state_adjoint)
    switch = pair_view(switches)
    flag = pair_view(flags[None])[0]
    tracers, columns, levels = state.shape[:3]
    order = lax.axis_index("trc").astype(jnp.int32).reshape(1)
    column = f32(tracers, levels, 8, LANES)
    rows = -(-2 * columns * levels // 8) * 8
    dma = pltpu.SemaphoreType.DMA
    fields = tuple(stay(x) for x in (air_mass, x_flux, y_flux, vertical_mixing))

    col0, col1, col2, packed, flag = call(
        head_kernel,
        (column, column, column, f32(rows, LANES), jax.ShapeDtypeStruct(flag.shape, flag.dtype)),
        (HBM,) * 6, [pltpu.VMEM(x.shape, x.dtype) for x in fields] + [dma((5,)), dma((columns, tracers))],
        10**5, 10**6, stay(state), stay(flag), *fields)
    west_halo = shifted(col2, "lon", 1)
    across = swapped(packed, "trc", 2)
    col0 = call(gate_kernel, column, (VMEM,) * 2, (), 1, 1, col0, across, aliases={0: 0})
    east_halo = shifted(col0, "lon", -1)
    others = [swapped(packed, "trc", 1), across, swapped(across, "trc", 1)]
    turn = call(turn_kernel, f32(2, tracers, columns, levels, 8, LANES), (VMEM,), (), 10**6, 10**6, switch)
    rates, factors, face = call(
        pre_kernel,
        (f32(4, columns, levels, 8, LANES), f32(3, columns, levels, 8, LANES), f32(2 * levels, LANES)),
        (VMEM,) * 5 + (SMEM, VMEM), [pltpu.VMEM((4, columns, 2, levels, LANES), jnp.float32)],
        1, 1, packed, *others, flag, order, turn)
    face = call(gate_kernel, f32(2 * levels, LANES), (VMEM,) * 2, (), 1, 1, face, west_halo, aliases={0: 0})
    face = shifted(face, "lon", -1)
    mid0 = call(west_kernel, column, (VMEM,) * 6, (), 10**6, 10**6, col0, col1, west_halo, rates, factors, turn)
    east_mid = shifted(mid0, "lon", -1)
    mid1 = call(inner_kernel, column, (VMEM,) * 6, (), 10**6, 10**6, col0, col1, col2, rates, factors, turn)
    mid2, east = call(east_kernel, (column, f32(levels, 8, LANES)), (VMEM,) * 8, (), 10**6, 10**6,
                      col1, col2, east_halo, face, rates, factors, turn, mid0)
    west_mid = shifted(mid2, "lon", 1)

    def last(kernel, aliases, *args):
        first = (HBM,) * len(aliases)
        return call(kernel, f32(*state.shape), first + (VMEM,) * (len(args) - len(first)),
                    [pltpu.VMEM(column.shape, jnp.float32), dma((2, tracers))], 10**6, 10**6,
                    *args, out_specs=HBM, aliases=aliases)

    out = last(last_inner_kernel, {}, mid0, mid1, mid2, rates, turn)
    out = last(last_east_kernel, {0: 0}, out, mid1, mid2, east_mid, east, rates, turn)
    out = last(last_west_kernel, {0: 0}, out, mid0, mid1, west_mid, rates, turn)
    return state_back(out)


def solution(mesh):
    placed = (
        P("trc", None, "lon", None, None),
        P("trc", None, "lon", None, None),
        P(None, "lon", None, None),
        P("lon", None, "trc"),
        P("lon", None, "trc"),
        P("lon", None, "trc"),
        P("lon", None, "trc"),
    )
    return jax.shard_map(
        body,
        mesh=mesh,
        in_specs=placed,
        out_specs=P("trc", None, "lon", None, None),
        check_vma=False,
    )
```

```python
import jax
import jax.numpy as jnp
from jax import lax
from jax.experimental import pallas as pl
from jax.experimental.pallas import tpu as pltpu
from jax.sharding import PartitionSpec as P

LANES = 128
MOMENTS = 4
PARTS = 4
VMEM = pl.BlockSpec(memory_space=pltpu.VMEM)
SMEM = pl.BlockSpec(memory_space=pltpu.SMEM)
HBM = pl.BlockSpec(memory_space=pltpu.HBM)


def state_view(x):
    t, m, c, l, n = x.shape
    b = n // LANES
    x = x.reshape(t, m, c, l, b, LANES).transpose(0, 2, 3, 4, 1, 5)
    return x.reshape(t, c, l, b * m, LANES)


def pair_view(x):
    t, d, c, l, n = x.shape
    b = n // LANES
    x = x.reshape(t, d, c, l, b, LANES).transpose(0, 2, 3, 4, 1, 5)
    return x.reshape(t, c, l * b * d, LANES)


def state_back(y):
    t, c, l, rows, _ = y.shape
    b = rows // MOMENTS
    y = y.reshape(t, c, l, b, MOMENTS, LANES).transpose(0, 4, 1, 2, 3, 5)
    return y.reshape(t, MOMENTS, c, l, b * LANES)


def shifted(value, axis, by):
    count = lax.axis_size(axis)
    return lax.ppermute(value, axis, [(i, (i + by) % count) for i in range(count)])


def swapped(value, axis, mask):
    count = lax.axis_size(axis)
    return lax.ppermute(value, axis, [(i, i ^ mask) for i in range(count)])


def call(kernel, out, in_specs, scratch, flops, moved, *args, out_specs=None, aliases=None):
    return pl.pallas_call(
        kernel,
        out_shape=out,
        in_specs=in_specs,
        out_specs=jax.tree.map(lambda _: VMEM, out) if out_specs is None else out_specs,
        scratch_shapes=scratch,
        input_output_aliases=aliases or {},
        compiler_params=pltpu.CompilerParams(vmem_limit_bytes=24 * 1024 * 1024),
        cost_estimate=pl.CostEstimate(flops=flops, bytes_accessed=moved, transcendentals=0),
    )(*args)


def stay(x):
    return pltpu.with_memory_space_constraint(x, pltpu.HBM)


def f32(*shape):
    return jax.ShapeDtypeStruct(shape, jnp.float32)


def tile_masks(slope):
    row = lax.broadcasted_iota(jnp.int32, (8, LANES), 0) % MOMENTS
    return row == 0, row == slope


def first_kernel(state, col2, sems):
    copies = [pltpu.make_async_copy(state.at[t, 2], col2.at[t], sems.at[t]) for t in range(state.shape[0])]
    for copy in copies:
        copy.start()
    for copy in copies:
        copy.wait()


def head_kernel(state, flags, mass, xf, yf, km, before, message, col1, packed, flags_v, mass_v, xf_v, yf_v, km_v, sems, column_sems):
    tracers, columns, levels = state.shape[0], mass.shape[0], mass.shape[1]
    half = LANES // 2
    pairs = ((mass, mass_v), (xf, xf_v), (yf, yf_v), (km, km_v), (flags, flags_v))
    copies = [pltpu.make_async_copy(src, dst, sems.at[i]) for i, (src, dst) in enumerate(pairs)]
    for t in range(tracers):
        for c, place in ((0, message.at[pl.ds(t * levels, levels)]), (1, col1.at[t])):
            copies.append(pltpu.make_async_copy(state.at[t, c], place, column_sems.at[c, t]))
    for copy in copies:
        copy.start()
    for copy in copies[:4]:
        copy.wait()
    for c in range(columns):
        low, top = c * levels, (columns + c) * levels
        packed[low : low + levels, :half] = mass_v[c]
        packed[low : low + levels, half:] = xf_v[c]
        packed[top : top + levels, :half] = yf_v[c]
        packed[top : top + levels - 1, half:] = km_v[c]
        packed[top + levels - 1 : top + levels, half:] = jnp.zeros((1, half), jnp.float32)
    for copy in copies[4:]:
        copy.wait()


def spread(upper_block, ref, *where):
    blocks = [jnp.broadcast_to(ref[(*index, pl.ds(r, 1), slice(None))], (8, LANES)) for index, r in where]
    return jnp.where(upper_block, blocks[1], blocks[0])


def face_row(rows, levels, b):
    return rows - -(-2 * levels // 8) * 8 + b * levels


def turn_kernel(switches, turn):
    tracers, columns = switches.shape[:2]
    levels = switches.shape[2] // 4
    row = lax.broadcasted_iota(jnp.int32, (8, LANES), 0)
    moment = row % MOMENTS
    for t in range(tracers):
        for c in range(columns):
            for l in range(levels):
                for d in range(2):
                    base = l * 4 + d
                    sw = spread(row >= MOMENTS, switches, ((t, c), base), ((t, c), base + 2))
                    take = jnp.where(sw == 1, 1.0, jnp.where(sw == 2, -1.0, 0.0))
                    keep = jnp.where(sw == 0, 1.0, 0.0)
                    turn[d, t, c, l] = jnp.where(moment == 0, take, jnp.where(moment == 1 + d, keep, 1.0))


def sorted_shards(refs, order, start, count):
    odd, high = order[0] % 2 == 1, order[0] >= 2
    a, b, c, d = (ref[start : start + count] for ref in refs)
    a, b, c, d = (jnp.where(odd, b, a), jnp.where(odd, a, b), jnp.where(odd, d, c), jnp.where(odd, c, d))
    return (jnp.where(high, c, a), jnp.where(high, d, b), jnp.where(high, a, c), jnp.where(high, b, d))


def gate_kernel(message, before, out):
    pass


def pre_kernel(own, first, second, third, flags, order, begun, also, rates, factors, message, fields):
    columns, levels = rates.shape[1], rates.shape[2]
    half = LANES // 2
    lane = lax.broadcasted_iota(jnp.int32, (8, LANES), 1)
    row = lax.broadcasted_iota(jnp.int32, (8, LANES), 0)
    upper_block = row >= MOMENTS
    lane_low = lax.broadcasted_iota(jnp.int32, (levels, LANES), 1) < half
    for pair in range(2):
        for c in range(columns):
            shards = sorted_shards((own, first, second, third), order, (pair * columns + c) * levels, levels)
            for b in range(2):
                lo, hi = shards[2 * b], shards[2 * b + 1]
                fields[2 * pair, c, b] = jnp.where(lane_low, lo, pltpu.roll(hi, half, 1))
                flux = jnp.where(lane_low, pltpu.roll(lo, half, 1), hi)
                fields[2 * pair + 1, c, b] = flux
                if pair == 0 and c == 0:
                    eastward = flags[0, pl.ds(2 * b, levels, stride=4), :].astype(jnp.float32)
                    start = face_row(message.shape[0], levels, b)
                    message[start : start + levels] = (2.0 * eastward - 1.0) * flux

    def field(f, c, l):
        return spread(upper_block, fields, ((f, c, 0), l), ((f, c, 1), l))

    def flag(c, l, d):
        base = l * 4 + d
        return spread(upper_block, flags, ((c,), base), ((c,), base + 2)).astype(jnp.float32)

    first_row = (lane == 0) & (row < MOMENTS)
    last_row = (lane == LANES - 1) & (row >= MOMENTS)
    for l in range(levels):
        flux_x = [field(1, c, l) for c in range(columns)]
        flag_x = [flag(c, l, 0) for c in range(columns)]
        east = [flag_x[c] * flux_x[c] for c in range(columns)]
        west = [flux_x[c] - east[c] for c in range(columns)]
        east.append(1.0)
        for c in range(columns):
            share = 1.0 / field(0, c, l)
            rates[0, c, l] = east[c + 1] * share
            rates[1, c, l] = west[c] * share
            flux_y = field(2, c, l)
            north = flag(c, l, 1) * flux_y
            south = pltpu.roll(flux_y - north, 1, 1)
            south = jnp.where(lane == 0, pltpu.roll(south, 4, 0), south)
            rates[2, c, l] = jnp.where(last_row, 0.0, north) * share
            rates[3, c, l] = jnp.where(first_row, 0.0, south) * share

    fixed = row % MOMENTS == 3
    zero = jnp.zeros((8, LANES), jnp.float32)
    below, upper = [None] * columns, [None] * columns
    for l in range(levels):
        for c in range(columns):
            diagonal = zero + 1.0
            if l > 0:
                diagonal = diagonal + below[c]
            if l < levels - 1:
                above = field(3, c, l)
                diagonal = diagonal + above
            if l > 0:
                diagonal = diagonal + below[c] * upper[c]
            inverse = 1.0 / diagonal
            factors[0, c, l] = jnp.where(fixed, 1.0, inverse)
            factors[2, c, l] = jnp.where(fixed, 0.0, below[c] * inverse) if l > 0 else zero
            if l < levels - 1:
                upper[c] = -above * inverse
                factors[1, c, l] = jnp.where(fixed, 0.0, upper[c])
                below[c] = above
            else:
                factors[1, c, l] = zero


def advect(own, east_side, west_side, east, west, turns, slope, masks):
    is_mass, is_slope = masks
    stay = 1.0 - (east + west)
    east_part = east * jnp.where(is_slope, east, 1.0)
    west_part = west * jnp.where(is_slope, west, 1.0)
    east_cross = east * (1.0 - east)
    west_cross = west * (1.0 - west)
    out = []
    for s, e, w, z in zip(own, east_side, west_side, turns):
        total = stay * s + east_part * e + west_part * w
        cross = east_cross * (e - s) - west_cross * (w - s)
        total = total + jnp.where(is_slope, pltpu.roll(cross, slope, 0), 0.0)
        slope_up = pltpu.roll(total, 8 - slope, 0)
        out.append(z * jnp.where(is_mass, slope_up, total) + jnp.where(is_mass, total, 0.0))
    return out


def middle(todo, own, east_side, west_side, east_rate, rates, factors, turn, out):
    tracers, levels = out.shape[0], out.shape[1]
    lane = lax.broadcasted_iota(jnp.int32, (8, LANES), 1)
    at_first, at_last = lane == 0, lane == LANES - 1
    x_masks, y_masks = tile_masks(1), tile_masks(2)
    every = range(tracers)
    c = todo

    def prev(v):
        r = pltpu.roll(v, 1, 1)
        return jnp.where(at_first, pltpu.roll(r, 4, 0), r)

    def following(v):
        r = pltpu.roll(v, LANES - 1, 1)
        return jnp.where(at_last, pltpu.roll(r, 4, 0), r)

    def y_step(values, l):
        return advect(values, [following(v) for v in values], [prev(v) for v in values],
                      rates[2, c, l], rates[3, c, l], [turn[1, t, c, l] for t in every], 2, y_masks)

    carried = [None] * tracers
    for l in range(levels):
        sides = [[side(t, l) for t in every] for side in (own, east_side, west_side)]
        values = advect(*sides, east_rate(l), rates[1, c, l], [turn[0, t, c, l] for t in every], 1, x_masks)
        values = y_step(values, l)
        for t in every:
            v = values[t] * factors[0, c, l]
            if l > 0:
                v = v + factors[2, c, l] * carried[t]
            carried[t] = v
            out[t, l] = v
    for l in range(levels - 1, -1, -1):
        if l < levels - 1:
            for t in every:
                carried[t] = out[t, l] - factors[1, c, l] * carried[t]
        values = y_step(carried, l)
        for t in every:
            out[t, l] = values[t]


def tiles(ref, levels):
    if len(ref.shape) == 4:
        return lambda t, l: ref[t, l]
    return lambda t, l: ref[(t * levels + l) * 8 : (t * levels + l + 1) * 8]


def west_kernel(message, col1, west_halo, rates, factors, turn, out):
    levels = out.shape[1]
    middle(0, tiles(message, levels), tiles(col1, levels), tiles(west_halo, levels),
           lambda l: rates[0, 0, l], rates, factors, turn, out)


def inner_kernel(message, col1, col2, rates, factors, turn, out):
    levels = out.shape[1]
    middle(1, tiles(col1, levels), tiles(col2, levels), tiles(message, levels),
           lambda l: rates[0, 1, l], rates, factors, turn, out)


def east_kernel(col1, col2, halo, rates, factors, turn, before, out, east):
    levels = out.shape[1]
    upper_block = lax.broadcasted_iota(jnp.int32, (8, LANES), 0) >= MOMENTS
    rows = [face_row(halo.shape[0], levels, b) for b in range(2)]

    def east_rate(l):
        flux = spread(upper_block, halo, ((), rows[0] + l), ((), rows[1] + l))
        east[l] = jnp.maximum(flux, 0.0) * rates[0, 2, l]
        return east[l]

    middle(2, tiles(col2, levels), tiles(halo, levels), tiles(col1, levels), east_rate, rates, factors, turn, out)


def finish(c, own, east_side, west_side, east_rate, rates, turn, out, buf, sems):
    tracers, levels = buf.shape[0], buf.shape[1]
    masks = tile_masks(1)
    every = range(tracers)
    copies = []
    for part in range(PARTS):
        low, high = part * levels // PARTS, (part + 1) * levels // PARTS
        for l in range(low, high):
            values = advect(*([side[t, l] for t in every] for side in (own, east_side, west_side)),
                            east_rate(l), rates[1, c, l], [turn[0, t, c, l] for t in every], 1, masks)
            for t in every:
                buf[t, l] = values[t]
        for t in every:
            span = pl.ds(low, high - low)
            copies.append(pltpu.make_async_copy(buf.at[t, span], out.at[t, c, span], sems.at[part, t]))
            copies[-1].start()
    for copy in copies:
        copy.wait()


def last_inner_kernel(mid0, mid1, mid2, rates, turn, out, buf, sems):
    finish(1, mid1, mid2, mid0, lambda l: rates[0, 1, l], rates, turn, out, buf, sems)


def last_east_kernel(begun, mid1, mid2, halo, east, rates, turn, out, buf, sems):
    finish(2, mid2, halo, mid1, lambda l: east[l], rates, turn, out, buf, sems)


def last_west_kernel(begun, mid0, mid1, halo, rates, turn, out, buf, sems):
    finish(0, mid0, mid1, halo, lambda l: rates[0, 0, l], rates, turn, out, buf, sems)


def body(state_adjoint, switches, flags, air_mass, x_flux, y_flux, vertical_mixing):
    state = state_view(state_adjoint)
    switch = pair_view(switches)
    flag = pair_view(flags[None])[0]
    tracers, columns, levels = state.shape[:3]
    order = lax.axis_index("trc").astype(jnp.int32).reshape(1)
    column = f32(tracers, levels, 8, LANES)
    rows = -(-2 * columns * levels // 8) * 8
    length = tracers * levels + -(-2 * levels // 8)
    dma = pltpu.SemaphoreType.DMA
    fields = tuple(stay(x) for x in (air_mass, x_flux, y_flux, vertical_mixing))

    col2 = call(first_kernel, column, (HBM,), [dma((tracers,))], 1, 1, stay(state))
    west_halo = shifted(col2, "lon", 1)
    message, col1, packed, flag = call(
        head_kernel,
        (f32(length, 8, LANES), column, f32(rows, LANES), jax.ShapeDtypeStruct(flag.shape, flag.dtype)),
        (HBM,) * 6 + (VMEM,), [pltpu.VMEM(x.shape, x.dtype) for x in fields] + [dma((5,)), dma((columns, tracers))],
        10**5, 10**6, stay(state), stay(flag), *fields, col2)
    across = swapped(packed, "trc", 2)
    others = [swapped(packed, "trc", 1), across, swapped(across, "trc", 1)]
    turn = call(turn_kernel, f32(2, tracers, columns, levels, 8, LANES), (VMEM,), (), 10**6, 10**6, switch)
    rates, factors, message = call(
        pre_kernel,
        (f32(4, columns, levels, 8, LANES), f32(3, columns, levels, 8, LANES), f32(length * 8, LANES)),
        (VMEM,) * 5 + (SMEM,) + (VMEM,) * 2, [pltpu.VMEM((4, columns, 2, levels, LANES), jnp.float32)], 1, 1,
        packed, *others, flag, order, message.reshape(length * 8, LANES), turn, aliases={6: 2})
    message = call(gate_kernel, f32(length * 8, LANES), (VMEM,) * 2, (), 1, 1, message, west_halo, aliases={0: 0})
    east_message = shifted(message, "lon", -1)
    mid0 = call(west_kernel, column, (VMEM,) * 6, (), 10**6, 10**6, message, col1, west_halo, rates, factors, turn)
    east_halo = shifted(mid0, "lon", -1)
    mid1 = call(inner_kernel, column, (VMEM,) * 6, (), 10**6, 10**6, message, col1, col2, rates, factors, turn)
    mid2, east = call(east_kernel, (column, f32(levels, 8, LANES)), (VMEM,) * 7, (), 10**6, 10**6,
                      col1, col2, east_message, rates, factors, turn, mid0)
    west_halo = shifted(mid2, "lon", 1)

    def last(kernel, aliases, *args):
        first = (HBM,) * len(aliases)
        return call(kernel, f32(*state.shape), first + (VMEM,) * (len(args) - len(first)),
                    [pltpu.VMEM(column.shape, jnp.float32), dma((PARTS, tracers))], 10**6, 10**6,
                    *args, out_specs=HBM, aliases=aliases)

    out = last(last_inner_kernel, {}, mid0, mid1, mid2, rates, turn)
    out = last(last_east_kernel, {0: 0}, out, mid1, mid2, east_halo, east, rates, turn)
    out = last(last_west_kernel, {0: 0}, out, mid0, mid1, west_halo, rates, turn)
    return state_back(out)


def solution(mesh):
    placed = (
        P("trc", None, "lon", None, None),
        P("trc", None, "lon", None, None),
        P(None, "lon", None, None),
        P("lon", None, "trc"),
        P("lon", None, "trc"),
        P("lon", None, "trc"),
        P("lon", None, "trc"),
    )
    return jax.shard_map(
        body,
        mesh=mesh,
        in_specs=placed,
        out_specs=P("trc", None, "lon", None, None),
        check_vma=False,
    )
```

```python
import jax
import jax.numpy as jnp
from jax import lax
from jax.experimental import pallas as pl
from jax.experimental.pallas import tpu as pltpu
from jax.sharding import PartitionSpec as P

LANES = 128
MOMENTS = 4
PARTS = 4
VMEM = pl.BlockSpec(memory_space=pltpu.VMEM)
SMEM = pl.BlockSpec(memory_space=pltpu.SMEM)
HBM = pl.BlockSpec(memory_space=pltpu.HBM)


def state_view(x):
    t, m, c, l, n = x.shape
    b = n // LANES
    x = x.reshape(t, m, c, l, b, LANES).transpose(0, 2, 3, 4, 1, 5)
    return x.reshape(t, c, l, b * m, LANES)


def pair_view(x):
    t, d, c, l, n = x.shape
    b = n // LANES
    x = x.reshape(t, d, c, l, b, LANES).transpose(0, 2, 3, 4, 1, 5)
    return x.reshape(t, c, l * b * d, LANES)


def state_back(y):
    t, c, l, rows, _ = y.shape
    b = rows // MOMENTS
    y = y.reshape(t, c, l, b, MOMENTS, LANES).transpose(0, 4, 1, 2, 3, 5)
    return y.reshape(t, MOMENTS, c, l, b * LANES)


def shifted(value, axis, by):
    count = lax.axis_size(axis)
    return lax.ppermute(value, axis, [(i, (i + by) % count) for i in range(count)])


def swapped(value, axis, mask):
    count = lax.axis_size(axis)
    return lax.ppermute(value, axis, [(i, i ^ mask) for i in range(count)])


def call(kernel, out, in_specs, scratch, flops, moved, *args, out_specs=None, aliases=None):
    return pl.pallas_call(
        kernel,
        out_shape=out,
        in_specs=in_specs,
        out_specs=jax.tree.map(lambda _: VMEM, out) if out_specs is None else out_specs,
        scratch_shapes=scratch,
        input_output_aliases=aliases or {},
        compiler_params=pltpu.CompilerParams(vmem_limit_bytes=24 * 1024 * 1024),
        cost_estimate=pl.CostEstimate(flops=flops, bytes_accessed=moved, transcendentals=0),
    )(*args)


def stay(x):
    return pltpu.with_memory_space_constraint(x, pltpu.HBM)


def f32(*shape):
    return jax.ShapeDtypeStruct(shape, jnp.float32)


def tile_masks(slope):
    row = lax.broadcasted_iota(jnp.int32, (8, LANES), 0) % MOMENTS
    return row == 0, row == slope


def first_kernel(state, col2, sems):
    copies = [pltpu.make_async_copy(state.at[t, 2], col2.at[t], sems.at[t]) for t in range(state.shape[0])]
    for copy in copies:
        copy.start()
    for copy in copies:
        copy.wait()


def head_kernel(flags, mass, xf, yf, km, before, packed, flags_v, mass_v, xf_v, yf_v, km_v, sems):
    columns, levels = mass.shape[0], mass.shape[1]
    half = LANES // 2
    pairs = ((mass, mass_v), (xf, xf_v), (yf, yf_v), (km, km_v), (flags, flags_v))
    copies = [pltpu.make_async_copy(src, dst, sems.at[i]) for i, (src, dst) in enumerate(pairs)]
    for copy in copies:
        copy.start()
    for copy in copies[:4]:
        copy.wait()
    for c in range(columns):
        low, top = c * levels, (columns + c) * levels
        packed[low : low + levels, :half] = mass_v[c]
        packed[low : low + levels, half:] = xf_v[c]
        packed[top : top + levels, :half] = yf_v[c]
        packed[top : top + levels - 1, half:] = km_v[c]
        packed[top + levels - 1 : top + levels, half:] = jnp.zeros((1, half), jnp.float32)
    copies[4].wait()


def spread(upper_block, ref, *where):
    blocks = [jnp.broadcast_to(ref[(*index, pl.ds(r, 1), slice(None))], (8, LANES)) for index, r in where]
    return jnp.where(upper_block, blocks[1], blocks[0])


def face_row(rows, levels, b):
    return rows - -(-2 * levels // 8) * 8 + b * levels


def turn_kernel(state, switches, message, col1, turn, sems):
    tracers, columns = switches.shape[:2]
    levels = switches.shape[2] // 4
    copies = []
    for t in range(tracers):
        for c, place in ((0, message.at[pl.ds(t * levels, levels)]), (1, col1.at[t])):
            copies.append(pltpu.make_async_copy(state.at[t, c], place, sems.at[c, t]))
            copies[-1].start()
    row = lax.broadcasted_iota(jnp.int32, (8, LANES), 0)
    moment = row % MOMENTS
    for t in range(tracers):
        for c in range(columns):
            for l in range(levels):
                for d in range(2):
                    base = l * 4 + d
                    sw = spread(row >= MOMENTS, switches, ((t, c), base), ((t, c), base + 2))
                    take = jnp.where(sw == 1, 1.0, jnp.where(sw == 2, -1.0, 0.0))
                    keep = jnp.where(sw == 0, 1.0, 0.0)
                    turn[d, t, c, l] = jnp.where(moment == 0, take, jnp.where(moment == 1 + d, keep, 1.0))
    for copy in copies:
        copy.wait()


def sorted_shards(refs, order, start, count):
    odd, high = order[0] % 2 == 1, order[0] >= 2
    a, b, c, d = (ref[start : start + count] for ref in refs)
    a, b, c, d = (jnp.where(odd, b, a), jnp.where(odd, a, b), jnp.where(odd, d, c), jnp.where(odd, c, d))
    return (jnp.where(high, c, a), jnp.where(high, d, b), jnp.where(high, a, c), jnp.where(high, b, d))


def gate_kernel(message, before, out):
    pass


def pre_kernel(own, first, second, third, flags, order, begun, also, rates, factors, message, fields):
    columns, levels = rates.shape[1], rates.shape[2]
    half = LANES // 2
    lane = lax.broadcasted_iota(jnp.int32, (8, LANES), 1)
    row = lax.broadcasted_iota(jnp.int32, (8, LANES), 0)
    upper_block = row >= MOMENTS
    lane_low = lax.broadcasted_iota(jnp.int32, (levels, LANES), 1) < half
    for pair in range(2):
        for c in range(columns):
            shards = sorted_shards((own, first, second, third), order, (pair * columns + c) * levels, levels)
            for b in range(2):
                lo, hi = shards[2 * b], shards[2 * b + 1]
                fields[2 * pair, c, b] = jnp.where(lane_low, lo, pltpu.roll(hi, half, 1))
                flux = jnp.where(lane_low, pltpu.roll(lo, half, 1), hi)
                fields[2 * pair + 1, c, b] = flux
                if pair == 0 and c == 0:
                    eastward = flags[0, pl.ds(2 * b, levels, stride=4), :].astype(jnp.float32)
                    start = face_row(message.shape[0], levels, b)
                    message[start : start + levels] = (2.0 * eastward - 1.0) * flux

    def field(f, c, l):
        return spread(upper_block, fields, ((f, c, 0), l), ((f, c, 1), l))

    def flag(c, l, d):
        base = l * 4 + d
        return spread(upper_block, flags, ((c,), base), ((c,), base + 2)).astype(jnp.float32)

    first_row = (lane == 0) & (row < MOMENTS)
    last_row = (lane == LANES - 1) & (row >= MOMENTS)
    for l in range(levels):
        flux_x = [field(1, c, l) for c in range(columns)]
        flag_x = [flag(c, l, 0) for c in range(columns)]
        east = [flag_x[c] * flux_x[c] for c in range(columns)]
        west = [flux_x[c] - east[c] for c in range(columns)]
        east.append(1.0)
        for c in range(columns):
            share = 1.0 / field(0, c, l)
            rates[0, c, l] = east[c + 1] * share
            rates[1, c, l] = west[c] * share
            flux_y = field(2, c, l)
            north = flag(c, l, 1) * flux_y
            south = pltpu.roll(flux_y - north, 1, 1)
            south = jnp.where(lane == 0, pltpu.roll(south, 4, 0), south)
            rates[2, c, l] = jnp.where(last_row, 0.0, north) * share
            rates[3, c, l] = jnp.where(first_row, 0.0, south) * share

    fixed = row % MOMENTS == 3
    zero = jnp.zeros((8, LANES), jnp.float32)
    below, upper = [None] * columns, [None] * columns
    for l in range(levels):
        for c in range(columns):
            diagonal = zero + 1.0
            if l > 0:
                diagonal = diagonal + below[c]
            if l < levels - 1:
                above = field(3, c, l)
                diagonal = diagonal + above
            if l > 0:
                diagonal = diagonal + below[c] * upper[c]
            inverse = 1.0 / diagonal
            factors[0, c, l] = jnp.where(fixed, 1.0, inverse)
            factors[2, c, l] = jnp.where(fixed, 0.0, below[c] * inverse) if l > 0 else zero
            if l < levels - 1:
                upper[c] = -above * inverse
                factors[1, c, l] = jnp.where(fixed, 0.0, upper[c])
                below[c] = above
            else:
                factors[1, c, l] = zero


def advect(own, east_side, west_side, east, west, turns, slope, masks):
    is_mass, is_slope = masks
    stay = 1.0 - (east + west)
    east_part = east * jnp.where(is_slope, east, 1.0)
    west_part = west * jnp.where(is_slope, west, 1.0)
    east_cross = east * (1.0 - east)
    west_cross = west * (1.0 - west)
    out = []
    for s, e, w, z in zip(own, east_side, west_side, turns):
        total = stay * s + east_part * e + west_part * w
        cross = east_cross * (e - s) - west_cross * (w - s)
        total = total + jnp.where(is_slope, pltpu.roll(cross, slope, 0), 0.0)
        slope_up = pltpu.roll(total, 8 - slope, 0)
        out.append(z * jnp.where(is_mass, slope_up, total) + jnp.where(is_mass, total, 0.0))
    return out


def middle(todo, own, east_side, west_side, east_rate, rates, factors, turn, out):
    tracers, levels = out.shape[0], out.shape[1]
    lane = lax.broadcasted_iota(jnp.int32, (8, LANES), 1)
    at_first, at_last = lane == 0, lane == LANES - 1
    x_masks, y_masks = tile_masks(1), tile_masks(2)
    every = range(tracers)
    c = todo

    def prev(v):
        r = pltpu.roll(v, 1, 1)
        return jnp.where(at_first, pltpu.roll(r, 4, 0), r)

    def following(v):
        r = pltpu.roll(v, LANES - 1, 1)
        return jnp.where(at_last, pltpu.roll(r, 4, 0), r)

    def y_step(values, l):
        return advect(values, [following(v) for v in values], [prev(v) for v in values],
                      rates[2, c, l], rates[3, c, l], [turn[1, t, c, l] for t in every], 2, y_masks)

    carried = [None] * tracers
    for l in range(levels):
        sides = [[side(t, l) for t in every] for side in (own, east_side, west_side)]
        values = advect(*sides, east_rate(l), rates[1, c, l], [turn[0, t, c, l] for t in every], 1, x_masks)
        values = y_step(values, l)
        for t in every:
            v = values[t] * factors[0, c, l]
            if l > 0:
                v = v + factors[2, c, l] * carried[t]
            carried[t] = v
            out[t, l] = v
    for l in range(levels - 1, -1, -1):
        if l < levels - 1:
            for t in every:
                carried[t] = out[t, l] - factors[1, c, l] * carried[t]
        values = y_step(carried, l)
        for t in every:
            out[t, l] = values[t]


def tiles(ref, levels):
    if len(ref.shape) == 4:
        return lambda t, l: ref[t, l]
    return lambda t, l: ref[(t * levels + l) * 8 : (t * levels + l + 1) * 8]


def west_kernel(message, col1, west_halo, rates, factors, turn, out):
    levels = out.shape[1]
    middle(0, tiles(message, levels), tiles(col1, levels), tiles(west_halo, levels),
           lambda l: rates[0, 0, l], rates, factors, turn, out)


def inner_kernel(message, col1, col2, rates, factors, turn, out):
    levels = out.shape[1]
    middle(1, tiles(col1, levels), tiles(col2, levels), tiles(message, levels),
           lambda l: rates[0, 1, l], rates, factors, turn, out)


def east_kernel(col1, col2, halo, rates, factors, turn, before, out, east):
    levels = out.shape[1]
    upper_block = lax.broadcasted_iota(jnp.int32, (8, LANES), 0) >= MOMENTS
    rows = [face_row(halo.shape[0], levels, b) for b in range(2)]

    def east_rate(l):
        flux = spread(upper_block, halo, ((), rows[0] + l), ((), rows[1] + l))
        east[l] = jnp.maximum(flux, 0.0) * rates[0, 2, l]
        return east[l]

    middle(2, tiles(col2, levels), tiles(halo, levels), tiles(col1, levels), east_rate, rates, factors, turn, out)


def finish(c, own, east_side, west_side, east_rate, rates, turn, out, buf, sems):
    tracers, levels = buf.shape[0], buf.shape[1]
    masks = tile_masks(1)
    every = range(tracers)
    copies = []
    for part in range(PARTS):
        low, high = part * levels // PARTS, (part + 1) * levels // PARTS
        for l in range(low, high):
            values = advect(*([side[t, l] for t in every] for side in (own, east_side, west_side)),
                            east_rate(l), rates[1, c, l], [turn[0, t, c, l] for t in every], 1, masks)
            for t in every:
                buf[t, l] = values[t]
        for t in every:
            span = pl.ds(low, high - low)
            copies.append(pltpu.make_async_copy(buf.at[t, span], out.at[t, c, span], sems.at[part, t]))
            copies[-1].start()
    for copy in copies:
        copy.wait()


def last_inner_kernel(mid0, mid1, mid2, rates, turn, out, buf, sems):
    finish(1, mid1, mid2, mid0, lambda l: rates[0, 1, l], rates, turn, out, buf, sems)


def last_east_kernel(begun, mid1, mid2, halo, east, rates, turn, out, buf, sems):
    finish(2, mid2, halo, mid1, lambda l: east[l], rates, turn, out, buf, sems)


def last_west_kernel(begun, mid0, mid1, halo, rates, turn, out, buf, sems):
    finish(0, mid0, mid1, halo, lambda l: rates[0, 0, l], rates, turn, out, buf, sems)


def body(state_adjoint, switches, flags, air_mass, x_flux, y_flux, vertical_mixing):
    state = state_view(state_adjoint)
    switch = pair_view(switches)
    flag = pair_view(flags[None])[0]
    tracers, columns, levels = state.shape[:3]
    order = lax.axis_index("trc").astype(jnp.int32).reshape(1)
    column = f32(tracers, levels, 8, LANES)
    rows = -(-2 * columns * levels // 8) * 8
    length = tracers * levels + -(-2 * levels // 8)
    dma = pltpu.SemaphoreType.DMA
    fields = tuple(stay(x) for x in (air_mass, x_flux, y_flux, vertical_mixing))

    col2 = call(first_kernel, column, (HBM,), [dma((tracers,))], 1, 1, stay(state))
    west_halo = shifted(col2, "lon", 1)
    packed, flag = call(
        head_kernel, (f32(rows, LANES), jax.ShapeDtypeStruct(flag.shape, flag.dtype)), (HBM,) * 5 + (VMEM,),
        [pltpu.VMEM(x.shape, x.dtype) for x in fields] + [dma((5,))], 10**5, 10**6, stay(flag), *fields, col2)
    across = swapped(packed, "trc", 2)
    others = [swapped(packed, "trc", 1), across, swapped(across, "trc", 1)]
    message, col1, turn = call(
        turn_kernel, (f32(length, 8, LANES), column, f32(2, tracers, columns, levels, 8, LANES)), (HBM, VMEM),
        [dma((2, tracers))], 10**6, 10**6, stay(state), switch)
    rates, factors, message = call(
        pre_kernel,
        (f32(4, columns, levels, 8, LANES), f32(3, columns, levels, 8, LANES), f32(length * 8, LANES)),
        (VMEM,) * 5 + (SMEM,) + (VMEM,) * 2, [pltpu.VMEM((4, columns, 2, levels, LANES), jnp.float32)], 1, 1,
        packed, *others, flag, order, message.reshape(length * 8, LANES), turn, aliases={6: 2})
    message = call(gate_kernel, f32(length * 8, LANES), (VMEM,) * 2, (), 1, 1, message, west_halo, aliases={0: 0})
    east_message = shifted(message, "lon", -1)
    mid0 = call(west_kernel, column, (VMEM,) * 6, (), 10**6, 10**6, message, col1, west_halo, rates, factors, turn)
    east_halo = shifted(mid0, "lon", -1)
    mid1 = call(inner_kernel, column, (VMEM,) * 6, (), 10**6, 10**6, message, col1, col2, rates, factors, turn)
    mid2, east = call(east_kernel, (column, f32(levels, 8, LANES)), (VMEM,) * 7, (), 10**6, 10**6,
                      col1, col2, east_message, rates, factors, turn, mid0)
    west_halo = shifted(mid2, "lon", 1)

    def last(kernel, aliases, *args):
        first = (HBM,) * len(aliases)
        return call(kernel, f32(*state.shape), first + (VMEM,) * (len(args) - len(first)),
                    [pltpu.VMEM(column.shape, jnp.float32), dma((PARTS, tracers))], 10**6, 10**6,
                    *args, out_specs=HBM, aliases=aliases)

    out = last(last_inner_kernel, {}, mid0, mid1, mid2, rates, turn)
    out = last(last_east_kernel, {0: 0}, out, mid1, mid2, east_halo, east, rates, turn)
    out = last(last_west_kernel, {0: 0}, out, mid0, mid1, west_halo, rates, turn)
    return state_back(out)


def solution(mesh):
    placed = (
        P("trc", None, "lon", None, None),
        P("trc", None, "lon", None, None),
        P(None, "lon", None, None),
        P("lon", None, "trc"),
        P("lon", None, "trc"),
        P("lon", None, "trc"),
        P("lon", None, "trc"),
    )
    return jax.shard_map(
        body,
        mesh=mesh,
        in_specs=placed,
        out_specs=P("trc", None, "lon", None, None),
        check_vma=False,
    )
```

```python
import functools

import jax
import jax.numpy as jnp
from jax import lax
from jax.experimental import pallas as pl
from jax.experimental.pallas import tpu as pltpu
from jax.sharding import PartitionSpec as P

LANES = 128
MOMENTS = 4
PARTS = 4
VMEM = pl.BlockSpec(memory_space=pltpu.VMEM)
SMEM = pl.BlockSpec(memory_space=pltpu.SMEM)
HBM = pl.BlockSpec(memory_space=pltpu.HBM)


def state_view(x):
    t, m, c, l, n = x.shape
    b = n // LANES
    x = x.reshape(t, m, c, l, b, LANES).transpose(0, 2, 3, 4, 1, 5)
    return x.reshape(t, c, l, b * m, LANES)


def pair_view(x):
    t, d, c, l, n = x.shape
    b = n // LANES
    x = x.reshape(t, d, c, l, b, LANES).transpose(0, 2, 3, 4, 1, 5)
    return x.reshape(t, c, l * b * d, LANES)


def state_back(y):
    t, c, l, rows, _ = y.shape
    b = rows // MOMENTS
    y = y.reshape(t, c, l, b, MOMENTS, LANES).transpose(0, 4, 1, 2, 3, 5)
    return y.reshape(t, MOMENTS, c, l, b * LANES)


def shifted(value, axis, by):
    count = lax.axis_size(axis)
    return lax.ppermute(value, axis, [(i, (i + by) % count) for i in range(count)])


def swapped(value, axis, mask):
    count = lax.axis_size(axis)
    return lax.ppermute(value, axis, [(i, i ^ mask) for i in range(count)])


def call(kernel, out, in_specs, scratch, flops, moved, *args, out_specs=None, aliases=None):
    return pl.pallas_call(
        kernel,
        out_shape=out,
        in_specs=in_specs,
        out_specs=jax.tree.map(lambda _: VMEM, out) if out_specs is None else out_specs,
        scratch_shapes=scratch,
        input_output_aliases=aliases or {},
        compiler_params=pltpu.CompilerParams(vmem_limit_bytes=24 * 1024 * 1024),
        cost_estimate=pl.CostEstimate(flops=flops, bytes_accessed=moved, transcendentals=0),
    )(*args)


def stay(x):
    return pltpu.with_memory_space_constraint(x, pltpu.HBM)


def f32(*shape):
    return jax.ShapeDtypeStruct(shape, jnp.float32)


def tile_masks(slope):
    row = lax.broadcasted_iota(jnp.int32, (8, LANES), 0) % MOMENTS
    return row == 0, row == slope


def first_kernel(state, col2, sems):
    copies = [pltpu.make_async_copy(state.at[t, 2], col2.at[t], sems.at[t]) for t in range(state.shape[0])]
    for copy in copies:
        copy.start()
    for copy in copies:
        copy.wait()


def head_kernel(flags, mass, xf, yf, km, before, packed, flags_v, mass_v, xf_v, yf_v, km_v, sems):
    columns, levels = mass.shape[0], mass.shape[1]
    half = LANES // 2
    pairs = ((mass, mass_v), (xf, xf_v), (yf, yf_v), (km, km_v), (flags, flags_v))
    copies = [pltpu.make_async_copy(src, dst, sems.at[i]) for i, (src, dst) in enumerate(pairs)]
    for copy in copies:
        copy.start()
    for copy in copies[:4]:
        copy.wait()
    for c in range(columns):
        low, top = c * levels, (columns + c) * levels
        packed[low : low + levels, :half] = mass_v[c]
        packed[low : low + levels, half:] = xf_v[c]
        packed[top : top + levels, :half] = yf_v[c]
        packed[top : top + levels - 1, half:] = km_v[c]
        packed[top + levels - 1 : top + levels, half:] = jnp.zeros((1, half), jnp.float32)
    copies[4].wait()


def spread(upper_block, ref, *where):
    blocks = [jnp.broadcast_to(ref[(*index, pl.ds(r, 1), slice(None))], (8, LANES)) for index, r in where]
    return jnp.where(upper_block, blocks[1], blocks[0])


def face_row(rows, levels, b):
    return rows - -(-2 * levels // 8) * 8 + b * levels


def turn_kernel(state, switches, message, col1, turn, sems):
    tracers, columns = switches.shape[:2]
    levels = switches.shape[2] // 4
    copies = []
    for t in range(tracers):
        for c, place in ((0, message.at[pl.ds(t * levels, levels)]), (1, col1.at[t])):
            copies.append(pltpu.make_async_copy(state.at[t, c], place, sems.at[c, t]))
            copies[-1].start()
    row = lax.broadcasted_iota(jnp.int32, (8, LANES), 0)
    moment = row % MOMENTS
    for t in range(tracers):
        for c in range(columns):
            for l in range(levels):
                for d in range(2):
                    base = l * 4 + d
                    sw = spread(row >= MOMENTS, switches, ((t, c), base), ((t, c), base + 2))
                    take = jnp.where(sw == 1, 1.0, jnp.where(sw == 2, -1.0, 0.0))
                    keep = jnp.where(sw == 0, 1.0, 0.0)
                    turn[d, t, c, l] = jnp.where(moment == 0, take, jnp.where(moment == 1 + d, keep, 1.0))
    for copy in copies:
        copy.wait()


def sorted_shards(refs, order, start, count):
    odd, high = order[0] % 2 == 1, order[0] >= 2
    a, b, c, d = (ref[start : start + count] for ref in refs)
    a, b, c, d = (jnp.where(odd, b, a), jnp.where(odd, a, b), jnp.where(odd, d, c), jnp.where(odd, c, d))
    return (jnp.where(high, c, a), jnp.where(high, d, b), jnp.where(high, a, c), jnp.where(high, b, d))


def gate_kernel(message, before, out):
    pass


def pre_kernel(own, first, second, third, flags, order, begun, also, rates, factors, message, fields):
    columns, levels = rates.shape[1], rates.shape[2]
    half = LANES // 2
    lane = lax.broadcasted_iota(jnp.int32, (8, LANES), 1)
    row = lax.broadcasted_iota(jnp.int32, (8, LANES), 0)
    upper_block = row >= MOMENTS
    lane_low = lax.broadcasted_iota(jnp.int32, (levels, LANES), 1) < half
    for pair in range(2):
        for c in range(columns):
            shards = sorted_shards((own, first, second, third), order, (pair * columns + c) * levels, levels)
            for b in range(2):
                lo, hi = shards[2 * b], shards[2 * b + 1]
                fields[2 * pair, c, b] = jnp.where(lane_low, lo, pltpu.roll(hi, half, 1))
                flux = jnp.where(lane_low, pltpu.roll(lo, half, 1), hi)
                fields[2 * pair + 1, c, b] = flux
                if pair == 0 and c == 0:
                    eastward = flags[0, pl.ds(2 * b, levels, stride=4), :].astype(jnp.float32)
                    start = face_row(message.shape[0], levels, b)
                    message[start : start + levels] = (2.0 * eastward - 1.0) * flux

    def field(f, c, l):
        return spread(upper_block, fields, ((f, c, 0), l), ((f, c, 1), l))

    def flag(c, l, d):
        base = l * 4 + d
        return spread(upper_block, flags, ((c,), base), ((c,), base + 2)).astype(jnp.float32)

    first_row = (lane == 0) & (row < MOMENTS)
    last_row = (lane == LANES - 1) & (row >= MOMENTS)
    for l in range(levels):
        flux_x = [field(1, c, l) for c in range(columns)]
        flag_x = [flag(c, l, 0) for c in range(columns)]
        east = [flag_x[c] * flux_x[c] for c in range(columns)]
        west = [flux_x[c] - east[c] for c in range(columns)]
        east.append(1.0)
        for c in range(columns):
            share = 1.0 / field(0, c, l)
            rates[0, c, l] = east[c + 1] * share
            rates[1, c, l] = west[c] * share
            flux_y = field(2, c, l)
            north = flag(c, l, 1) * flux_y
            south = pltpu.roll(flux_y - north, 1, 1)
            south = jnp.where(lane == 0, pltpu.roll(south, 4, 0), south)
            rates[2, c, l] = jnp.where(last_row, 0.0, north) * share
            rates[3, c, l] = jnp.where(first_row, 0.0, south) * share

    fixed = row % MOMENTS == 3
    zero = jnp.zeros((8, LANES), jnp.float32)
    below, upper = [None] * columns, [None] * columns
    for l in range(levels):
        for c in range(columns):
            diagonal = zero + 1.0
            if l > 0:
                diagonal = diagonal + below[c]
            if l < levels - 1:
                above = field(3, c, l)
                diagonal = diagonal + above
            if l > 0:
                diagonal = diagonal + below[c] * upper[c]
            inverse = 1.0 / diagonal
            factors[0, c, l] = jnp.where(fixed, 1.0, inverse)
            factors[2, c, l] = jnp.where(fixed, 0.0, below[c] * inverse) if l > 0 else zero
            if l < levels - 1:
                upper[c] = -above * inverse
                factors[1, c, l] = jnp.where(fixed, 0.0, upper[c])
                below[c] = above
            else:
                factors[1, c, l] = zero


def advect(own, east_side, west_side, east, west, turns, slope, masks):
    is_mass, is_slope = masks
    stay = 1.0 - (east + west)
    east_part = east * jnp.where(is_slope, east, 1.0)
    west_part = west * jnp.where(is_slope, west, 1.0)
    east_cross = east * (1.0 - east)
    west_cross = west * (1.0 - west)
    out = []
    for s, e, w, z in zip(own, east_side, west_side, turns):
        total = stay * s + east_part * e + west_part * w
        cross = east_cross * (e - s) - west_cross * (w - s)
        total = total + jnp.where(is_slope, pltpu.roll(cross, slope, 0), 0.0)
        slope_up = pltpu.roll(total, 8 - slope, 0)
        out.append(z * jnp.where(is_mass, slope_up, total) + jnp.where(is_mass, total, 0.0))
    return out


def middle(todo, own, east_side, west_side, east_rate, rates, factors, turn, out):
    tracers, levels = out.shape[0], out.shape[1]
    lane = lax.broadcasted_iota(jnp.int32, (8, LANES), 1)
    at_first, at_last = lane == 0, lane == LANES - 1
    x_masks, y_masks = tile_masks(1), tile_masks(2)
    every = range(tracers)
    c = todo

    def prev(v):
        r = pltpu.roll(v, 1, 1)
        return jnp.where(at_first, pltpu.roll(r, 4, 0), r)

    def following(v):
        r = pltpu.roll(v, LANES - 1, 1)
        return jnp.where(at_last, pltpu.roll(r, 4, 0), r)

    def y_step(values, l):
        return advect(values, [following(v) for v in values], [prev(v) for v in values],
                      rates[2, c, l], rates[3, c, l], [turn[1, t, c, l] for t in every], 2, y_masks)

    carried = [None] * tracers
    for l in range(levels):
        sides = [[side(t, l) for t in every] for side in (own, east_side, west_side)]
        values = advect(*sides, east_rate(l), rates[1, c, l], [turn[0, t, c, l] for t in every], 1, x_masks)
        values = y_step(values, l)
        for t in every:
            v = values[t] * factors[0, c, l]
            if l > 0:
                v = v + factors[2, c, l] * carried[t]
            carried[t] = v
            out[t, l] = v
    for l in range(levels - 1, -1, -1):
        if l < levels - 1:
            for t in every:
                carried[t] = out[t, l] - factors[1, c, l] * carried[t]
        values = y_step(carried, l)
        for t in every:
            out[t, l] = values[t]


def tiles(ref, levels):
    if len(ref.shape) == 4:
        return lambda t, l: ref[t, l]
    return lambda t, l: ref[(t * levels + l) * 8 : (t * levels + l + 1) * 8]


def west_kernel(message, col1, west_halo, rates, factors, turn, out):
    levels = out.shape[1]
    middle(0, tiles(message, levels), tiles(col1, levels), tiles(west_halo, levels),
           lambda l: rates[0, 0, l], rates, factors, turn, out)


def inner_kernel(message, col1, col2, rates, factors, turn, out):
    levels = out.shape[1]
    middle(1, tiles(col1, levels), tiles(col2, levels), tiles(message, levels),
           lambda l: rates[0, 1, l], rates, factors, turn, out)


def east_kernel(col1, col2, halo, rates, factors, turn, before, out, east):
    levels = out.shape[1]
    upper_block = lax.broadcasted_iota(jnp.int32, (8, LANES), 0) >= MOMENTS
    rows = [face_row(halo.shape[0], levels, b) for b in range(2)]

    def east_rate(l):
        flux = spread(upper_block, halo, ((), rows[0] + l), ((), rows[1] + l))
        east[l] = jnp.maximum(flux, 0.0) * rates[0, 2, l]
        return east[l]

    middle(2, tiles(col2, levels), tiles(halo, levels), tiles(col1, levels), east_rate, rates, factors, turn, out)


def local_part(own, near, near_rate, far_rate, sign, masks):
    is_slope = masks[1]
    stay_rate = 1.0 - (near_rate + far_rate)
    near_part = near_rate * jnp.where(is_slope, near_rate, 1.0)
    near_cross = sign * near_rate * (1.0 - near_rate)
    far_cross = -sign * far_rate * (1.0 - far_rate)
    return [stay_rate * s + near_part * n
            + jnp.where(is_slope, pltpu.roll(near_cross * (n - s) - far_cross * s, 1, 0), 0.0) for s, n in zip(own, near)]


def far_part(local, far, far_rate, sign, turns, masks):
    is_mass, is_slope = masks
    part = far_rate * jnp.where(is_slope, far_rate, 1.0)
    cross = -sign * far_rate * (1.0 - far_rate)
    out = []
    for p, f, z in zip(local, far, turns):
        total = p + part * f + jnp.where(is_slope, pltpu.roll(cross * f, 1, 0), 0.0)
        slope_up = pltpu.roll(total, 7, 0)
        out.append(z * jnp.where(is_mass, slope_up, total) + jnp.where(is_mass, total, 0.0))
    return out


def finish(c, values, out, buf, sems):
    tracers, levels = buf.shape[0], buf.shape[1]
    copies = []
    for part in range(PARTS):
        low, high = part * levels // PARTS, (part + 1) * levels // PARTS
        for l in range(low, high):
            for t, value in enumerate(values(l)):
                buf[t, l] = value
        for t in range(tracers):
            span = pl.ds(low, high - low)
            copies.append(pltpu.make_async_copy(buf.at[t, span], out.at[t, c, span], sems.at[part, t]))
            copies[-1].start()
    return copies


def last_inner_kernel(mid0, mid1, mid2, rates, east, turn, out, local0, local2, buf, sems):
    tracers, levels = buf.shape[0], buf.shape[1]
    every = range(tracers)
    masks = tile_masks(1)

    def values(l):
        return advect(*([side[t, l] for t in every] for side in (mid1, mid2, mid0)), rates[0, 1, l], rates[1, 1, l],
                      [turn[0, t, 1, l] for t in every], 1, masks)

    copies = finish(1, values, out, buf, sems)
    for l in range(levels):
        inner = [mid1[t, l] for t in every]
        first = local_part([mid0[t, l] for t in every], inner, rates[0, 0, l], rates[1, 0, l], 1.0, masks)
        final = local_part([mid2[t, l] for t in every], inner, rates[1, 2, l], east[l], -1.0, masks)
        for t in every:
            local0[t, l] = first[t]
            local2[t, l] = final[t]
    for copy in copies:
        copy.wait()


def last_outer_kernel(c, begun, local, halo, far_rate, turn, out, buf, sems):
    every = range(buf.shape[0])
    masks = tile_masks(1)

    def values(l):
        rate = far_rate[l] if c else far_rate[1, c, l]
        return far_part([local[t, l] for t in every], [halo[t, l] for t in every], rate, -1.0 if c else 1.0,
                        [turn[0, t, c, l] for t in every], masks)

    for copy in finish(c, values, out, buf, sems):
        copy.wait()


def body(state_adjoint, switches, flags, air_mass, x_flux, y_flux, vertical_mixing):
    state = state_view(state_adjoint)
    switch = pair_view(switches)
    flag = pair_view(flags[None])[0]
    tracers, columns, levels = state.shape[:3]
    order = lax.axis_index("trc").astype(jnp.int32).reshape(1)
    column = f32(tracers, levels, 8, LANES)
    rows = -(-2 * columns * levels // 8) * 8
    length = tracers * levels + -(-2 * levels // 8)
    dma = pltpu.SemaphoreType.DMA
    fields = tuple(stay(x) for x in (air_mass, x_flux, y_flux, vertical_mixing))

    col2 = call(first_kernel, column, (HBM,), [dma((tracers,))], 1, 1, stay(state))
    west_halo = shifted(col2, "lon", 1)
    packed, flag = call(
        head_kernel, (f32(rows, LANES), jax.ShapeDtypeStruct(flag.shape, flag.dtype)), (HBM,) * 5 + (VMEM,),
        [pltpu.VMEM(x.shape, x.dtype) for x in fields] + [dma((5,))], 10**5, 10**6, stay(flag), *fields, col2)
    across = swapped(packed, "trc", 2)
    others = [swapped(packed, "trc", 1), across, swapped(across, "trc", 1)]
    message, col1, turn = call(
        turn_kernel, (f32(length, 8, LANES), column, f32(2, tracers, columns, levels, 8, LANES)), (HBM, VMEM),
        [dma((2, tracers))], 10**6, 10**6, stay(state), switch)
    rates, factors, message = call(
        pre_kernel,
        (f32(4, columns, levels, 8, LANES), f32(3, columns, levels, 8, LANES), f32(length * 8, LANES)),
        (VMEM,) * 5 + (SMEM,) + (VMEM,) * 2, [pltpu.VMEM((4, columns, 2, levels, LANES), jnp.float32)], 1, 1,
        packed, *others, flag, order, message.reshape(length * 8, LANES), turn, aliases={6: 2})
    message = call(gate_kernel, f32(length * 8, LANES), (VMEM,) * 2, (), 1, 1, message, west_halo, aliases={0: 0})
    east_message = shifted(message, "lon", -1)
    mid0 = call(west_kernel, column, (VMEM,) * 6, (), 10**6, 10**6, message, col1, west_halo, rates, factors, turn)
    east_halo = shifted(mid0, "lon", -1)
    mid1 = call(inner_kernel, column, (VMEM,) * 6, (), 10**6, 10**6, message, col1, col2, rates, factors, turn)
    mid2, east = call(east_kernel, (column, f32(levels, 8, LANES)), (VMEM,) * 7, (), 10**6, 10**6,
                      col1, col2, east_message, rates, factors, turn, mid0)
    west_halo = shifted(mid2, "lon", 1)

    scratch = [pltpu.VMEM(column.shape, jnp.float32), dma((PARTS, tracers))]
    out, local0, local2 = call(last_inner_kernel, (f32(*state.shape), column, column), (VMEM,) * 6, scratch,
                               10**6, 10**6, mid0, mid1, mid2, rates, east, turn, out_specs=(HBM, VMEM, VMEM))
    for c, local, halo, rate in ((2, local2, east_halo, east), (0, local0, west_halo, rates)):
        out = call(functools.partial(last_outer_kernel, c), f32(*state.shape), (HBM,) + (VMEM,) * 4, scratch,
                   10**6, 10**6, out, local, halo, rate, turn, out_specs=HBM, aliases={0: 0})
    return state_back(out)


def solution(mesh):
    placed = (
        P("trc", None, "lon", None, None),
        P("trc", None, "lon", None, None),
        P(None, "lon", None, None),
        P("lon", None, "trc"),
        P("lon", None, "trc"),
        P("lon", None, "trc"),
        P("lon", None, "trc"),
    )
    return jax.shard_map(
        body,
        mesh=mesh,
        in_specs=placed,
        out_specs=P("trc", None, "lon", None, None),
        check_vma=False,
    )
```

```python
import functools

import jax
import jax.numpy as jnp
from jax import lax
from jax.experimental import pallas as pl
from jax.experimental.pallas import tpu as pltpu
from jax.sharding import PartitionSpec as P

LANES = 128
MOMENTS = 4
PARTS = 4
VMEM = pl.BlockSpec(memory_space=pltpu.VMEM)
SMEM = pl.BlockSpec(memory_space=pltpu.SMEM)
HBM = pl.BlockSpec(memory_space=pltpu.HBM)


def state_view(x):
    t, m, c, l, n = x.shape
    b = n // LANES
    x = x.reshape(t, m, c, l, b, LANES).transpose(0, 2, 3, 4, 1, 5)
    return x.reshape(t, c, l, b * m, LANES)


def pair_view(x):
    t, d, c, l, n = x.shape
    b = n // LANES
    x = x.reshape(t, d, c, l, b, LANES).transpose(0, 2, 3, 4, 1, 5)
    return x.reshape(t, c, l * b * d, LANES)


def state_back(y):
    t, c, l, rows, _ = y.shape
    b = rows // MOMENTS
    y = y.reshape(t, c, l, b, MOMENTS, LANES).transpose(0, 4, 1, 2, 3, 5)
    return y.reshape(t, MOMENTS, c, l, b * LANES)


def shifted(value, axis, by):
    count = lax.axis_size(axis)
    return lax.ppermute(value, axis, [(i, (i + by) % count) for i in range(count)])


def swapped(value, axis, mask):
    count = lax.axis_size(axis)
    return lax.ppermute(value, axis, [(i, i ^ mask) for i in range(count)])


def call(kernel, out, in_specs, scratch, flops, moved, *args, out_specs=None, aliases=None):
    return pl.pallas_call(
        kernel,
        out_shape=out,
        in_specs=in_specs,
        out_specs=jax.tree.map(lambda _: VMEM, out) if out_specs is None else out_specs,
        scratch_shapes=scratch,
        input_output_aliases=aliases or {},
        compiler_params=pltpu.CompilerParams(vmem_limit_bytes=24 * 1024 * 1024),
        cost_estimate=pl.CostEstimate(flops=flops, bytes_accessed=moved, transcendentals=0),
    )(*args)


def stay(x):
    return pltpu.with_memory_space_constraint(x, pltpu.HBM)


def f32(*shape):
    return jax.ShapeDtypeStruct(shape, jnp.float32)


def tile_masks(slope):
    row = lax.broadcasted_iota(jnp.int32, (8, LANES), 0) % MOMENTS
    return row == 0, row == slope


def first_kernel(state, col2, sems):
    copies = [pltpu.make_async_copy(state.at[t, 2], col2.at[t], sems.at[t]) for t in range(state.shape[0])]
    for copy in copies:
        copy.start()
    for copy in copies:
        copy.wait()


def head_kernel(flags, mass, xf, yf, km, before, packed, flags_v, mass_v, xf_v, yf_v, km_v, sems):
    columns, levels = mass.shape[0], mass.shape[1]
    half = LANES // 2
    pairs = ((mass, mass_v), (xf, xf_v), (yf, yf_v), (km, km_v), (flags, flags_v))
    copies = [pltpu.make_async_copy(src, dst, sems.at[i]) for i, (src, dst) in enumerate(pairs)]
    for copy in copies:
        copy.start()
    for copy in copies[:4]:
        copy.wait()
    for c in range(columns):
        low, top = c * levels, (columns + c) * levels
        packed[low : low + levels, :half] = mass_v[c]
        packed[low : low + levels, half:] = xf_v[c]
        packed[top : top + levels, :half] = yf_v[c]
        packed[top : top + levels - 1, half:] = km_v[c]
        packed[top + levels - 1 : top + levels, half:] = jnp.zeros((1, half), jnp.float32)
    copies[4].wait()


def spread(upper_block, ref, *where):
    blocks = [jnp.broadcast_to(ref[(*index, pl.ds(r, 1), slice(None))], (8, LANES)) for index, r in where]
    return jnp.where(upper_block, blocks[1], blocks[0])


def face_row(rows, levels, b):
    return rows - -(-2 * levels // 8) * 8 + b * levels


def turn_kernel(state, switches, message, col1, turn, sems):
    tracers, columns = switches.shape[:2]
    levels = switches.shape[2] // 4
    copies = []
    for t in range(tracers):
        for c, place in ((0, message.at[pl.ds(t * levels, levels)]), (1, col1.at[t])):
            copies.append(pltpu.make_async_copy(state.at[t, c], place, sems.at[c, t]))
            copies[-1].start()
    row = lax.broadcasted_iota(jnp.int32, (8, LANES), 0)
    moment = row % MOMENTS
    for t in range(tracers):
        for c in range(columns):
            for l in range(levels):
                for d in range(2):
                    base = l * 4 + d
                    sw = spread(row >= MOMENTS, switches, ((t, c), base), ((t, c), base + 2))
                    take = jnp.where(sw == 1, 1.0, jnp.where(sw == 2, -1.0, 0.0))
                    keep = jnp.where(sw == 0, 1.0, 0.0)
                    turn[d, t, c, l] = jnp.where(moment == 0, take, jnp.where(moment == 1 + d, keep, 1.0))
    for copy in copies:
        copy.wait()


def sorted_shards(refs, order, start, count):
    odd, high = order[0] % 2 == 1, order[0] >= 2
    a, b, c, d = (ref[start : start + count] for ref in refs)
    a, b, c, d = (jnp.where(odd, b, a), jnp.where(odd, a, b), jnp.where(odd, d, c), jnp.where(odd, c, d))
    return (jnp.where(high, c, a), jnp.where(high, d, b), jnp.where(high, a, c), jnp.where(high, b, d))


def gate_kernel(message, before, out):
    pass


def pre_kernel(own, first, second, third, flags, order, begun, also, rates, factors, message, fields):
    columns, levels = rates.shape[1], rates.shape[2]
    half = LANES // 2
    lane = lax.broadcasted_iota(jnp.int32, (8, LANES), 1)
    row = lax.broadcasted_iota(jnp.int32, (8, LANES), 0)
    upper_block = row >= MOMENTS
    lane_low = lax.broadcasted_iota(jnp.int32, (levels, LANES), 1) < half
    for pair in range(2):
        for c in range(columns):
            shards = sorted_shards((own, first, second, third), order, (pair * columns + c) * levels, levels)
            for b in range(2):
                lo, hi = shards[2 * b], shards[2 * b + 1]
                fields[2 * pair, c, b] = jnp.where(lane_low, lo, pltpu.roll(hi, half, 1))
                flux = jnp.where(lane_low, pltpu.roll(lo, half, 1), hi)
                fields[2 * pair + 1, c, b] = flux
                if pair == 0 and c == 0:
                    eastward = flags[0, pl.ds(2 * b, levels, stride=4), :].astype(jnp.float32)
                    start = face_row(message.shape[0], levels, b)
                    message[start : start + levels] = (2.0 * eastward - 1.0) * flux

    def field(f, c, l):
        return spread(upper_block, fields, ((f, c, 0), l), ((f, c, 1), l))

    def flag(c, l, d):
        base = l * 4 + d
        return spread(upper_block, flags, ((c,), base), ((c,), base + 2)).astype(jnp.float32)

    first_row = (lane == 0) & (row < MOMENTS)
    last_row = (lane == LANES - 1) & (row >= MOMENTS)
    for l in range(levels):
        flux_x = [field(1, c, l) for c in range(columns)]
        flag_x = [flag(c, l, 0) for c in range(columns)]
        east = [flag_x[c] * flux_x[c] for c in range(columns)]
        west = [flux_x[c] - east[c] for c in range(columns)]
        east.append(1.0)
        for c in range(columns):
            share = 1.0 / field(0, c, l)
            rates[0, c, l] = east[c + 1] * share
            rates[1, c, l] = west[c] * share
            flux_y = field(2, c, l)
            north = flag(c, l, 1) * flux_y
            south = pltpu.roll(flux_y - north, 1, 1)
            south = jnp.where(lane == 0, pltpu.roll(south, 4, 0), south)
            rates[2, c, l] = jnp.where(last_row, 0.0, north) * share
            rates[3, c, l] = jnp.where(first_row, 0.0, south) * share

    fixed = row % MOMENTS == 3
    zero = jnp.zeros((8, LANES), jnp.float32)
    below, upper = [None] * columns, [None] * columns
    for l in range(levels):
        for c in range(columns):
            diagonal = zero + 1.0
            if l > 0:
                diagonal = diagonal + below[c]
            if l < levels - 1:
                above = field(3, c, l)
                diagonal = diagonal + above
            if l > 0:
                diagonal = diagonal + below[c] * upper[c]
            inverse = 1.0 / diagonal
            factors[0, c, l] = jnp.where(fixed, 1.0, inverse)
            factors[2, c, l] = jnp.where(fixed, 0.0, below[c] * inverse) if l > 0 else zero
            if l < levels - 1:
                upper[c] = -above * inverse
                factors[1, c, l] = jnp.where(fixed, 0.0, upper[c])
                below[c] = above
            else:
                factors[1, c, l] = zero


def advect(own, east_side, west_side, east, west, turns, slope, masks):
    is_mass, is_slope = masks
    stay = 1.0 - (east + west)
    east_part = east * jnp.where(is_slope, east, 1.0)
    west_part = west * jnp.where(is_slope, west, 1.0)
    east_cross = east * (1.0 - east)
    west_cross = west * (1.0 - west)
    out = []
    for s, e, w, z in zip(own, east_side, west_side, turns):
        total = stay * s + east_part * e + west_part * w
        cross = east_cross * (e - s) - west_cross * (w - s)
        total = total + jnp.where(is_slope, pltpu.roll(cross, slope, 0), 0.0)
        slope_up = pltpu.roll(total, 8 - slope, 0)
        out.append(z * jnp.where(is_mass, slope_up, total) + jnp.where(is_mass, total, 0.0))
    return out


def middle(todo, own, east_side, west_side, east_rate, rates, factors, turn, out):
    tracers, levels = out.shape[0], out.shape[1]
    lane = lax.broadcasted_iota(jnp.int32, (8, LANES), 1)
    at_first, at_last = lane == 0, lane == LANES - 1
    x_masks, y_masks = tile_masks(1), tile_masks(2)
    every = range(tracers)
    c = todo

    def prev(v):
        r = pltpu.roll(v, 1, 1)
        return jnp.where(at_first, pltpu.roll(r, 4, 0), r)

    def following(v):
        r = pltpu.roll(v, LANES - 1, 1)
        return jnp.where(at_last, pltpu.roll(r, 4, 0), r)

    def y_step(values, l):
        return advect(values, [following(v) for v in values], [prev(v) for v in values],
                      rates[2, c, l], rates[3, c, l], [turn[1, t, c, l] for t in every], 2, y_masks)

    carried = [None] * tracers
    for l in range(levels):
        sides = [[side(t, l) for t in every] for side in (own, east_side, west_side)]
        values = advect(*sides, east_rate(l), rates[1, c, l], [turn[0, t, c, l] for t in every], 1, x_masks)
        values = y_step(values, l)
        for t in every:
            v = values[t] * factors[0, c, l]
            if l > 0:
                v = v + factors[2, c, l] * carried[t]
            carried[t] = v
            out[t, l] = v
    for l in range(levels - 1, -1, -1):
        if l < levels - 1:
            for t in every:
                carried[t] = out[t, l] - factors[1, c, l] * carried[t]
        values = y_step(carried, l)
        for t in every:
            out[t, l] = values[t]


def tiles(ref, levels):
    if len(ref.shape) == 4:
        return lambda t, l: ref[t, l]
    return lambda t, l: ref[(t * levels + l) * 8 : (t * levels + l + 1) * 8]


def west_kernel(message, col1, west_halo, rates, factors, turn, out):
    levels = out.shape[1]
    middle(0, tiles(message, levels), tiles(col1, levels), tiles(west_halo, levels),
           lambda l: rates[0, 0, l], rates, factors, turn, out)


def inner_kernel(message, col1, col2, rates, factors, turn, out):
    levels = out.shape[1]
    middle(1, tiles(col1, levels), tiles(col2, levels), tiles(message, levels),
           lambda l: rates[0, 1, l], rates, factors, turn, out)


def east_kernel(col1, col2, halo, rates, factors, turn, before, out, east):
    levels = out.shape[1]
    upper_block = lax.broadcasted_iota(jnp.int32, (8, LANES), 0) >= MOMENTS
    rows = [face_row(halo.shape[0], levels, b) for b in range(2)]

    def east_rate(l):
        flux = spread(upper_block, halo, ((), rows[0] + l), ((), rows[1] + l))
        east[l] = jnp.maximum(flux, 0.0) * rates[0, 2, l]
        return east[l]

    middle(2, tiles(col2, levels), tiles(halo, levels), tiles(col1, levels), east_rate, rates, factors, turn, out)


def local_part(own, near, near_rate, far_rate, sign, masks):
    is_slope = masks[1]
    stay_rate = 1.0 - (near_rate + far_rate)
    near_part = near_rate * jnp.where(is_slope, near_rate, 1.0)
    near_cross = sign * near_rate * (1.0 - near_rate)
    far_cross = -sign * far_rate * (1.0 - far_rate)
    return [stay_rate * s + near_part * n
            + jnp.where(is_slope, pltpu.roll(near_cross * (n - s) - far_cross * s, 1, 0), 0.0) for s, n in zip(own, near)]


def far_part(local, far, far_rate, sign, turns, masks):
    is_mass, is_slope = masks
    part = far_rate * jnp.where(is_slope, far_rate, 1.0)
    cross = -sign * far_rate * (1.0 - far_rate)
    out = []
    for p, f, z in zip(local, far, turns):
        total = p + part * f + jnp.where(is_slope, pltpu.roll(cross * f, 1, 0), 0.0)
        slope_up = pltpu.roll(total, 7, 0)
        out.append(z * jnp.where(is_mass, slope_up, total) + jnp.where(is_mass, total, 0.0))
    return out


def finish(c, values, out, buf, sems):
    tracers, levels = buf.shape[0], buf.shape[1]
    copies = []
    for part in range(PARTS):
        low, high = part * levels // PARTS, (part + 1) * levels // PARTS
        for l in range(low, high):
            for t, value in enumerate(values(l)):
                buf[t, l] = value
        for t in range(tracers):
            span = pl.ds(low, high - low)
            copies.append(pltpu.make_async_copy(buf.at[t, span], out.at[t, c, span], sems.at[part, t]))
            copies[-1].start()
    return copies


def last_inner_kernel(mid0, mid1, mid2, rates, east, turn, out, local0, local2, buf, sems):
    tracers, levels = buf.shape[0], buf.shape[1]
    every = range(tracers)
    masks = tile_masks(1)

    def values(l):
        return advect(*([side[t, l] for t in every] for side in (mid1, mid2, mid0)), rates[0, 1, l], rates[1, 1, l],
                      [turn[0, t, 1, l] for t in every], 1, masks)

    copies = finish(1, values, out, buf, sems)
    for l in range(levels):
        inner = [mid1[t, l] for t in every]
        first = local_part([mid0[t, l] for t in every], inner, rates[0, 0, l], rates[1, 0, l], 1.0, masks)
        final = local_part([mid2[t, l] for t in every], inner, rates[1, 2, l], east[l], -1.0, masks)
        for t in every:
            local0[t, l] = first[t]
            local2[t, l] = final[t]
    for copy in copies:
        copy.wait()


def last_outer_kernel(c, begun, local, halo, far_rate, turn, out, buf, sems):
    every = range(buf.shape[0])
    masks = tile_masks(1)

    def values(l):
        rate = far_rate[l] if c else far_rate[1, c, l]
        return far_part([local[t, l] for t in every], [halo[t, l] for t in every], rate, -1.0 if c else 1.0,
                        [turn[0, t, c, l] for t in every], masks)

    for copy in finish(c, values, out, buf, sems):
        copy.wait()


def body(state_adjoint, switches, flags, air_mass, x_flux, y_flux, vertical_mixing):
    state = state_view(state_adjoint)
    switch = pair_view(switches)
    flag = pair_view(flags[None])[0]
    tracers, columns, levels = state.shape[:3]
    order = lax.axis_index("trc").astype(jnp.int32).reshape(1)
    column = f32(tracers, levels, 8, LANES)
    rows = -(-2 * columns * levels // 8) * 8
    length = tracers * levels + -(-2 * levels // 8)
    dma = pltpu.SemaphoreType.DMA
    fields = tuple(stay(x) for x in (air_mass, x_flux, y_flux, vertical_mixing))

    col2 = call(first_kernel, column, (HBM,), [dma((tracers,))], 1, 1, stay(state))
    west_halo = shifted(col2, "lon", 1)
    packed, flag = call(
        head_kernel, (f32(rows, LANES), jax.ShapeDtypeStruct(flag.shape, flag.dtype)), (HBM,) * 5 + (VMEM,),
        [pltpu.VMEM(x.shape, x.dtype) for x in fields] + [dma((5,))], 10**5, 10**6, stay(flag), *fields, col2)
    across = swapped(packed, "trc", 2)
    others = [swapped(packed, "trc", 1), across, swapped(across, "trc", 1)]
    message, col1, turn = call(
        turn_kernel, (f32(length, 8, LANES), column, f32(2, tracers, columns, levels, 8, LANES)), (HBM, VMEM),
        [dma((2, tracers))], 10**6, 10**6, stay(state), switch)
    rates, factors, message = call(
        pre_kernel,
        (f32(4, columns, levels, 8, LANES), f32(3, columns, levels, 8, LANES), f32(length * 8, LANES)),
        (VMEM,) * 5 + (SMEM,) + (VMEM,) * 2, [pltpu.VMEM((4, columns, 2, levels, LANES), jnp.float32)], 1, 1,
        packed, *others, flag, order, message.reshape(length * 8, LANES), turn, aliases={6: 2})
    message = call(gate_kernel, f32(length * 8, LANES), (VMEM,) * 2, (), 1, 1, message, west_halo, aliases={0: 0})
    east_message = shifted(message, "lon", -1)
    mid0 = call(west_kernel, column, (VMEM,) * 6, (), 10**6, 10**6, message, col1, west_halo, rates, factors, turn)
    mid0 = call(gate_kernel, column, (VMEM,) * 2, (), 1, 1, mid0, east_message, aliases={0: 0})
    east_halo = shifted(mid0, "lon", -1)
    mid1 = call(inner_kernel, column, (VMEM,) * 6, (), 10**6, 10**6, message, col1, col2, rates, factors, turn)
    mid2, east = call(east_kernel, (column, f32(levels, 8, LANES)), (VMEM,) * 7, (), 10**6, 10**6,
                      col1, col2, east_message, rates, factors, turn, mid0)
    west_halo = shifted(mid2, "lon", 1)

    scratch = [pltpu.VMEM(column.shape, jnp.float32), dma((PARTS, tracers))]
    out, local0, local2 = call(last_inner_kernel, (f32(*state.shape), column, column), (VMEM,) * 6, scratch,
                               10**6, 10**6, mid0, mid1, mid2, rates, east, turn, out_specs=(HBM, VMEM, VMEM))
    for c, local, halo, rate in ((2, local2, east_halo, east), (0, local0, west_halo, rates)):
        out = call(functools.partial(last_outer_kernel, c), f32(*state.shape), (HBM,) + (VMEM,) * 4, scratch,
                   10**6, 10**6, out, local, halo, rate, turn, out_specs=HBM, aliases={0: 0})
    return state_back(out)


def solution(mesh):
    placed = (
        P("trc", None, "lon", None, None),
        P("trc", None, "lon", None, None),
        P(None, "lon", None, None),
        P("lon", None, "trc"),
        P("lon", None, "trc"),
        P("lon", None, "trc"),
        P("lon", None, "trc"),
    )
    return jax.shard_map(
        body,
        mesh=mesh,
        in_specs=placed,
        out_specs=P("trc", None, "lon", None, None),
        check_vma=False,
    )
```

```python
import jax
import jax.numpy as jnp
from jax import lax
from jax.experimental import pallas as pl
from jax.experimental.pallas import tpu as pltpu
from jax.sharding import PartitionSpec as P

LANES = 128
MOMENTS = 4
PARTS = 4
VMEM = pl.BlockSpec(memory_space=pltpu.VMEM)
SMEM = pl.BlockSpec(memory_space=pltpu.SMEM)
HBM = pl.BlockSpec(memory_space=pltpu.HBM)


def state_view(x):
    t, m, c, l, n = x.shape
    b = n // LANES
    x = x.reshape(t, m, c, l, b, LANES).transpose(0, 2, 3, 4, 1, 5)
    return x.reshape(t, c, l, b * m, LANES)


def pair_view(x):
    t, d, c, l, n = x.shape
    b = n // LANES
    x = x.reshape(t, d, c, l, b, LANES).transpose(0, 2, 3, 4, 1, 5)
    return x.reshape(t, c, l * b * d, LANES)


def state_back(y):
    t, c, l, rows, _ = y.shape
    b = rows // MOMENTS
    y = y.reshape(t, c, l, b, MOMENTS, LANES).transpose(0, 4, 1, 2, 3, 5)
    return y.reshape(t, MOMENTS, c, l, b * LANES)


def shifted(value, axis, by):
    count = lax.axis_size(axis)
    return lax.ppermute(value, axis, [(i, (i + by) % count) for i in range(count)])


def swapped(value, axis, mask):
    count = lax.axis_size(axis)
    return lax.ppermute(value, axis, [(i, i ^ mask) for i in range(count)])


def call(kernel, out, in_specs, scratch, flops, moved, *args, out_specs=None, aliases=None):
    return pl.pallas_call(
        kernel,
        out_shape=out,
        in_specs=in_specs,
        out_specs=jax.tree.map(lambda _: VMEM, out) if out_specs is None else out_specs,
        scratch_shapes=scratch,
        input_output_aliases=aliases or {},
        compiler_params=pltpu.CompilerParams(vmem_limit_bytes=24 * 1024 * 1024),
        cost_estimate=pl.CostEstimate(flops=flops, bytes_accessed=moved, transcendentals=0),
    )(*args)


def stay(x):
    return pltpu.with_memory_space_constraint(x, pltpu.HBM)


def f32(*shape):
    return jax.ShapeDtypeStruct(shape, jnp.float32)


def tile_masks(slope):
    row = lax.broadcasted_iota(jnp.int32, (8, LANES), 0) % MOMENTS
    return row == 0, row == slope


def head_kernel(state, mass, xf, yf, km, col2, packed, mass_v, xf_v, yf_v, km_v, sems):
    columns, levels = mass.shape[0], mass.shape[1]
    half = LANES // 2
    pairs = [(state.at[t, 2], col2.at[t]) for t in range(state.shape[0])]
    pairs = [(mass, mass_v), (xf, xf_v), (yf, yf_v), (km, km_v)] + pairs
    copies = [pltpu.make_async_copy(src, dst, sems.at[i]) for i, (src, dst) in enumerate(pairs)]
    for copy in copies:
        copy.start()
    for copy in copies[:4]:
        copy.wait()
    for c in range(columns):
        low, top = c * levels, (columns + c) * levels
        packed[low : low + levels, :half] = mass_v[c]
        packed[low : low + levels, half:] = xf_v[c]
        packed[top : top + levels, :half] = yf_v[c]
        packed[top : top + levels - 1, half:] = km_v[c]
        packed[top + levels - 1 : top + levels, half:] = jnp.zeros((1, half), jnp.float32)
    for copy in copies[4:]:
        copy.wait()


def spread(upper_block, ref, *where):
    blocks = [jnp.broadcast_to(ref[(*index, pl.ds(r, 1), slice(None))], (8, LANES)) for index, r in where]
    return jnp.where(upper_block, blocks[1], blocks[0])


def face_row(rows, levels, b):
    return rows - -(-2 * levels // 8) * 8 + b * levels


def turn_kernel(state, flags, switches_hbm, message, col1, flags_v, turn, switches, sems, flag_sem, switch_sem):
    tracers, columns = switches.shape[:2]
    levels = switches.shape[2] // 4
    fetch = pltpu.make_async_copy(switches_hbm, switches, switch_sem)
    fetch.start()
    copies = [pltpu.make_async_copy(flags, flags_v, flag_sem)]
    copies[0].start()
    for t in range(tracers):
        for c, place in ((0, message.at[pl.ds(t * levels, levels)]), (1, col1.at[t])):
            copies.append(pltpu.make_async_copy(state.at[t, c], place, sems.at[c, t]))
            copies[-1].start()
    fetch.wait()
    row = lax.broadcasted_iota(jnp.int32, (8, LANES), 0)
    moment = row % MOMENTS
    for t in range(tracers):
        for c in range(columns):
            for l in range(levels):
                for d in range(2):
                    base = l * 4 + d
                    sw = spread(row >= MOMENTS, switches, ((t, c), base), ((t, c), base + 2))
                    take = jnp.where(sw == 1, 1.0, jnp.where(sw == 2, -1.0, 0.0))
                    keep = jnp.where(sw == 0, 1.0, 0.0)
                    turn[d, t, c, l] = jnp.where(moment == 0, take, jnp.where(moment == 1 + d, keep, 1.0))
    for copy in copies:
        copy.wait()


def sorted_shards(refs, order, start, count):
    odd, high = order[0] % 2 == 1, order[0] >= 2
    a, b, c, d = (ref[start : start + count] for ref in refs)
    a, b, c, d = (jnp.where(odd, b, a), jnp.where(odd, a, b), jnp.where(odd, d, c), jnp.where(odd, c, d))
    return (jnp.where(high, c, a), jnp.where(high, d, b), jnp.where(high, a, c), jnp.where(high, b, d))


def gate_kernel(message, before, out):
    pass


def pre_kernel(own, first, second, third, flags, order, begun, also, rates, factors, message, fields):
    columns, levels = rates.shape[1], rates.shape[2]
    half = LANES // 2
    lane = lax.broadcasted_iota(jnp.int32, (8, LANES), 1)
    row = lax.broadcasted_iota(jnp.int32, (8, LANES), 0)
    upper_block = row >= MOMENTS
    lane_low = lax.broadcasted_iota(jnp.int32, (levels, LANES), 1) < half
    for pair in range(2):
        for c in range(columns):
            shards = sorted_shards((own, first, second, third), order, (pair * columns + c) * levels, levels)
            for b in range(2):
                lo, hi = shards[2 * b], shards[2 * b + 1]
                fields[2 * pair, c, b] = jnp.where(lane_low, lo, pltpu.roll(hi, half, 1))
                flux = jnp.where(lane_low, pltpu.roll(lo, half, 1), hi)
                fields[2 * pair + 1, c, b] = flux
                if pair == 0 and c == 0:
                    eastward = flags[0, pl.ds(2 * b, levels, stride=4), :].astype(jnp.float32)
                    start = face_row(message.shape[0], levels, b)
                    message[start : start + levels] = (2.0 * eastward - 1.0) * flux

    def field(f, c, l):
        return spread(upper_block, fields, ((f, c, 0), l), ((f, c, 1), l))

    def flag(c, l, d):
        base = l * 4 + d
        return spread(upper_block, flags, ((c,), base), ((c,), base + 2)).astype(jnp.float32)

    first_row = (lane == 0) & (row < MOMENTS)
    last_row = (lane == LANES - 1) & (row >= MOMENTS)
    for l in range(levels):
        flux_x = [field(1, c, l) for c in range(columns)]
        flag_x = [flag(c, l, 0) for c in range(columns)]
        east = [flag_x[c] * flux_x[c] for c in range(columns)]
        west = [flux_x[c] - east[c] for c in range(columns)]
        east.append(1.0)
        for c in range(columns):
            share = 1.0 / field(0, c, l)
            rates[0, c, l] = east[c + 1] * share
            rates[1, c, l] = west[c] * share
            flux_y = field(2, c, l)
            north = flag(c, l, 1) * flux_y
            south = pltpu.roll(flux_y - north, 1, 1)
            south = jnp.where(lane == 0, pltpu.roll(south, 4, 0), south)
            rates[2, c, l] = jnp.where(last_row, 0.0, north) * share
            rates[3, c, l] = jnp.where(first_row, 0.0, south) * share

    fixed = row % MOMENTS == 3
    zero = jnp.zeros((8, LANES), jnp.float32)
    below, upper = [None] * columns, [None] * columns
    for l in range(levels):
        for c in range(columns):
            diagonal = zero + 1.0
            if l > 0:
                diagonal = diagonal + below[c]
            if l < levels - 1:
                above = field(3, c, l)
                diagonal = diagonal + above
            if l > 0:
                diagonal = diagonal + below[c] * upper[c]
            inverse = 1.0 / diagonal
            factors[0, c, l] = jnp.where(fixed, 1.0, inverse)
            factors[2, c, l] = jnp.where(fixed, 0.0, below[c] * inverse) if l > 0 else zero
            if l < levels - 1:
                upper[c] = -above * inverse
                factors[1, c, l] = jnp.where(fixed, 0.0, upper[c])
                below[c] = above
            else:
                factors[1, c, l] = zero


def advect(own, east_side, west_side, east, west, turns, slope, masks):
    is_mass, is_slope = masks
    stay = 1.0 - (east + west)
    east_part = east * jnp.where(is_slope, east, 1.0)
    west_part = west * jnp.where(is_slope, west, 1.0)
    east_cross = east * (1.0 - east)
    west_cross = west * (1.0 - west)
    out = []
    for s, e, w, z in zip(own, east_side, west_side, turns):
        total = stay * s + east_part * e + west_part * w
        cross = east_cross * (e - s) - west_cross * (w - s)
        total = total + jnp.where(is_slope, pltpu.roll(cross, slope, 0), 0.0)
        slope_up = pltpu.roll(total, 8 - slope, 0)
        out.append(z * jnp.where(is_mass, slope_up, total) + jnp.where(is_mass, total, 0.0))
    return out


def middle(todo, own, east_side, west_side, east_rate, rates, factors, turn, out):
    tracers, levels = out.shape[0], out.shape[1]
    lane = lax.broadcasted_iota(jnp.int32, (8, LANES), 1)
    at_first, at_last = lane == 0, lane == LANES - 1
    x_masks, y_masks = tile_masks(1), tile_masks(2)
    every = range(tracers)
    c = todo

    def prev(v):
        r = pltpu.roll(v, 1, 1)
        return jnp.where(at_first, pltpu.roll(r, 4, 0), r)

    def following(v):
        r = pltpu.roll(v, LANES - 1, 1)
        return jnp.where(at_last, pltpu.roll(r, 4, 0), r)

    def y_step(values, l):
        return advect(values, [following(v) for v in values], [prev(v) for v in values],
                      rates[2, c, l], rates[3, c, l], [turn[1, t, c, l] for t in every], 2, y_masks)

    carried = [None] * tracers
    for l in range(levels):
        sides = [[side(t, l) for t in every] for side in (own, east_side, west_side)]
        values = advect(*sides, east_rate(l), rates[1, c, l], [turn[0, t, c, l] for t in every], 1, x_masks)
        values = y_step(values, l)
        for t in every:
            v = values[t] * factors[0, c, l]
            if l > 0:
                v = v + factors[2, c, l] * carried[t]
            carried[t] = v
            out[t, l] = v
    for l in range(levels - 1, -1, -1):
        if l < levels - 1:
            for t in every:
                carried[t] = out[t, l] - factors[1, c, l] * carried[t]
        values = y_step(carried, l)
        for t in every:
            out[t, l] = values[t]


def tiles(ref, levels):
    if len(ref.shape) == 4:
        return lambda t, l: ref[t, l]
    return lambda t, l: ref[(t * levels + l) * 8 : (t * levels + l + 1) * 8]


def west_kernel(message, col1, west_halo, rates, factors, turn, out):
    levels = out.shape[1]
    middle(0, tiles(message, levels), tiles(col1, levels), tiles(west_halo, levels),
           lambda l: rates[0, 0, l], rates, factors, turn, out)


def inner_kernel(message, col1, col2, rates, factors, turn, out):
    levels = out.shape[1]
    middle(1, tiles(col1, levels), tiles(col2, levels), tiles(message, levels),
           lambda l: rates[0, 1, l], rates, factors, turn, out)


def east_kernel(col1, col2, halo, rates, factors, turn, before, out, east):
    levels = out.shape[1]
    upper_block = lax.broadcasted_iota(jnp.int32, (8, LANES), 0) >= MOMENTS
    rows = [face_row(halo.shape[0], levels, b) for b in range(2)]

    def east_rate(l):
        flux = spread(upper_block, halo, ((), rows[0] + l), ((), rows[1] + l))
        east[l] = jnp.maximum(flux, 0.0) * rates[0, 2, l]
        return east[l]

    middle(2, tiles(col2, levels), tiles(halo, levels), tiles(col1, levels), east_rate, rates, factors, turn, out)


def finish(c, own, east_side, west_side, east_rate, rates, turn, out, buf, sems):
    tracers, levels = buf.shape[0], buf.shape[1]
    masks = tile_masks(1)
    every = range(tracers)
    copies = []
    for part in range(PARTS):
        low, high = part * levels // PARTS, (part + 1) * levels // PARTS
        for l in range(low, high):
            values = advect(*([side[t, l] for t in every] for side in (own, east_side, west_side)),
                            east_rate(l), rates[1, c, l], [turn[0, t, c, l] for t in every], 1, masks)
            for t in every:
                buf[t, l] = values[t]
        for t in every:
            span = pl.ds(low, high - low)
            copies.append(pltpu.make_async_copy(buf.at[t, span], out.at[t, c, span], sems.at[part, t]))
            copies[-1].start()
    for copy in copies:
        copy.wait()


def last_inner_kernel(mid0, mid1, mid2, rates, turn, out, buf, sems):
    finish(1, mid1, mid2, mid0, lambda l: rates[0, 1, l], rates, turn, out, buf, sems)


def last_east_kernel(begun, mid1, mid2, halo, east, rates, turn, out, buf, sems):
    finish(2, mid2, halo, mid1, lambda l: east[l], rates, turn, out, buf, sems)


def last_west_kernel(begun, mid0, mid1, halo, rates, turn, out, buf, sems):
    finish(0, mid0, mid1, halo, lambda l: rates[0, 0, l], rates, turn, out, buf, sems)


def body(state_adjoint, switches, flags, air_mass, x_flux, y_flux, vertical_mixing):
    state = state_view(state_adjoint)
    switch = pair_view(switches)
    flag = pair_view(flags[None])[0]
    tracers, columns, levels = state.shape[:3]
    order = lax.axis_index("trc").astype(jnp.int32).reshape(1)
    column = f32(tracers, levels, 8, LANES)
    rows = -(-2 * columns * levels // 8) * 8
    length = tracers * levels + -(-2 * levels // 8)
    dma = pltpu.SemaphoreType.DMA
    fields = tuple(stay(x) for x in (air_mass, x_flux, y_flux, vertical_mixing))

    col2, packed = call(
        head_kernel, (column, f32(rows, LANES)), (HBM,) * 5,
        [pltpu.VMEM(x.shape, x.dtype) for x in fields] + [dma((4 + tracers,))], 10**5, 10**6, stay(state), *fields)
    west_halo = shifted(col2, "lon", 1)
    across = swapped(packed, "trc", 2)
    others = [swapped(packed, "trc", 1), across, swapped(across, "trc", 1)]
    message, col1, flag, turn = call(
        turn_kernel,
        (f32(length, 8, LANES), column, jax.ShapeDtypeStruct(flag.shape, flag.dtype),
         f32(2, tracers, columns, levels, 8, LANES)),
        (HBM,) * 3, [pltpu.VMEM(switch.shape, switch.dtype), dma((2, tracers)), dma, dma],
        10**6, 10**6, stay(state), stay(flag), stay(switch))
    rates, factors, message = call(
        pre_kernel,
        (f32(4, columns, levels, 8, LANES), f32(3, columns, levels, 8, LANES), f32(length * 8, LANES)),
        (VMEM,) * 5 + (SMEM,) + (VMEM,) * 2, [pltpu.VMEM((4, columns, 2, levels, LANES), jnp.float32)], 1, 1,
        packed, *others, flag, order, message.reshape(length * 8, LANES), turn, aliases={6: 2})
    message = call(gate_kernel, f32(length * 8, LANES), (VMEM,) * 2, (), 1, 1, message, west_halo, aliases={0: 0})
    east_message = shifted(message, "lon", -1)
    mid0 = call(west_kernel, column, (VMEM,) * 6, (), 10**6, 10**6, message, col1, west_halo, rates, factors, turn)
    east_halo = shifted(mid0, "lon", -1)
    mid1 = call(inner_kernel, column, (VMEM,) * 6, (), 10**6, 10**6, message, col1, col2, rates, factors, turn)
    mid2, east = call(east_kernel, (column, f32(levels, 8, LANES)), (VMEM,) * 7, (), 10**6, 10**6,
                      col1, col2, east_message, rates, factors, turn, mid0)
    west_halo = shifted(mid2, "lon", 1)

    def last(kernel, aliases, *args):
        first = (HBM,) * len(aliases)
        return call(kernel, f32(*state.shape), first + (VMEM,) * (len(args) - len(first)),
                    [pltpu.VMEM(column.shape, jnp.float32), dma((PARTS, tracers))], 10**6, 10**6,
                    *args, out_specs=HBM, aliases=aliases)

    out = last(last_inner_kernel, {}, mid0, mid1, mid2, rates, turn)
    out = last(last_east_kernel, {0: 0}, out, mid1, mid2, east_halo, east, rates, turn)
    out = last(last_west_kernel, {0: 0}, out, mid0, mid1, west_halo, rates, turn)
    return state_back(out)


def solution(mesh):
    placed = (
        P("trc", None, "lon", None, None),
        P("trc", None, "lon", None, None),
        P(None, "lon", None, None),
        P("lon", None, "trc"),
        P("lon", None, "trc"),
        P("lon", None, "trc"),
        P("lon", None, "trc"),
    )
    return jax.shard_map(
        body,
        mesh=mesh,
        in_specs=placed,
        out_specs=P("trc", None, "lon", None, None),
        check_vma=False,
    )
```
